32 devices in a mesh: seq: 8 (over z, x), ch: 4 (over y, core).
Axes of the slice: x: 2, y: 2, z: 4, core: 2. Of those that a mesh axis runs over, the one named last changes fastest.
Arguments:
- features: bfloat16 [1024, 8192], P('seq', 'ch'), may hold values from -6 to 6
- qkv_weight: bfloat16 [1664, 3, 8192], P('seq', None, 'ch'), may hold values from -0.0625 to 0.0625
- grad_out: bfloat16 [1664, 1024], P('ch', 'seq'), may hold values from -6 to 6
- residues: float32 [1664, 16], P('ch'), may hold values from -1 to 1
- log_rates: float32 [1664, 16], P('ch'), may hold values from -10 to -1, as said below
- skip_gain: float32 [1664], P('ch'), may hold values from -1 to 1
Outputs:
- weight_grad: float32 [1664, 3, 8192], P('seq', None, 'ch')
- residue_grad: float32 [1664, 16], P('ch')
- rate_grad: float32 [1664, 16], P('ch')
- skip_grad: float32 [1664], P('ch')
The draws below stay inside these ranges and needn't reach their ends.
Inputs may be any that keep to these rules, and one draw needn't show every extreme that they name: Each channel's decay rates exp(log_rates) lie between about 1 / 1024 and 3 / 20.
All inputs are finite; a program needn't handle non-finite values.
Results may differ from the reference program's by a relative error of at most 0.029.
Values may be sent and summed in bfloat16 or wider, within the bound.
No kernel may reach another device: no remote copies, remote signals or barrier semaphores. Data moves between devices by JAX's collectives and lax.ppermute only.
A program may use at most 64 MiB of HBM per device.

```python
import math
import jax
import jax.numpy as jnp
from jax import lax

D = 8192
C = 1664
ORDER = 16
TOK_DEV = 128
TOKENS = 1024
N_SEQ = 8


def decay_logs(key):
    fraction = jax.random.uniform(jax.random.fold_in(key, 11), (C, 1), jnp.float32)
    fraction = 1.0 - (1.0 - fraction) ** 3
    fastest = math.log(1.0 / 20.0)
    slowest = math.log(1.0 / TOKENS)
    baseline = fastest + fraction * (slowest - fastest)
    spread = jax.random.uniform(jax.random.fold_in(key, 12), (C, ORDER), jnp.float32, 0.0, math.log(3.0))
    return baseline + spread


def draw_log_rates(key, part):
    return decay_logs(key)


def draw_residues(key, part):
    rates = jnp.exp(decay_logs(key))
    normals = jnp.clip(jax.random.normal(jax.random.fold_in(key, 13), (C, ORDER), jnp.float32), -4.0, 4.0)
    return normals * jnp.sqrt(2.0 * rates / ORDER)


def steps_of(stream_key, shape, cuts, smallest, largest):
    level = 1.0
    for dim, parts in cuts:
        heights = jax.random.uniform(jax.random.fold_in(jax.random.fold_in(stream_key, 6), dim), (parts,), jnp.float32, smallest / len(cuts), largest / len(cuts))
        level = level * jnp.repeat(jnp.exp(heights), shape[dim] // parts).reshape((-1,) + (1,) * (len(shape) - 1 - dim))
    return level


def gaussian(stream_key, shape, scale, reach, split=(), kind=jnp.bfloat16):
    factor_of = steps_of(stream_key, shape, split, -0.22, 0.18) if split else 1.0
    entries = jax.random.normal(stream_key, shape, jnp.float32) * scale * factor_of
    return jnp.minimum(jnp.maximum(entries, -reach), reach).astype(kind)


def setup_inputs(seed: int = 0) -> dict:
    seeds = jax.random.split(jax.random.key(seed), 7)
    features = gaussian(seeds[0], (TOKENS, D), 1.0, 6.0, ((0, 8), (1, 4)))
    qkv_weight = gaussian(seeds[1], (C, 3, D), D ** -0.5, 0.0625, ((0, 8), (2, 4)))
    grad_out = gaussian(seeds[2], (C, TOKENS), 1.0, 6.0, ((0, 4), (1, 8)))
    residues = draw_residues(jax.random.fold_in(seeds[6], 71), 0)
    log_rates = draw_log_rates(jax.random.fold_in(seeds[6], 71), 0)
    skip_gain = jnp.clip(jax.random.uniform(seeds[5], (C,), jnp.float32, -1.0, 1.0) * steps_of(seeds[5], (C,), ((0, 4),), -0.4, 0.0), -1.0, 1.0)
    return {"features": features, "qkv_weight": qkv_weight, "grad_out": grad_out, "residues": residues, "log_rates": log_rates, "skip_gain": skip_gain}


def reference(features, qkv_weight, grad_out, residues, log_rates, skip_gain):
    period = 2 * TOKENS
    flat_weight = qkv_weight.reshape(C * 3, D)
    projected = jnp.dot(features, flat_weight.T, preferred_element_type=jnp.float32).astype(jnp.bfloat16)
    projected = projected.reshape(TOKENS, C, 3).transpose(1, 2, 0)
    queries = projected[:, 0].astype(jnp.float32)
    keys = projected[:, 1].astype(jnp.float32)
    values = projected[:, 2].astype(jnp.float32)
    kv_product = keys * values
    rates = jnp.exp(log_rates)
    steps = jnp.arange(TOKENS, dtype=jnp.float32)
    taps = jnp.zeros((C, TOKENS), jnp.float32)
    for order_index in range(ORDER):
        taps = taps + residues[:, order_index:order_index + 1] * jnp.exp(-rates[:, order_index:order_index + 1] * steps[None, :])
    spec_mixed = jnp.fft.rfft(kv_product, n=period, axis=1)
    spec_taps = jnp.fft.rfft(taps, n=period, axis=1)
    conv_out = jnp.fft.irfft(spec_taps * spec_mixed, n=period, axis=1)[:, :TOKENS]
    grad_upper = grad_out.astype(jnp.float32)
    grad_mid = grad_upper * queries
    spec_mid = jnp.fft.rfft(grad_mid, n=period, axis=1)
    corr_out = jnp.fft.irfft(jnp.conj(spec_taps) * spec_mid, n=period, axis=1)[:, :TOKENS]
    taps_grad = jnp.fft.irfft(jnp.conj(spec_mixed) * spec_mid, n=period, axis=1)[:, :TOKENS]
    skip_col = skip_gain[:, None]
    grad_query = grad_upper * (conv_out + skip_col * kv_product)
    grad_mix = corr_out + skip_col * grad_mid
    grad_proj = jnp.stack([grad_query, grad_mix * values, grad_mix * keys], axis=1).astype(jnp.bfloat16)
    grad_blocks = grad_proj.reshape(C * 3, N_SEQ, TOK_DEV).transpose(1, 0, 2)
    feature_blocks = features.reshape(N_SEQ, TOK_DEV, D)

    def add_block(total, pieces):
        grad_piece, feature_piece = pieces
        partial_sum = jnp.dot(grad_piece, feature_piece, preferred_element_type=jnp.float32)
        rounded = lax.optimization_barrier(partial_sum.astype(jnp.bfloat16))
        return total + rounded.astype(jnp.float32), None

    weight_total, _ = lax.scan(add_block, jnp.zeros((C * 3, D), jnp.float32), (grad_blocks, feature_blocks))
    weight_grad = weight_total.reshape(C, 3, D)
    residue_cols = []
    rate_cols = []
    for order_index in range(ORDER):
        decays = jnp.exp(-rates[:, order_index:order_index + 1] * steps[None, :])
        residue_cols.append(jnp.sum(taps_grad * decays, axis=1))
        moment = jnp.sum(taps_grad * steps[None, :] * decays, axis=1)
        rate_cols.append(-residues[:, order_index] * rates[:, order_index] * moment)
    residue_grad = jnp.stack(residue_cols, axis=1)
    rate_grad = jnp.stack(rate_cols, axis=1)
    skip_grad = jnp.sum(grad_mid * kv_product, axis=1)
    return weight_grad, residue_grad, rate_grad, skip_grad
```

```python
import functools
import math

import jax
import jax.numpy as jnp
import ml_dtypes
import numpy as np
from jax import lax
from jax.experimental import pallas as pl
from jax.experimental.pallas import tpu as pltpu
from jax.sharding import PartitionSpec as P

F32 = jnp.float32
BF16 = jnp.bfloat16
VMEM_BYTES = 56 * 1024 * 1024


def round_up(value, multiple):
    return -(-value // multiple) * multiple


def wave_tables(tokens):
    odd = 2 * np.arange(tokens, dtype=np.int64) + 1
    angles = (odd[:, None] * odd[None, :] % (8 * tokens)) * (math.pi / (4 * tokens))
    twist = odd * (math.pi / (4 * tokens))
    return (
        np.cos(angles).astype(ml_dtypes.bfloat16),
        np.sin(angles).astype(ml_dtypes.bfloat16),
        np.stack([np.cos(twist), np.sin(twist)]).astype(np.float32),
    )


def dot(left, right):
    return jnp.dot(left, right, preferred_element_type=F32)


def two_parts(value):
    high = value.astype(BF16)
    low = (value - high.astype(F32)).astype(BF16)
    return jnp.concatenate([high, low], 0)


def wide_dot(value, table):
    rows = value.shape[0]
    both = dot(two_parts(value), table)
    return both[:rows] + both[rows:]


def taps_kernel(poles_ref, cos_ref, sin_ref, twist_ref, hc_ref, hs_ref, *, order):
    rows, tokens = hc_ref.shape
    steps = lax.broadcasted_iota(jnp.int32, (rows, tokens), 1).astype(F32)
    taps = jnp.zeros((rows, tokens), F32)
    for pole in range(order):
        residue = poles_ref[:, pole : pole + 1]
        rate = jnp.exp(poles_ref[:, order + pole : order + pole + 1])
        taps = taps + residue * jnp.exp(-rate * steps)
    even = wide_dot(taps, cos_ref[...])
    uneven = wide_dot(taps, sin_ref[...])
    cos_half = twist_ref[0:1, :]
    sin_half = twist_ref[1:2, :]
    hc_ref[...] = cos_half * even + sin_half * uneven
    hs_ref[...] = cos_half * uneven - sin_half * even


def conv_kernel(
    proj_ref, gout_ref, poles_ref, hc_ref, hs_ref, cos_ref, sin_ref, twist_ref,
    grad_ref, tgc_ref, tgs_ref, skip_ref, *, order,
):
    rows, tokens = hc_ref.shape
    queries = proj_ref[0].astype(F32)
    keys = proj_ref[1].astype(F32)
    values = proj_ref[2].astype(F32)
    upper = gout_ref[...].astype(F32)
    product = keys * values
    middle = upper * queries
    signals = jnp.concatenate([product, middle], 0)
    parts = two_parts(signals)
    even = dot(parts, cos_ref[...])
    uneven = dot(parts, sin_ref[...])
    even = even[: 2 * rows] + even[2 * rows :]
    uneven = uneven[: 2 * rows] + uneven[2 * rows :]
    ac, mc = even[:rows], even[rows:]
    as_, ms = uneven[:rows], uneven[rows:]
    hc = hc_ref[...]
    hs = hs_ref[...]
    scale = 1.0 / tokens
    cos_sums = jnp.concatenate([hc * ac - hs * as_, hc * mc + hs * ms], 0) * scale
    sin_sums = jnp.concatenate([hc * as_ + hs * ac, hc * ms - hs * mc], 0) * scale
    tc = (ac * mc + as_ * ms) * scale
    ts = (ac * ms - as_ * mc) * scale
    cos_half = twist_ref[0:1, :]
    sin_half = twist_ref[1:2, :]
    tgc_ref[...] = tc * cos_half - ts * sin_half
    tgs_ref[...] = ts * cos_half + tc * sin_half
    restored = wide_dot(cos_sums, cos_ref[...]) + wide_dot(sin_sums, sin_ref[...])
    skip = poles_ref[:, 2 * order : 2 * order + 1]
    mix = restored[rows:] + skip * middle
    grad_ref[0] = (upper * (restored[:rows] + skip * product)).astype(BF16)
    grad_ref[1] = (mix * values).astype(BF16)
    grad_ref[2] = (mix * keys).astype(BF16)
    skip_ref[...] = jnp.sum(product * middle, axis=1, keepdims=True)


def pole_kernel(poles_ref, tgc_ref, tgs_ref, cos_ref, sin_ref, skip_ref, out_ref, *, order):
    rows, tokens = tgc_ref.shape
    taps_grad = wide_dot(tgc_ref[...], cos_ref[...]) + wide_dot(tgs_ref[...], sin_ref[...])
    steps = lax.broadcasted_iota(jnp.int32, (rows, tokens), 1).astype(F32)
    for pole in range(order):
        residue = poles_ref[:, pole : pole + 1]
        rate = jnp.exp(poles_ref[:, order + pole : order + pole + 1])
        decayed = taps_grad * jnp.exp(-rate * steps)
        out_ref[:, pole : pole + 1] = jnp.sum(decayed, axis=1, keepdims=True)
        moment = jnp.sum(decayed * steps, axis=1, keepdims=True)
        out_ref[:, order + pole : order + pole + 1] = -residue * rate * moment
    out_ref[:, 2 * order : 2 * order + 1] = skip_ref[...]


def call(kernel, outs, flops, transcendentals, *operands):
    size = sum(a.size * a.dtype.itemsize for a in operands) + sum(
        o.size * o.dtype.itemsize for o in outs
    )
    return pl.pallas_call(
        kernel,
        out_shape=outs,
        compiler_params=pltpu.CompilerParams(vmem_limit_bytes=VMEM_BYTES),
        cost_estimate=pl.CostEstimate(
            flops=flops, bytes_accessed=size, transcendentals=transcendentals
        ),
    )(*operands)


def local(features, qkv_weight, grad_out, residues, log_rates, skip_gain):
    n_seq = lax.axis_size("seq")
    n_ch = lax.axis_size("ch")
    seq_index = lax.axis_index("seq")
    rows, gates, width = qkv_weight.shape
    block_len = features.shape[0]
    tokens = n_seq * block_len
    order = residues.shape[1]
    part = round_up(-(-rows // n_ch), 8)
    starts = [min(h * part, rows - part) for h in range(n_ch)]
    per_ch = n_seq // n_ch
    cos_table, sin_table, twist = (jnp.asarray(a) for a in wave_tables(tokens))

    piece_starts = [(j // n_ch) * rows + starts[j % n_ch] for j in range(n_seq)]
    spread = [((q % n_seq) * n_ch + q // n_seq, q) for q in range(n_seq * n_ch)]
    gather_back = [(b, a) for a, b in spread]

    grad_pieces = jnp.stack([grad_out[p : p + part] for p in piece_starts])
    grad_pieces = lax.all_to_all(grad_pieces, "seq", split_axis=0, concat_axis=0, tiled=True)
    grad_pieces = lax.ppermute(grad_pieces, ("seq", "ch"), spread)
    upper = grad_pieces.transpose(1, 0, 2).reshape(part, tokens)

    packed = jnp.concatenate([residues, log_rates, skip_gain[:, None]], 1)
    own_start = jnp.asarray(piece_starts, jnp.int32)[seq_index]
    poles = lax.dynamic_slice_in_dim(packed, own_start, part, 0)
    poles = lax.ppermute(poles, ("seq", "ch"), spread)

    square = part * tokens * tokens
    spectrum = jax.ShapeDtypeStruct((part, tokens), F32)
    hc, hs = call(
        functools.partial(taps_kernel, order=order), (spectrum, spectrum),
        8 * square, part * tokens * order, poles, cos_table, sin_table, twist,
    )

    weight = qkv_weight.transpose(1, 0, 2)
    every_feature = lax.all_gather(features, "seq", axis=0, tiled=True)
    partial = jnp.einsum("gcd,td->gct", weight, every_feature, preferred_element_type=F32)
    partial = partial.astype(BF16)
    partial = jnp.stack([partial[:, p : p + part] for p in starts])
    projected = lax.psum_scatter(partial, "ch", scatter_dimension=0, tiled=False)

    grads, tgc, tgs, skip_sum = call(
        functools.partial(conv_kernel, order=order),
        (
            jax.ShapeDtypeStruct((gates, part, tokens), BF16),
            spectrum,
            spectrum,
            jax.ShapeDtypeStruct((part, 1), F32),
        ),
        32 * square, 0, projected, upper, poles, hc, hs, cos_table, sin_table, twist,
    )
    (pole_sums,) = call(
        functools.partial(pole_kernel, order=order),
        (jax.ShapeDtypeStruct((part, 2 * order + 1), F32),),
        8 * square, part * tokens * order, poles, tgc, tgs, cos_table, sin_table, skip_sum,
    )

    gathered = lax.all_gather(grads, "ch", axis=0)
    pieces, filled = [], 0
    for h, begin in enumerate(starts):
        if begin + part > filled:
            pieces.append(gathered[h, :, filled - begin :])
            filled = begin + part
    own_rows = jnp.concatenate(pieces, 1)
    weight_grad = jnp.einsum("gct,td->gcd", own_rows, every_feature, preferred_element_type=F32)
    weight_grad = weight_grad.transpose(1, 0, 2)

    returned = lax.ppermute(pole_sums, ("seq", "ch"), gather_back)
    returned = lax.all_gather(returned, "seq", axis=0)
    pieces = []
    for block in range(per_ch):
        filled = 0
        for h, begin in enumerate(starts):
            if begin + part > filled:
                pieces.append(returned[block * n_ch + h, filled - begin :])
                filled = begin + part
    sums = jnp.concatenate(pieces, 0)
    return (weight_grad, sums[:, :order], sums[:, order : 2 * order], sums[:, 2 * order])


def solution(mesh):
    placed = (
        P("seq", "ch"),
        P("seq", None, "ch"),
        P("ch", "seq"),
        P("ch", None),
        P("ch", None),
        P("ch"),
    )
    return jax.shard_map(
        local,
        mesh=mesh,
        in_specs=placed,
        out_specs=(P("seq", None, "ch"), P("ch", None), P("ch", None), P("ch")),
        check_vma=False,
    )
```

```python
import functools
import math

import jax
import jax.numpy as jnp
import ml_dtypes
import numpy as np
from jax import lax
from jax.experimental import pallas as pl
from jax.experimental.pallas import tpu as pltpu
from jax.sharding import PartitionSpec as P

F32 = jnp.float32
BF16 = jnp.bfloat16
VMEM_BYTES = 56 * 1024 * 1024


def round_up(value, multiple):
    return -(-value // multiple) * multiple


def wave_tables(tokens):
    odd = 2 * np.arange(tokens, dtype=np.int64) + 1
    angles = (odd[:, None] * odd[None, :] % (8 * tokens)) * (math.pi / (4 * tokens))
    twist = odd * (math.pi / (4 * tokens))
    return (
        np.cos(angles).astype(ml_dtypes.bfloat16),
        np.sin(angles).astype(ml_dtypes.bfloat16),
        np.stack([np.cos(twist), np.sin(twist)]).astype(np.float32),
    )


def dot(left, right):
    return jnp.dot(left, right, preferred_element_type=F32)


def two_parts(value):
    high = value.astype(BF16)
    low = (value - high.astype(F32)).astype(BF16)
    return jnp.concatenate([high, low], 0)


def wide_dot(value, table):
    rows = value.shape[0]
    both = dot(two_parts(value), table)
    return both[:rows] + both[rows:]


def taps_kernel(poles_ref, cos_ref, sin_ref, twist_ref, hc_ref, hs_ref, *, order):
    rows, tokens = hc_ref.shape
    steps = lax.broadcasted_iota(jnp.int32, (rows, tokens), 1).astype(F32)
    taps = jnp.zeros((rows, tokens), F32)
    for pole in range(order):
        residue = poles_ref[:, pole : pole + 1]
        rate = jnp.exp(poles_ref[:, order + pole : order + pole + 1])
        taps = taps + residue * jnp.exp(-rate * steps)
    even = wide_dot(taps, cos_ref[...])
    uneven = wide_dot(taps, sin_ref[...])
    cos_half = twist_ref[0:1, :]
    sin_half = twist_ref[1:2, :]
    hc_ref[...] = cos_half * even + sin_half * uneven
    hs_ref[...] = cos_half * uneven - sin_half * even


def project_kernel(starts_ref, weight_ref, *refs, pieces):
    feature_refs = refs[:pieces]
    out_refs = refs[pieces:-2]
    features_ref, sums_ref = refs[-2:]
    gates, _, _ = weight_ref.shape
    part = out_refs[0].shape[1]
    row = 0
    for feature_ref in feature_refs:
        features_ref[row : row + feature_ref.shape[0], :] = feature_ref[...]
        row += feature_ref.shape[0]
    for gate in range(gates):
        sums_ref[gate] = lax.dot_general(
            weight_ref[gate], features_ref[...], (((1,), (1,)), ((), ())),
            preferred_element_type=F32,
        )
    for step, out_ref in enumerate(out_refs):
        start = pl.multiple_of(starts_ref[step], 8)
        out_ref[...] = sums_ref[:, pl.ds(start, part), :].astype(out_ref.dtype)


def conv_kernel(slots_ref, *refs, order, group_slots, shares):
    partial_refs = refs[: len(group_slots) * shares]
    (
        gout_ref, poles_ref, hc_ref, hs_ref, cos_ref, sin_ref, twist_ref,
        grad_ref, tgc_ref, tgs_ref, skip_ref, proj_ref,
    ) = refs[len(group_slots) * shares :]
    rows, tokens = hc_ref.shape
    blocks, _, _, block_len = proj_ref.shape
    slot = 0
    for group, count in enumerate(group_slots):
        own_ref, *other_refs = partial_refs[group * shares : (group + 1) * shares]
        total = own_ref[...]
        for other_ref in other_refs:
            total = total + other_ref[...].astype(F32)
        total = total.astype(BF16).astype(F32)
        for place in range(count):
            proj_ref[slot] = total[:, :, place * block_len : (place + 1) * block_len]
            slot += 1

    def in_order(gate):
        return jnp.concatenate([proj_ref[slots_ref[b], gate] for b in range(blocks)], 1)

    queries = in_order(0)
    keys = in_order(1)
    values = in_order(2)
    upper = jnp.concatenate(
        [gout_ref[slots_ref[blocks + b]].astype(F32) for b in range(blocks)], 1
    )
    product = keys * values
    middle = upper * queries
    signals = jnp.concatenate([product, middle], 0)
    parts = two_parts(signals)
    even = dot(parts, cos_ref[...])
    uneven = dot(parts, sin_ref[...])
    even = even[: 2 * rows] + even[2 * rows :]
    uneven = uneven[: 2 * rows] + uneven[2 * rows :]
    ac, mc = even[:rows], even[rows:]
    as_, ms = uneven[:rows], uneven[rows:]
    hc = hc_ref[...]
    hs = hs_ref[...]
    scale = 1.0 / tokens
    cos_sums = jnp.concatenate([hc * ac - hs * as_, hc * mc + hs * ms], 0) * scale
    sin_sums = jnp.concatenate([hc * as_ + hs * ac, hc * ms - hs * mc], 0) * scale
    tc = (ac * mc + as_ * ms) * scale
    ts = (ac * ms - as_ * mc) * scale
    cos_half = twist_ref[0:1, :]
    sin_half = twist_ref[1:2, :]
    tgc_ref[...] = tc * cos_half - ts * sin_half
    tgs_ref[...] = ts * cos_half + tc * sin_half
    restored = wide_dot(cos_sums, cos_ref[...]) + wide_dot(sin_sums, sin_ref[...])
    skip = poles_ref[:, 2 * order : 2 * order + 1]
    mix = restored[rows:] + skip * middle
    grads = (upper * (restored[:rows] + skip * product), mix * values, mix * keys)
    for gate, grad in enumerate(grads):
        for b in range(blocks):
            place = pl.multiple_of(slots_ref[b] * block_len, block_len)
            grad_ref[gate, :, pl.ds(place, block_len)] = grad[
                :, b * block_len : (b + 1) * block_len
            ].astype(BF16)
    skip_ref[...] = jnp.sum(product * middle, axis=1, keepdims=True)


def pole_kernel(poles_ref, tgc_ref, tgs_ref, cos_ref, sin_ref, skip_ref, out_ref, *, order):
    rows, tokens = tgc_ref.shape
    taps_grad = wide_dot(tgc_ref[...], cos_ref[...]) + wide_dot(tgs_ref[...], sin_ref[...])
    steps = lax.broadcasted_iota(jnp.int32, (rows, tokens), 1).astype(F32)
    for pole in range(order):
        residue = poles_ref[:, pole : pole + 1]
        rate = jnp.exp(poles_ref[:, order + pole : order + pole + 1])
        decayed = taps_grad * jnp.exp(-rate * steps)
        out_ref[:, pole : pole + 1] = jnp.sum(decayed, axis=1, keepdims=True)
        moment = jnp.sum(decayed * steps, axis=1, keepdims=True)
        out_ref[:, order + pole : order + pole + 1] = -residue * rate * moment
    out_ref[:, 2 * order : 2 * order + 1] = skip_ref[...]


def weight_kernel(starts_ref, *refs, shares):
    grad_refs = refs[:shares]
    feature_ref, out_ref, wide_ref, rows_ref = refs[shares:]
    gates = out_ref.shape[0]
    part = grad_refs[0].shape[1]

    @pl.when(pl.program_id(0) == 0)
    def _():
        for share, grad_ref in enumerate(grad_refs):
            start = pl.multiple_of(starts_ref[share], 8)
            wide_ref[:, pl.ds(start, part), :] = grad_ref[...].astype(F32)
        rows_ref[...] = wide_ref[...].astype(BF16)

    for gate in range(gates):
        out_ref[gate] = dot(rows_ref[gate], feature_ref[...])


def call(kernel, outs, flops, transcendentals, *operands, scratch=(), indexed=False):
    size = sum(a.size * a.dtype.itemsize for a in operands) + sum(
        o.size * o.dtype.itemsize for o in outs
    )
    whole = pl.BlockSpec(memory_space=pltpu.VMEM)
    specs = [whole] * len(operands)
    if indexed:
        specs[0] = pl.BlockSpec(memory_space=pltpu.SMEM)
    return pl.pallas_call(
        kernel,
        out_shape=outs,
        in_specs=specs,
        out_specs=[whole] * len(outs),
        scratch_shapes=scratch,
        compiler_params=pltpu.CompilerParams(vmem_limit_bytes=VMEM_BYTES),
        cost_estimate=pl.CostEstimate(
            flops=flops, bytes_accessed=size, transcendentals=transcendentals
        ),
    )(*operands)


def picked(table, index):
    return jnp.asarray(np.asarray(table, np.int32))[index]


def ring_gather(features, ring):
    count = len(ring)
    half = features.shape[0] // 2
    ahead = [(ring[i], ring[(i + 1) % count]) for i in range(count)]
    behind = [(b, a) for a, b in ahead]
    own = (features[:half], features[half:])
    slots = [own]
    from_behind, from_ahead = own, own
    for _ in range(count // 2 - 1):
        from_behind = tuple(lax.ppermute(a, "seq", ahead) for a in from_behind)
        from_ahead = tuple(lax.ppermute(a, "seq", behind) for a in from_ahead)
        slots += [from_behind, from_ahead]
    slots.append(
        (lax.ppermute(from_behind[0], "seq", ahead), lax.ppermute(from_ahead[1], "seq", behind))
    )
    return slots


def local(features, qkv_weight, grad_out, residues, log_rates, skip_gain):
    n_seq = lax.axis_size("seq")
    n_ch = lax.axis_size("ch")
    seq_index = lax.axis_index("seq")
    ch_index = lax.axis_index("ch")
    rows, gates, width = qkv_weight.shape
    block_len = features.shape[0]
    tokens = n_seq * block_len
    order = residues.shape[1]
    part = round_up(-(-rows // n_ch), 8)
    starts = [min(h * part, rows - part) for h in range(n_ch)]
    per_ch = n_seq // n_ch
    cos_table, sin_table, twist = (jnp.asarray(a) for a in wave_tables(tokens))

    ring = list(range(0, n_seq, 2)) + list(range(n_seq - 1, 0, -2))
    offsets = [0] + [o for k in range(1, n_seq // 2) for o in (-k, k)] + [n_seq // 2]
    slot_of = np.zeros((n_seq, n_seq), np.int32)
    for place, index in enumerate(ring):
        for slot, offset in enumerate(offsets):
            slot_of[index, ring[(place + offset) % n_seq]] = slot
    slots = ring_gather(features, ring)

    piece_starts = [(j // n_ch) * rows + starts[j % n_ch] for j in range(n_seq)]
    spread = [((q % n_seq) * n_ch + q // n_seq, q) for q in range(n_seq * n_ch)]
    gather_back = [(b, a) for a, b in spread]

    packed = jnp.concatenate([residues, log_rates, skip_gain[:, None]], 1)
    poles = lax.dynamic_slice_in_dim(packed, picked(piece_starts, seq_index), part, 0)
    poles = lax.ppermute(poles, ("seq", "ch"), spread)

    upper = []
    for k in range(n_seq):
        route = [
            (((q % n_seq + k) % n_seq) * n_ch + q // n_seq, q) for q in range(n_seq * n_ch)
        ]
        begin = picked([piece_starts[(s - k) % n_seq] for s in range(n_seq)], seq_index)
        sent = lax.dynamic_slice_in_dim(grad_out, begin, part, 0)
        upper.append(lax.ppermute(sent, ("seq", "ch"), route))
    upper = jnp.stack(upper)
    own_piece = (seq_index * n_ch + ch_index) % n_seq
    upper_slots = (jnp.arange(n_seq, dtype=jnp.int32) - own_piece) % n_seq
    conv_slots = jnp.concatenate([picked(slot_of, seq_index), upper_slots.astype(jnp.int32)])

    square = part * tokens * tokens
    spectrum = jax.ShapeDtypeStruct((part, tokens), F32)
    hc, hs = call(
        functools.partial(taps_kernel, order=order), (spectrum, spectrum),
        8 * square, part * tokens * order, poles, cos_table, sin_table, twist,
    )

    weight = qkv_weight.transpose(1, 0, 2)
    ahead_starts = picked(
        [[starts[(h + d) % n_ch] for d in range(n_ch)] for h in range(n_ch)], ch_index
    )
    behind_starts = picked(
        [[starts[(h - d) % n_ch] for d in range(n_ch)] for h in range(n_ch)], ch_index
    )
    groups = [slots[:3]] + [slots[i : i + 2] for i in range(3, n_seq, 2)]
    group_slots = [len(group) for group in groups]
    partials = []
    for group in groups:
        pieces = [piece for slot in group for piece in slot]
        span = len(group) * block_len
        sums = call(
            functools.partial(project_kernel, pieces=len(pieces)),
            [
                jax.ShapeDtypeStruct((gates, part, span), F32 if d == 0 else BF16)
                for d in range(n_ch)
            ],
            2 * gates * rows * width * span, 0, ahead_starts, weight, *pieces,
            scratch=[pltpu.VMEM((span, width), BF16), pltpu.VMEM((gates, rows, span), F32)],
            indexed=True,
        )
        partials.append(sums[0])
        for d in range(1, n_ch):
            partials.append(
                lax.ppermute(sums[d], "ch", [(h, (h + d) % n_ch) for h in range(n_ch)])
            )

    grads, tgc, tgs, skip_sum = call(
        functools.partial(conv_kernel, order=order, group_slots=group_slots, shares=n_ch),
        (
            jax.ShapeDtypeStruct((gates, part, tokens), BF16),
            spectrum,
            spectrum,
            jax.ShapeDtypeStruct((part, 1), F32),
        ),
        32 * square, 0, conv_slots, *partials, upper, poles, hc, hs,
        cos_table, sin_table, twist,
        scratch=[pltpu.VMEM((n_seq, gates, part, block_len), F32)], indexed=True,
    )

    held = [grads] + [
        lax.ppermute(grads, "ch", [(h, (h + d) % n_ch) for h in range(n_ch)])
        for d in range(2, n_ch, 2)
    ]
    swap = [(h, h ^ 1) for h in range(n_ch)]
    held += [lax.ppermute(a, "ch", swap) for a in held]
    order_of = [
        [starts[((h ^ core) - d) % n_ch] for core in (0, 1) for d in range(0, n_ch, 2)]
        for h in range(n_ch)
    ]

    (pole_sums,) = call(
        functools.partial(pole_kernel, order=order),
        (jax.ShapeDtypeStruct((part, 2 * order + 1), F32),),
        8 * square, part * tokens * order, poles, tgc, tgs, cos_table, sin_table, skip_sum,
    )

    every_feature = jnp.concatenate([piece for slot in slots for piece in slot], 0)
    tile = min(512, width)
    weight_grad = pl.pallas_call(
        functools.partial(weight_kernel, shares=n_ch),
        out_shape=jax.ShapeDtypeStruct((gates, rows, width), F32),
        grid=(width // tile,),
        in_specs=[pl.BlockSpec(memory_space=pltpu.SMEM)]
        + [pl.BlockSpec((gates, part, tokens), lambda i: (0, 0, 0))] * n_ch
        + [pl.BlockSpec((tokens, tile), lambda i: (0, i))],
        out_specs=pl.BlockSpec((gates, rows, tile), lambda i: (0, 0, i)),
        scratch_shapes=[
            pltpu.VMEM((gates, rows, tokens), F32),
            pltpu.VMEM((gates, rows, tokens), BF16),
        ],
        compiler_params=pltpu.CompilerParams(vmem_limit_bytes=VMEM_BYTES),
        cost_estimate=pl.CostEstimate(
            flops=2 * gates * rows * width * tokens,
            bytes_accessed=4 * gates * rows * width + 2 * tokens * (width + gates * rows),
            transcendentals=0,
        ),
    )(picked(order_of, ch_index), *held, every_feature)
    weight_grad = weight_grad.transpose(1, 0, 2)

    returned = lax.ppermute(pole_sums, ("seq", "ch"), gather_back)[None]
    reach = 1
    while reach < n_seq:
        other = lax.ppermute(returned, "seq", [(s, s ^ reach) for s in range(n_seq)])
        returned = jnp.concatenate([returned, other], 0)
        reach *= 2
    returned = returned[jnp.arange(n_seq) ^ seq_index]
    pieces = []
    for block in range(per_ch):
        filled = 0
        for h, begin in enumerate(starts):
            if begin + part > filled:
                pieces.append(returned[block * n_ch + h, filled - begin :])
                filled = begin + part
    sums = jnp.concatenate(pieces, 0)
    return (weight_grad, sums[:, :order], sums[:, order : 2 * order], sums[:, 2 * order])


def solution(mesh):
    placed = (
        P("seq", "ch"),
        P("seq", None, "ch"),
        P("ch", "seq"),
        P("ch", None),
        P("ch", None),
        P("ch"),
    )
    return jax.shard_map(
        local,
        mesh=mesh,
        in_specs=placed,
        out_specs=(P("seq", None, "ch"), P("ch", None), P("ch", None), P("ch")),
        check_vma=False,
    )
```

```python
import functools
import math

import jax
import jax.numpy as jnp
import ml_dtypes
import numpy as np
from jax import lax
from jax.experimental import pallas as pl
from jax.experimental.pallas import tpu as pltpu
from jax.sharding import PartitionSpec as P

F32 = jnp.float32
BF16 = jnp.bfloat16
MIB = 1024 * 1024


def round_up(value, multiple):
    return -(-value // multiple) * multiple


def wave_tables(tokens):
    odd = 2 * np.arange(tokens, dtype=np.int64) + 1
    angles = (odd[:, None] * odd[None, :] % (8 * tokens)) * (math.pi / (4 * tokens))
    twist = odd * (math.pi / (4 * tokens))
    return (
        np.cos(angles).astype(ml_dtypes.bfloat16),
        np.sin(angles).astype(ml_dtypes.bfloat16),
        np.stack([np.cos(twist), np.sin(twist)]).astype(np.float32),
    )


def dot(left, right):
    return jnp.dot(left, right, preferred_element_type=F32)


def two_parts(value):
    high = value.astype(BF16)
    low = (value - high.astype(F32)).astype(BF16)
    return jnp.concatenate([high, low], 0)


def wide_dot(value, table):
    rows = value.shape[0]
    both = dot(two_parts(value), table)
    return both[:rows] + both[rows:]


def taps_kernel(poles_ref, cos_ref, sin_ref, twist_ref, hc_ref, hs_ref, *, order):
    rows, tokens = hc_ref.shape
    steps = lax.broadcasted_iota(jnp.int32, (rows, tokens), 1).astype(F32)
    taps = jnp.zeros((rows, tokens), F32)
    for pole in range(order):
        residue = poles_ref[:, pole : pole + 1]
        rate = jnp.exp(poles_ref[:, order + pole : order + pole + 1])
        taps = taps + residue * jnp.exp(-rate * steps)
    even = wide_dot(taps, cos_ref[...])
    uneven = wide_dot(taps, sin_ref[...])
    cos_half = twist_ref[0:1, :]
    sin_half = twist_ref[1:2, :]
    hc_ref[...] = cos_half * even + sin_half * uneven
    hs_ref[...] = cos_half * uneven - sin_half * even


def part_start(index, part, rows):
    return pl.multiple_of(jnp.minimum(index * part, rows - part), 8)


def pack_kernel(place_ref, grad_ref, packed_ref, pieces_ref, poles_ref, *, rows, n_ch):
    part = poles_ref.shape[0]
    grad = grad_ref[...].astype(F32)
    for piece in range(pieces_ref.shape[0]):
        start = piece // n_ch * rows + min(piece % n_ch * part, rows - part)
        pieces_ref[piece] = grad[start : start + part].astype(BF16)
    own = place_ref[0]
    start = own // n_ch * rows + part_start(own % n_ch, part, rows)
    poles_ref[...] = packed_ref[pl.ds(pl.multiple_of(start, 8), part), :]


def project_kernel(place_ref, weight_ref, *refs, pieces):
    feature_refs = refs[:pieces]
    out_refs = refs[pieces:-2]
    features_ref, sums_ref = refs[-2:]
    gates, _, _ = weight_ref.shape
    part = out_refs[0].shape[1]
    row = 0
    for feature_ref in feature_refs:
        features_ref[row : row + feature_ref.shape[0], :] = feature_ref[...]
        row += feature_ref.shape[0]
    for gate in range(gates):
        sums_ref[gate] = lax.dot_general(
            weight_ref[gate], features_ref[...], (((1,), (1,)), ((), ())),
            preferred_element_type=F32,
        )
    for step, out_ref in enumerate(out_refs):
        start = part_start((place_ref[1] + step) % len(out_refs), part, weight_ref.shape[1])
        out_ref[...] = sums_ref[:, pl.ds(start, part), :].astype(out_ref.dtype)


def ring_place(index, count):
    return jnp.where(index % 2 == 0, index // 2, count - (index + 1) // 2)


def ring_slot(index, place, count):
    ahead = (ring_place(index, count) - place + count) % count
    near = jnp.where(ahead * 2 < count, 2 * ahead, 2 * (count - ahead) - 1)
    return jnp.where(ahead * 2 == count, count - 1, near)


def conv_kernel(place_ref, *refs, order, group_slots, shares):
    partial_refs = refs[: len(group_slots) * shares]
    (
        gout_ref, poles_ref, hc_ref, hs_ref, cos_ref, sin_ref, twist_ref,
        grad_ref, tgc_ref, tgs_ref, skip_ref, proj_ref,
    ) = refs[len(group_slots) * shares :]
    rows, tokens = hc_ref.shape
    blocks, _, _, block_len = proj_ref.shape
    slot = 0
    for group, count in enumerate(group_slots):
        own_ref, *other_refs = partial_refs[group * shares : (group + 1) * shares]
        total = own_ref[...]
        for other_ref in other_refs:
            total = total + other_ref[...].astype(F32)
        total = total.astype(BF16).astype(F32)
        for place in range(count):
            proj_ref[slot] = total[:, :, place * block_len : (place + 1) * block_len]
            slot += 1

    place = ring_place(place_ref[0], blocks)
    slots = [ring_slot(jnp.int32(b), place, blocks) for b in range(blocks)]

    def in_order(gate):
        return jnp.concatenate([proj_ref[slots[b], gate] for b in range(blocks)], 1)

    queries = in_order(0)
    keys = in_order(1)
    values = in_order(2)
    upper = jnp.concatenate(
        [gout_ref[b].astype(F32) for b in range(blocks)], 1
    )
    product = keys * values
    middle = upper * queries
    signals = jnp.concatenate([product, middle], 0)
    parts = two_parts(signals)
    even = dot(parts, cos_ref[...])
    uneven = dot(parts, sin_ref[...])
    even = even[: 2 * rows] + even[2 * rows :]
    uneven = uneven[: 2 * rows] + uneven[2 * rows :]
    ac, mc = even[:rows], even[rows:]
    as_, ms = uneven[:rows], uneven[rows:]
    hc = hc_ref[...]
    hs = hs_ref[...]
    scale = 1.0 / tokens
    cos_sums = jnp.concatenate([hc * ac - hs * as_, hc * mc + hs * ms], 0) * scale
    sin_sums = jnp.concatenate([hc * as_ + hs * ac, hc * ms - hs * mc], 0) * scale
    tc = (ac * mc + as_ * ms) * scale
    ts = (ac * ms - as_ * mc) * scale
    cos_half = twist_ref[0:1, :]
    sin_half = twist_ref[1:2, :]
    tgc_ref[...] = tc * cos_half - ts * sin_half
    tgs_ref[...] = ts * cos_half + tc * sin_half
    restored = wide_dot(cos_sums, cos_ref[...]) + wide_dot(sin_sums, sin_ref[...])
    skip = poles_ref[:, 2 * order : 2 * order + 1]
    mix = restored[rows:] + skip * middle
    grads = (upper * (restored[:rows] + skip * product), mix * values, mix * keys)
    for gate, grad in enumerate(grads):
        for b in range(blocks):
            column = pl.multiple_of(slots[b] * block_len, block_len)
            grad_ref[gate, :, pl.ds(column, block_len)] = grad[
                :, b * block_len : (b + 1) * block_len
            ].astype(BF16)
    skip_ref[...] = jnp.sum(product * middle, axis=1, keepdims=True)


def pole_kernel(poles_ref, tgc_ref, tgs_ref, cos_ref, sin_ref, skip_ref, out_ref, *, order):
    rows, tokens = tgc_ref.shape
    taps_grad = wide_dot(tgc_ref[...], cos_ref[...]) + wide_dot(tgs_ref[...], sin_ref[...])
    steps = lax.broadcasted_iota(jnp.int32, (rows, tokens), 1).astype(F32)
    for pole in range(order):
        residue = poles_ref[:, pole : pole + 1]
        rate = jnp.exp(poles_ref[:, order + pole : order + pole + 1])
        decayed = taps_grad * jnp.exp(-rate * steps)
        out_ref[:, pole : pole + 1] = jnp.sum(decayed, axis=1, keepdims=True)
        moment = jnp.sum(decayed * steps, axis=1, keepdims=True)
        out_ref[:, order + pole : order + pole + 1] = -residue * rate * moment
    out_ref[:, 2 * order : 2 * order + 1] = skip_ref[...]


def weight_kernel(place_ref, *refs, shares):
    grad_refs = refs[:shares]
    feature_ref, out_ref, wide_ref, rows_ref = refs[shares:]
    gates = out_ref.shape[0]
    part = grad_refs[0].shape[1]

    @pl.when(pl.program_id(0) == 0)
    def _():
        for share, grad_ref in enumerate(grad_refs):
            core, step = share // (shares // 2), 2 * (share % (shares // 2))
            owner = place_ref[1] + core * (1 - 2 * (place_ref[1] % 2))
            start = part_start((owner - step + shares) % shares, part, out_ref.shape[1])
            wide_ref[:, pl.ds(start, part), :] = grad_ref[...].astype(F32)
        rows_ref[...] = wide_ref[...].astype(BF16)

    for gate in range(gates):
        out_ref[gate] = dot(rows_ref[gate], feature_ref[...])


def call(kernel, outs, flops, transcendentals, *operands, scratch=(), indexed=False):
    size = sum(a.size * a.dtype.itemsize for a in operands) + sum(
        o.size * o.dtype.itemsize for o in outs
    )
    scratch_size = sum(math.prod(a.shape) * a.dtype.itemsize for a in scratch)
    limit = min(56 * MIB, 2 * (size + scratch_size) + 8 * MIB)
    whole = pl.BlockSpec(memory_space=pltpu.VMEM)
    specs = [whole] * len(operands)
    if indexed:
        specs[0] = pl.BlockSpec(memory_space=pltpu.SMEM)
    return pl.pallas_call(
        kernel,
        out_shape=outs,
        in_specs=specs,
        out_specs=[whole] * len(outs),
        scratch_shapes=scratch,
        compiler_params=pltpu.CompilerParams(vmem_limit_bytes=limit),
        cost_estimate=pl.CostEstimate(
            flops=flops, bytes_accessed=size, transcendentals=transcendentals
        ),
    )(*operands)


def ring_gather(features, ring):
    count = len(ring)
    half = features.shape[0] // 2
    ahead = [(ring[i], ring[(i + 1) % count]) for i in range(count)]
    behind = [(b, a) for a, b in ahead]
    own = (features[:half], features[half:])
    slots = [own]
    from_behind, from_ahead = own, own
    for _ in range(count // 2 - 1):
        from_behind = tuple(lax.ppermute(a, "seq", ahead) for a in from_behind)
        from_ahead = tuple(lax.ppermute(a, "seq", behind) for a in from_ahead)
        slots += [from_behind, from_ahead]
    slots.append(
        (lax.ppermute(from_behind[0], "seq", ahead), lax.ppermute(from_ahead[1], "seq", behind))
    )
    return slots


def local(features, qkv_weight, grad_out, residues, log_rates, skip_gain):
    n_seq = lax.axis_size("seq")
    n_ch = lax.axis_size("ch")
    seq_index = lax.axis_index("seq")
    ch_index = lax.axis_index("ch")
    rows, gates, width = qkv_weight.shape
    block_len = features.shape[0]
    tokens = n_seq * block_len
    order = residues.shape[1]
    part = round_up(-(-rows // n_ch), 8)
    starts = [min(h * part, rows - part) for h in range(n_ch)]
    per_ch = n_seq // n_ch
    cos_table, sin_table, twist = (jnp.asarray(a) for a in wave_tables(tokens))

    place = jnp.stack([seq_index, ch_index]).astype(jnp.int32)

    ring = list(range(0, n_seq, 2)) + list(range(n_seq - 1, 0, -2))
    slots = ring_gather(features, ring)

    first = slots[1]
    grad_out, residues, log_rates, skip_gain, first = lax.optimization_barrier(
        (grad_out, residues, log_rates, skip_gain, first)
    )
    slots[1] = first

    spread = [((q % n_seq) * n_ch + q // n_seq, q) for q in range(n_seq * n_ch)]
    gather_back = [(b, a) for a, b in spread]
    packed = jnp.concatenate([residues, log_rates, skip_gain[:, None]], 1)
    upper, poles = call(
        functools.partial(pack_kernel, rows=rows, n_ch=n_ch),
        (
            jax.ShapeDtypeStruct((n_seq, part, block_len), BF16),
            jax.ShapeDtypeStruct((part, packed.shape[1]), F32),
        ),
        0, 0, place, grad_out, packed, indexed=True,
    )
    poles = lax.ppermute(poles, ("seq", "ch"), spread)
    upper = lax.all_to_all(upper, "seq", split_axis=0, concat_axis=0, tiled=True)
    upper = lax.ppermute(upper, ("seq", "ch"), spread)

    square = part * tokens * tokens
    spectrum = jax.ShapeDtypeStruct((part, tokens), F32)
    hc, hs = call(
        functools.partial(taps_kernel, order=order), (spectrum, spectrum),
        8 * square, part * tokens * order, poles, cos_table, sin_table, twist,
    )

    weight = qkv_weight.transpose(1, 0, 2)
    groups = [slots[:3]] + [slots[i : i + 4] for i in range(3, n_seq - 1, 4)] + [slots[n_seq - 1 :]]
    group_slots = [len(group) for group in groups]
    partials = []
    for group in groups:
        pieces = [piece for slot in group for piece in slot]
        span = len(group) * block_len
        sums = call(
            functools.partial(project_kernel, pieces=len(pieces)),
            [
                jax.ShapeDtypeStruct((gates, part, span), F32 if d == 0 else BF16)
                for d in range(n_ch)
            ],
            2 * gates * rows * width * span, 0, place, weight, *pieces,
            scratch=[pltpu.VMEM((span, width), BF16), pltpu.VMEM((gates, rows, span), F32)],
            indexed=True,
        )
        partials.append(sums[0])
        for d in range(1, n_ch):
            partials.append(
                lax.ppermute(sums[d], "ch", [(h, (h + d) % n_ch) for h in range(n_ch)])
            )

    grads, tgc, tgs, skip_sum = call(
        functools.partial(conv_kernel, order=order, group_slots=group_slots, shares=n_ch),
        (
            jax.ShapeDtypeStruct((gates, part, tokens), BF16),
            spectrum,
            spectrum,
            jax.ShapeDtypeStruct((part, 1), F32),
        ),
        32 * square, 0, place, *partials, upper, poles, hc, hs,
        cos_table, sin_table, twist,
        scratch=[pltpu.VMEM((n_seq, gates, part, block_len), F32)], indexed=True,
    )

    swap = [(h, h ^ 1) for h in range(n_ch)]
    across = [
        lax.ppermute(grads, "ch", [(h, (h + d) % n_ch) for h in range(n_ch)])
        for d in range(2, n_ch, 2)
    ]
    swapped = lax.ppermute(grads, "ch", swap)
    tgc, swapped = lax.optimization_barrier((tgc, swapped))
    (pole_sums,) = call(
        functools.partial(pole_kernel, order=order),
        (jax.ShapeDtypeStruct((part, 2 * order + 1), F32),),
        8 * square, part * tokens * order, poles, tgc, tgs, cos_table, sin_table, skip_sum,
    )

    pole_sums, across = lax.optimization_barrier((pole_sums, across))
    held = [grads] + across + [swapped] + [lax.ppermute(a, "ch", swap) for a in across]

    every_feature = jnp.concatenate([piece for slot in slots for piece in slot], 0)
    tile = min(512, width)
    weight_grad = pl.pallas_call(
        functools.partial(weight_kernel, shares=n_ch),
        out_shape=jax.ShapeDtypeStruct((gates, rows, width), F32),
        grid=(width // tile,),
        in_specs=[pl.BlockSpec(memory_space=pltpu.SMEM)]
        + [pl.BlockSpec((gates, part, tokens), lambda i: (0, 0, 0))] * n_ch
        + [pl.BlockSpec((tokens, tile), lambda i: (0, i))],
        out_specs=pl.BlockSpec((gates, rows, tile), lambda i: (0, 0, i)),
        scratch_shapes=[
            pltpu.VMEM((gates, rows, tokens), F32),
            pltpu.VMEM((gates, rows, tokens), BF16),
        ],
        compiler_params=pltpu.CompilerParams(
            vmem_limit_bytes=min(56 * MIB, 16 * MIB + 12 * gates * rows * tokens + 4 * tokens * tile)
        ),
        cost_estimate=pl.CostEstimate(
            flops=2 * gates * rows * width * tokens,
            bytes_accessed=4 * gates * rows * width + 2 * tokens * (width + gates * rows),
            transcendentals=0,
        ),
    )(place, *held, every_feature)
    weight_grad = weight_grad.transpose(1, 0, 2)

    returned = lax.ppermute(pole_sums, ("seq", "ch"), gather_back)
    returned = jnp.broadcast_to(returned[None], (n_seq,) + returned.shape)
    returned = lax.all_to_all(returned, "seq", split_axis=0, concat_axis=0, tiled=True)
    pieces = []
    for block in range(per_ch):
        filled = 0
        for h, begin in enumerate(starts):
            if begin + part > filled:
                pieces.append(returned[block * n_ch + h, filled - begin :])
                filled = begin + part
    sums = jnp.concatenate(pieces, 0)
    return (weight_grad, sums[:, :order], sums[:, order : 2 * order], sums[:, 2 * order])


def solution(mesh):
    placed = (
        P("seq", "ch"),
        P("seq", None, "ch"),
        P("ch", "seq"),
        P("ch", None),
        P("ch", None),
        P("ch"),
    )
    return jax.shard_map(
        local,
        mesh=mesh,
        in_specs=placed,
        out_specs=(P("seq", None, "ch"), P("ch", None), P("ch", None), P("ch")),
        check_vma=False,
    )
```

```python
import functools
import math

import jax
import jax.numpy as jnp
import ml_dtypes
import numpy as np
from jax import lax
from jax.experimental import pallas as pl
from jax.experimental.pallas import tpu as pltpu
from jax.sharding import PartitionSpec as P

F32 = jnp.float32
BF16 = jnp.bfloat16
MIB = 1024 * 1024


def round_up(value, multiple):
    return -(-value // multiple) * multiple


def wave_tables(tokens):
    odd = 2 * np.arange(tokens, dtype=np.int64) + 1
    angles = (odd[:, None] * odd[None, :] % (8 * tokens)) * (math.pi / (4 * tokens))
    twist = odd * (math.pi / (4 * tokens))
    return (
        np.cos(angles).astype(ml_dtypes.bfloat16),
        np.sin(angles).astype(ml_dtypes.bfloat16),
        np.stack([np.cos(twist), np.sin(twist)]).astype(np.float32),
    )


def dot(left, right):
    return jnp.dot(left, right, preferred_element_type=F32)


def two_parts(value):
    high = value.astype(BF16)
    low = (value - high.astype(F32)).astype(BF16)
    return jnp.concatenate([high, low], 0)


def wide_dot(value, table):
    rows = value.shape[0]
    both = dot(two_parts(value), table)
    return both[:rows] + both[rows:]


def taps_kernel(poles_ref, cos_ref, sin_ref, twist_ref, hc_ref, hs_ref, *, order):
    rows, tokens = hc_ref.shape
    steps = lax.broadcasted_iota(jnp.int32, (rows, tokens), 1).astype(F32)
    taps = jnp.zeros((rows, tokens), F32)
    for pole in range(order):
        residue = poles_ref[:, pole : pole + 1]
        rate = jnp.exp(poles_ref[:, order + pole : order + pole + 1])
        taps = taps + residue * jnp.exp(-rate * steps)
    even = wide_dot(taps, cos_ref[...])
    uneven = wide_dot(taps, sin_ref[...])
    cos_half = twist_ref[0:1, :]
    sin_half = twist_ref[1:2, :]
    hc_ref[...] = cos_half * even + sin_half * uneven
    hs_ref[...] = cos_half * uneven - sin_half * even


def part_start(index, part, rows):
    return pl.multiple_of(jnp.minimum(index * part, rows - part), 8)


def pieces_kernel(grad_ref, pieces_ref, *, rows, n_ch):
    part = pieces_ref.shape[1]
    grad = grad_ref[...].astype(F32)
    for piece in range(pieces_ref.shape[0]):
        start = piece // n_ch * rows + min(piece % n_ch * part, rows - part)
        pieces_ref[piece] = grad[start : start + part].astype(BF16)


def poles_kernel(place_ref, packed_ref, poles_ref, *, rows, n_ch):
    part = poles_ref.shape[0]
    own = place_ref[0]
    start = own // n_ch * rows + part_start(own % n_ch, part, rows)
    poles_ref[...] = packed_ref[pl.ds(pl.multiple_of(start, 8), part), :]


def fetch(sources, targets, semaphores):
    copies = [
        pltpu.make_async_copy(source, target, semaphores.at[i])
        for i, (source, target) in enumerate(zip(sources, targets))
    ]
    for copy in copies:
        copy.start()
    for copy in copies:
        copy.wait()


def project_kernel(place_ref, weight_ref, *refs, pieces):
    feature_refs = refs[:pieces]
    out_refs = refs[pieces:-3]
    features_ref, sums_ref, semaphores = refs[-3:]
    gates, _, _ = weight_ref.shape
    part = out_refs[0].shape[1]
    targets, row = [], 0
    for feature_ref in feature_refs:
        targets.append(features_ref.at[pl.ds(row, feature_ref.shape[0]), :])
        row += feature_ref.shape[0]
    fetch(feature_refs, targets, semaphores)
    for gate in range(gates):
        sums_ref[gate] = lax.dot_general(
            weight_ref[gate], features_ref[...], (((1,), (1,)), ((), ())),
            preferred_element_type=F32,
        )
    for step, out_ref in enumerate(out_refs):
        start = part_start((place_ref[1] + step) % len(out_refs), part, weight_ref.shape[1])
        out_ref[...] = sums_ref[:, pl.ds(start, part), :].astype(out_ref.dtype)


def ring_place(index, count):
    return jnp.where(index % 2 == 0, index // 2, count - (index + 1) // 2)


def ring_slot(index, place, count):
    ahead = (ring_place(index, count) - place + count) % count
    near = jnp.where(ahead * 2 < count, 2 * ahead, 2 * (count - ahead) - 1)
    return jnp.where(ahead * 2 == count, count - 1, near)


def conv_kernel(place_ref, *refs, order, group_slots, shares):
    partial_refs = refs[: len(group_slots) * shares]
    (
        gout_ref, poles_ref, hc_ref, hs_ref, cos_ref, sin_ref, twist_ref,
        grad_ref, tgc_ref, tgs_ref, skip_ref, proj_ref, *scratch_refs,
    ) = refs[len(group_slots) * shares :]
    *held_refs, semaphores = scratch_refs
    fetch(partial_refs, held_refs, semaphores)
    rows, tokens = hc_ref.shape
    blocks, _, _, block_len = proj_ref.shape
    slot = 0
    for group, count in enumerate(group_slots):
        own_ref, *other_refs = held_refs[group * shares : (group + 1) * shares]
        total = own_ref[...]
        for other_ref in other_refs:
            total = total + other_ref[...].astype(F32)
        total = total.astype(BF16).astype(F32)
        for place in range(count):
            proj_ref[slot] = total[:, :, place * block_len : (place + 1) * block_len]
            slot += 1

    place = ring_place(place_ref[0], blocks)
    slots = [ring_slot(jnp.int32(b), place, blocks) for b in range(blocks)]

    def in_order(gate):
        return jnp.concatenate([proj_ref[slots[b], gate] for b in range(blocks)], 1)

    queries = in_order(0)
    keys = in_order(1)
    values = in_order(2)
    upper = jnp.concatenate(
        [gout_ref[b].astype(F32) for b in range(blocks)], 1
    )
    product = keys * values
    middle = upper * queries
    signals = jnp.concatenate([product, middle], 0)
    parts = two_parts(signals)
    even = dot(parts, cos_ref[...])
    uneven = dot(parts, sin_ref[...])
    even = even[: 2 * rows] + even[2 * rows :]
    uneven = uneven[: 2 * rows] + uneven[2 * rows :]
    ac, mc = even[:rows], even[rows:]
    as_, ms = uneven[:rows], uneven[rows:]
    hc = hc_ref[...]
    hs = hs_ref[...]
    scale = 1.0 / tokens
    cos_sums = jnp.concatenate([hc * ac - hs * as_, hc * mc + hs * ms], 0) * scale
    sin_sums = jnp.concatenate([hc * as_ + hs * ac, hc * ms - hs * mc], 0) * scale
    tc = (ac * mc + as_ * ms) * scale
    ts = (ac * ms - as_ * mc) * scale
    cos_half = twist_ref[0:1, :]
    sin_half = twist_ref[1:2, :]
    tgc_ref[...] = tc * cos_half - ts * sin_half
    tgs_ref[...] = ts * cos_half + tc * sin_half
    restored = wide_dot(cos_sums, cos_ref[...]) + wide_dot(sin_sums, sin_ref[...])
    skip = poles_ref[:, 2 * order : 2 * order + 1]
    mix = restored[rows:] + skip * middle
    grads = (upper * (restored[:rows] + skip * product), mix * values, mix * keys)
    for gate, grad in enumerate(grads):
        for b in range(blocks):
            column = pl.multiple_of(slots[b] * block_len, block_len)
            grad_ref[gate, :, pl.ds(column, block_len)] = grad[
                :, b * block_len : (b + 1) * block_len
            ].astype(BF16)
    skip_ref[...] = jnp.sum(product * middle, axis=1, keepdims=True)


def pole_kernel(poles_ref, tgc_ref, tgs_ref, cos_ref, sin_ref, skip_ref, out_ref, *, order):
    rows, tokens = tgc_ref.shape
    taps_grad = wide_dot(tgc_ref[...], cos_ref[...]) + wide_dot(tgs_ref[...], sin_ref[...])
    steps = lax.broadcasted_iota(jnp.int32, (rows, tokens), 1).astype(F32)
    for pole in range(order):
        residue = poles_ref[:, pole : pole + 1]
        rate = jnp.exp(poles_ref[:, order + pole : order + pole + 1])
        decayed = taps_grad * jnp.exp(-rate * steps)
        out_ref[:, pole : pole + 1] = jnp.sum(decayed, axis=1, keepdims=True)
        moment = jnp.sum(decayed * steps, axis=1, keepdims=True)
        out_ref[:, order + pole : order + pole + 1] = -residue * rate * moment
    out_ref[:, 2 * order : 2 * order + 1] = skip_ref[...]


def weight_kernel(place_ref, *refs, shares):
    grad_refs = refs[:shares]
    *feature_refs, out_ref, wide_ref, rows_ref, features_ref = refs[shares:]
    gates = out_ref.shape[0]
    part = grad_refs[0].shape[1]

    @pl.when(pl.program_id(0) == 0)
    def _():
        for share, grad_ref in enumerate(grad_refs):
            core, step = share // (shares // 2), 2 * (share % (shares // 2))
            owner = place_ref[1] + core * (1 - 2 * (place_ref[1] % 2))
            start = part_start((owner - step + shares) % shares, part, out_ref.shape[1])
            wide_ref[:, pl.ds(start, part), :] = grad_ref[...].astype(F32)
        rows_ref[...] = wide_ref[...].astype(BF16)

    row = 0
    for feature_ref in feature_refs:
        features_ref[row : row + feature_ref.shape[0], :] = feature_ref[...]
        row += feature_ref.shape[0]
    for gate in range(gates):
        out_ref[gate] = dot(rows_ref[gate], features_ref[...])


def call(kernel, outs, flops, transcendentals, *operands, scratch=(), indexed=False, late=()):
    size = sum(a.size * a.dtype.itemsize for a in operands) + sum(
        o.size * o.dtype.itemsize for o in outs
    )
    scratch_size = sum(math.prod(a.shape) * a.dtype.itemsize for a in scratch)
    if late:
        scratch = [*scratch, pltpu.SemaphoreType.DMA((len(late),))]
    limit = min(56 * MIB, 2 * (size + scratch_size) + 8 * MIB)
    whole = pl.BlockSpec(memory_space=pltpu.VMEM)
    specs = [whole] * len(operands)
    if indexed:
        specs[0] = pl.BlockSpec(memory_space=pltpu.SMEM)
    for operand in late:
        specs[operand] = pl.BlockSpec(memory_space=pltpu.HBM)
    return pl.pallas_call(
        kernel,
        out_shape=outs,
        in_specs=specs,
        out_specs=[whole] * len(outs),
        scratch_shapes=scratch,
        compiler_params=pltpu.CompilerParams(vmem_limit_bytes=limit),
        cost_estimate=pl.CostEstimate(
            flops=flops, bytes_accessed=size, transcendentals=transcendentals
        ),
    )(*operands)


def ring_routes(ring):
    ahead = [(a, ring[(i + 1) % len(ring)]) for i, a in enumerate(ring)]
    return ahead, [(b, a) for a, b in ahead]


def local(features, qkv_weight, grad_out, residues, log_rates, skip_gain):
    n_seq = lax.axis_size("seq")
    n_ch = lax.axis_size("ch")
    seq_index = lax.axis_index("seq")
    ch_index = lax.axis_index("ch")
    rows, gates, width = qkv_weight.shape
    block_len = features.shape[0]
    tokens = n_seq * block_len
    order = residues.shape[1]
    part = round_up(-(-rows // n_ch), 8)
    starts = [min(h * part, rows - part) for h in range(n_ch)]
    per_ch = n_seq // n_ch
    cos_table, sin_table, twist = (jnp.asarray(a) for a in wave_tables(tokens))

    place = jnp.stack([seq_index, ch_index]).astype(jnp.int32)

    ring = list(range(0, n_seq, 2)) + list(range(n_seq - 1, 0, -2))
    ahead, behind = ring_routes(ring)

    def send_on(pair):
        return lax.ppermute(pair[0], "seq", ahead), lax.ppermute(pair[1], "seq", behind)

    square = part * tokens * tokens
    spectrum = jax.ShapeDtypeStruct((part, tokens), F32)
    weight = qkv_weight.transpose(1, 0, 2)

    def project(pieces):
        span = sum(piece.shape[0] for piece in pieces)
        return call(
            functools.partial(project_kernel, pieces=len(pieces)),
            [
                jax.ShapeDtypeStruct((gates, part, span), F32 if d == 0 else BF16)
                for d in range(n_ch)
            ],
            2 * gates * rows * width * span, 0, place, weight, *pieces,
            scratch=[pltpu.VMEM((span, width), BF16), pltpu.VMEM((gates, rows, span), F32)],
            indexed=True, late=range(2, 2 + len(pieces)),
        )

    def to_owners(sums):
        return [sums[0]] + [
            lax.ppermute(sums[d], "ch", [(h, (h + d) % n_ch) for h in range(n_ch)])
            for d in range(1, n_ch)
        ]

    pair = send_on((features, features))
    pieces = [features, *pair]
    sums = list(project(pieces))
    grad_out, residues, log_rates, skip_gain, sums[0] = lax.optimization_barrier(
        (grad_out, residues, log_rates, skip_gain, sums[0])
    )
    (upper,) = call(
        functools.partial(pieces_kernel, rows=rows, n_ch=n_ch),
        (jax.ShapeDtypeStruct((n_seq, part, block_len), BF16),), 0, 0, grad_out,
    )
    upper = lax.all_to_all(upper, "seq", split_axis=0, concat_axis=0, tiled=True)
    group_slots = [3]
    partials = to_owners(sums)
    later = []
    for step in range(2, n_seq // 2):
        pair = send_on(pair)
        if step == 2:
            pair, upper = lax.optimization_barrier((pair, upper))
        pieces += pair
        later += pair
        if step % 2 == 1 or step == n_seq // 2 - 1:
            partials += to_owners(project(later))
            group_slots.append(len(later))
            later = []
    half = block_len // 2
    pair = send_on((pair[0][:half], pair[1][half:]))
    pieces += pair
    partials += to_owners(project(list(pair)))
    group_slots.append(1)

    spread = [((q % n_seq) * n_ch + q // n_seq, q) for q in range(n_seq * n_ch)]
    gather_back = [(b, a) for a, b in spread]
    upper = lax.ppermute(upper, ("seq", "ch"), spread)
    packed = jnp.concatenate([residues, log_rates, skip_gain[:, None]], 1)
    (poles,) = call(
        functools.partial(poles_kernel, rows=rows, n_ch=n_ch),
        (jax.ShapeDtypeStruct((part, packed.shape[1]), F32),), 0, 0, place, packed, indexed=True,
    )
    poles = lax.ppermute(poles, ("seq", "ch"), spread)
    hc, hs = call(
        functools.partial(taps_kernel, order=order), (spectrum, spectrum),
        8 * square, part * tokens * order, poles, cos_table, sin_table, twist,
    )

    grads, tgc, tgs, skip_sum = call(
        functools.partial(conv_kernel, order=order, group_slots=group_slots, shares=n_ch),
        (
            jax.ShapeDtypeStruct((gates, part, tokens), BF16),
            spectrum,
            spectrum,
            jax.ShapeDtypeStruct((part, 1), F32),
        ),
        32 * square, 0, place, *partials, upper, poles, hc, hs,
        cos_table, sin_table, twist,
        scratch=[pltpu.VMEM((n_seq, gates, part, block_len), F32)]
        + [pltpu.VMEM(a.shape, a.dtype) for a in partials],
        indexed=True, late=range(1, 1 + len(partials)),
    )

    swap = [(h, h ^ 1) for h in range(n_ch)]
    across = [
        lax.ppermute(grads, "ch", [(h, (h + d) % n_ch) for h in range(n_ch)])
        for d in range(2, n_ch, 2)
    ]
    swapped = lax.ppermute(grads, "ch", swap)
    tgc, swapped = lax.optimization_barrier((tgc, swapped))
    (pole_sums,) = call(
        functools.partial(pole_kernel, order=order),
        (jax.ShapeDtypeStruct((part, 2 * order + 1), F32),),
        8 * square, part * tokens * order, poles, tgc, tgs, cos_table, sin_table, skip_sum,
    )

    held = [grads] + across + [swapped] + [lax.ppermute(a, "ch", swap) for a in across]

    tile = min(512, width)
    weight_grad = pl.pallas_call(
        functools.partial(weight_kernel, shares=n_ch),
        out_shape=jax.ShapeDtypeStruct((gates, rows, width), F32),
        grid=(width // tile,),
        in_specs=[pl.BlockSpec(memory_space=pltpu.SMEM)]
        + [pl.BlockSpec((gates, part, tokens), lambda i: (0, 0, 0))] * n_ch
        + [pl.BlockSpec((piece.shape[0], tile), lambda i: (0, i)) for piece in pieces],
        out_specs=pl.BlockSpec((gates, rows, tile), lambda i: (0, 0, i)),
        scratch_shapes=[
            pltpu.VMEM((gates, rows, tokens), F32),
            pltpu.VMEM((gates, rows, tokens), BF16),
            pltpu.VMEM((tokens, tile), BF16),
        ],
        compiler_params=pltpu.CompilerParams(
            vmem_limit_bytes=min(56 * MIB, 16 * MIB + 12 * gates * rows * tokens + 4 * tokens * tile)
        ),
        cost_estimate=pl.CostEstimate(
            flops=2 * gates * rows * width * tokens,
            bytes_accessed=4 * gates * rows * width + 2 * tokens * (width + gates * rows),
            transcendentals=0,
        ),
    )(place, *held, *pieces)
    weight_grad = weight_grad.transpose(1, 0, 2)

    returned = lax.ppermute(pole_sums, ("seq", "ch"), gather_back)
    returned = jnp.broadcast_to(returned[None], (n_seq,) + returned.shape)
    returned = lax.all_to_all(returned, "seq", split_axis=0, concat_axis=0, tiled=True)
    pieces = []
    for block in range(per_ch):
        filled = 0
        for h, begin in enumerate(starts):
            if begin + part > filled:
                pieces.append(returned[block * n_ch + h, filled - begin :])
                filled = begin + part
    sums = jnp.concatenate(pieces, 0)
    return (weight_grad, sums[:, :order], sums[:, order : 2 * order], sums[:, 2 * order])


def solution(mesh):
    placed = (
        P("seq", "ch"),
        P("seq", None, "ch"),
        P("ch", "seq"),
        P("ch", None),
        P("ch", None),
        P("ch"),
    )
    return jax.shard_map(
        local,
        mesh=mesh,
        in_specs=placed,
        out_specs=(P("seq", None, "ch"), P("ch", None), P("ch", None), P("ch")),
        check_vma=False,
    )
```

```python
import functools
import math

import jax
import jax.numpy as jnp
import ml_dtypes
import numpy as np
from jax import lax
from jax.experimental import pallas as pl
from jax.experimental.pallas import tpu as pltpu
from jax.sharding import PartitionSpec as P

F32 = jnp.float32
BF16 = jnp.bfloat16
MIB = 1024 * 1024


def round_up(value, multiple):
    return -(-value // multiple) * multiple


def wave_tables(tokens):
    odd = 2 * np.arange(tokens, dtype=np.int64) + 1
    angles = (odd[:, None] * odd[None, :] % (8 * tokens)) * (math.pi / (4 * tokens))
    twist = odd * (math.pi / (4 * tokens))
    return (
        np.cos(angles).astype(ml_dtypes.bfloat16),
        np.sin(angles).astype(ml_dtypes.bfloat16),
        np.stack([np.cos(twist), np.sin(twist)]).astype(np.float32),
    )


def dot(left, right):
    return jnp.dot(left, right, preferred_element_type=F32)


def two_parts(value):
    high = value.astype(BF16)
    low = (value - high.astype(F32)).astype(BF16)
    return jnp.concatenate([high, low], 0)


def wide_dot(value, table):
    rows = value.shape[0]
    both = dot(two_parts(value), table)
    return both[:rows] + both[rows:]


def taps_kernel(poles_ref, cos_ref, sin_ref, twist_ref, hc_ref, hs_ref, *, order):
    rows, tokens = hc_ref.shape
    steps = lax.broadcasted_iota(jnp.int32, (rows, tokens), 1).astype(F32)
    taps = jnp.zeros((rows, tokens), F32)
    for pole in range(order):
        residue = poles_ref[:, pole : pole + 1]
        rate = jnp.exp(poles_ref[:, order + pole : order + pole + 1])
        taps = taps + residue * jnp.exp(-rate * steps)
    even = wide_dot(taps, cos_ref[...])
    uneven = wide_dot(taps, sin_ref[...])
    cos_half = twist_ref[0:1, :]
    sin_half = twist_ref[1:2, :]
    hc_ref[...] = cos_half * even + sin_half * uneven
    hs_ref[...] = cos_half * uneven - sin_half * even


def part_start(index, part, rows):
    return pl.multiple_of(jnp.minimum(index * part, rows - part), 8)


def pieces_kernel(place_ref, grad_ref, *refs, rows, n_ch):
    *out_refs, wide_ref = refs
    count = sum(out_ref.shape[0] for out_ref in out_refs)
    part = out_refs[0].shape[1]
    wide_ref[...] = grad_ref[...].astype(F32)
    slot = 0
    for out_ref in out_refs:
        for place in range(out_ref.shape[0]):
            piece = place_ref[0] ^ slot
            start = piece // n_ch * rows + part_start(piece % n_ch, part, rows)
            out_ref[place] = wide_ref[pl.ds(pl.multiple_of(start, 8), part), :].astype(BF16)
            slot += 1


def poles_kernel(place_ref, packed_ref, poles_ref, *, rows, n_ch):
    part = poles_ref.shape[0]
    own = place_ref[0]
    start = own // n_ch * rows + part_start(own % n_ch, part, rows)
    poles_ref[...] = packed_ref[pl.ds(pl.multiple_of(start, 8), part), :]


def fetch(sources, targets, semaphores):
    copies = [
        pltpu.make_async_copy(source, target, semaphores.at[i])
        for i, (source, target) in enumerate(zip(sources, targets))
    ]
    for copy in copies:
        copy.start()
    for copy in copies:
        copy.wait()


def project_kernel(place_ref, weight_ref, *refs, pieces):
    feature_refs = refs[:pieces]
    out_refs = refs[pieces:-3]
    features_ref, sums_ref, semaphores = refs[-3:]
    gates, _, _ = weight_ref.shape
    part = out_refs[0].shape[-2]
    targets, row = [], 0
    for feature_ref in feature_refs:
        targets.append(features_ref.at[pl.ds(row, feature_ref.shape[0]), :])
        row += feature_ref.shape[0]
    fetch(feature_refs, targets, semaphores)
    for gate in range(gates):
        sums_ref[gate] = lax.dot_general(
            weight_ref[gate], features_ref[...], (((1,), (1,)), ((), ())),
            preferred_element_type=F32,
        )
    rows = weight_ref.shape[1]
    if len(out_refs) == 1:
        for owner in range(out_refs[0].shape[0]):
            start = min(owner * part, rows - part)
            out_refs[0][owner] = sums_ref[:, start : start + part, :].astype(BF16)
        return
    for step, out_ref in enumerate(out_refs):
        start = part_start((place_ref[1] + step) % len(out_refs), part, rows)
        out_ref[...] = sums_ref[:, pl.ds(start, part), :].astype(out_ref.dtype)


def ring_place(index, count):
    return jnp.where(index % 2 == 0, index // 2, count - (index + 1) // 2)


def ring_slot(index, place, count):
    ahead = (ring_place(index, count) - place + count) % count
    near = jnp.where(ahead * 2 < count, 2 * ahead, 2 * (count - ahead) - 1)
    return jnp.where(ahead * 2 == count, count - 1, near)


def conv_kernel(place_ref, *refs, order, n_ch, group_slots, group_shares):
    shares = sum(group_shares)
    partial_refs = refs[:shares]
    (
        gout_ref, poles_ref, hc_ref, hs_ref, cos_ref, sin_ref, twist_ref,
        grad_ref, tgc_ref, tgs_ref, skip_ref, proj_ref, *scratch_refs,
    ) = refs[shares:]
    *held_refs, semaphores = scratch_refs
    fetch(partial_refs, held_refs, semaphores)
    rows, tokens = hc_ref.shape
    blocks, _, _, block_len = proj_ref.shape
    slot = 0
    for count, share in zip(group_slots, group_shares):
        own_ref, *other_refs = held_refs[:share]
        held_refs = held_refs[share:]
        total = own_ref[...].astype(F32)
        for other_ref in other_refs:
            total = total + other_ref[...].astype(F32)
        total = total.astype(BF16).astype(F32)
        for place in range(count):
            proj_ref[slot] = total[:, :, place * block_len : (place + 1) * block_len]
            slot += 1

    place = ring_place(place_ref[0], blocks)
    slots = [ring_slot(jnp.int32(b), place, blocks) for b in range(blocks)]

    def in_order(gate):
        return jnp.concatenate([proj_ref[slots[b], gate] for b in range(blocks)], 1)

    queries = in_order(0)
    keys = in_order(1)
    values = in_order(2)
    piece = (place_ref[0] * n_ch + place_ref[1]) % blocks
    upper = jnp.concatenate(
        [gout_ref[b ^ piece].astype(F32) for b in range(blocks)], 1
    )
    product = keys * values
    middle = upper * queries
    signals = jnp.concatenate([product, middle], 0)
    parts = two_parts(signals)
    even = dot(parts, cos_ref[...])
    uneven = dot(parts, sin_ref[...])
    even = even[: 2 * rows] + even[2 * rows :]
    uneven = uneven[: 2 * rows] + uneven[2 * rows :]
    ac, mc = even[:rows], even[rows:]
    as_, ms = uneven[:rows], uneven[rows:]
    hc = hc_ref[...]
    hs = hs_ref[...]
    scale = 1.0 / tokens
    cos_sums = jnp.concatenate([hc * ac - hs * as_, hc * mc + hs * ms], 0) * scale
    sin_sums = jnp.concatenate([hc * as_ + hs * ac, hc * ms - hs * mc], 0) * scale
    tc = (ac * mc + as_ * ms) * scale
    ts = (ac * ms - as_ * mc) * scale
    cos_half = twist_ref[0:1, :]
    sin_half = twist_ref[1:2, :]
    tgc_ref[...] = tc * cos_half - ts * sin_half
    tgs_ref[...] = ts * cos_half + tc * sin_half
    restored = wide_dot(cos_sums, cos_ref[...]) + wide_dot(sin_sums, sin_ref[...])
    skip = poles_ref[:, 2 * order : 2 * order + 1]
    mix = restored[rows:] + skip * middle
    grads = (upper * (restored[:rows] + skip * product), mix * values, mix * keys)
    for gate, grad in enumerate(grads):
        for b in range(blocks):
            column = pl.multiple_of(slots[b] * block_len, block_len)
            grad_ref[gate, :, pl.ds(column, block_len)] = grad[
                :, b * block_len : (b + 1) * block_len
            ].astype(BF16)
    skip_ref[...] = jnp.sum(product * middle, axis=1, keepdims=True)


def pole_kernel(poles_ref, tgc_ref, tgs_ref, cos_ref, sin_ref, skip_ref, out_ref, *, order):
    rows, tokens = tgc_ref.shape
    taps_grad = wide_dot(tgc_ref[...], cos_ref[...]) + wide_dot(tgs_ref[...], sin_ref[...])
    steps = lax.broadcasted_iota(jnp.int32, (rows, tokens), 1).astype(F32)
    for pole in range(order):
        residue = poles_ref[:, pole : pole + 1]
        rate = jnp.exp(poles_ref[:, order + pole : order + pole + 1])
        decayed = taps_grad * jnp.exp(-rate * steps)
        out_ref[:, pole : pole + 1] = jnp.sum(decayed, axis=1, keepdims=True)
        moment = jnp.sum(decayed * steps, axis=1, keepdims=True)
        out_ref[:, order + pole : order + pole + 1] = -residue * rate * moment
    out_ref[:, 2 * order : 2 * order + 1] = skip_ref[...]


def weight_kernel(place_ref, *refs, shares):
    grad_refs = refs[:shares]
    *feature_refs, out_ref, wide_ref, rows_ref, features_ref = refs[shares:]
    gates = out_ref.shape[0]
    part = grad_refs[0].shape[1]

    @pl.when(pl.program_id(0) == 0)
    def _():
        for share, grad_ref in enumerate(grad_refs):
            core, step = share // (shares // 2), 2 * (share % (shares // 2))
            owner = place_ref[1] + core * (1 - 2 * (place_ref[1] % 2))
            start = part_start((owner - step + shares) % shares, part, out_ref.shape[1])
            wide_ref[:, pl.ds(start, part), :] = grad_ref[...].astype(F32)
        rows_ref[...] = wide_ref[...].astype(BF16)

    row = 0
    for feature_ref in feature_refs:
        features_ref[row : row + feature_ref.shape[0], :] = feature_ref[...]
        row += feature_ref.shape[0]
    for gate in range(gates):
        out_ref[gate] = dot(rows_ref[gate], features_ref[...])


def assemble_kernel(place_ref, held_ref, out_ref, *, rows, n_ch):
    count, part, _ = held_ref.shape
    for piece in range(count):
        start = piece // n_ch * rows + min(piece % n_ch * part, rows - part)
        out_ref[start : start + part, :] = held_ref[piece ^ place_ref[0]]


def call(kernel, outs, flops, transcendentals, *operands, scratch=(), indexed=False, late=()):
    size = sum(a.size * a.dtype.itemsize for a in operands) + sum(
        o.size * o.dtype.itemsize for o in outs
    )
    scratch_size = sum(math.prod(a.shape) * a.dtype.itemsize for a in scratch)
    if late:
        scratch = [*scratch, pltpu.SemaphoreType.DMA((len(late),))]
    limit = min(56 * MIB, 2 * (size + scratch_size) + 8 * MIB)
    whole = pl.BlockSpec(memory_space=pltpu.VMEM)
    specs = [whole] * len(operands)
    if indexed:
        specs[0] = pl.BlockSpec(memory_space=pltpu.SMEM)
    for operand in late:
        specs[operand] = pl.BlockSpec(memory_space=pltpu.HBM)
    return pl.pallas_call(
        kernel,
        out_shape=outs,
        in_specs=specs,
        out_specs=[whole] * len(outs),
        scratch_shapes=scratch,
        compiler_params=pltpu.CompilerParams(vmem_limit_bytes=limit),
        cost_estimate=pl.CostEstimate(
            flops=flops, bytes_accessed=size, transcendentals=transcendentals
        ),
    )(*operands)


def ring_routes(ring):
    ahead = [(a, ring[(i + 1) % len(ring)]) for i, a in enumerate(ring)]
    return ahead, [(b, a) for a, b in ahead]


def local(features, qkv_weight, grad_out, residues, log_rates, skip_gain):
    n_seq = lax.axis_size("seq")
    n_ch = lax.axis_size("ch")
    seq_index = lax.axis_index("seq")
    ch_index = lax.axis_index("ch")
    rows, gates, width = qkv_weight.shape
    block_len = features.shape[0]
    tokens = n_seq * block_len
    order = residues.shape[1]
    part = round_up(-(-rows // n_ch), 8)
    cos_table, sin_table, twist = (jnp.asarray(a) for a in wave_tables(tokens))

    place = jnp.stack([seq_index, ch_index]).astype(jnp.int32)

    ring = list(range(0, n_seq, 2)) + list(range(n_seq - 1, 0, -2))
    ahead, behind = ring_routes(ring)

    def send_on(pair):
        return lax.ppermute(pair[0], "seq", ahead), lax.ppermute(pair[1], "seq", behind)

    square = part * tokens * tokens
    spectrum = jax.ShapeDtypeStruct((part, tokens), F32)
    weight = qkv_weight.transpose(1, 0, 2)

    def project(pieces, outs):
        span = sum(piece.shape[0] for piece in pieces)
        return call(
            functools.partial(project_kernel, pieces=len(pieces)), outs,
            2 * gates * rows * width * span, 0, place, weight, *pieces,
            scratch=[pltpu.VMEM((span, width), BF16), pltpu.VMEM((gates, rows, span), F32)],
            indexed=True, late=range(2, 2 + len(pieces)),
        )

    def early(pieces):
        span = sum(piece.shape[0] for piece in pieces)
        (sums,) = project(pieces, [jax.ShapeDtypeStruct((n_ch, gates, part, span), BF16)])
        return sums

    def to_owners(sums):
        return lax.psum_scatter(sums, "ch", scatter_dimension=0, tiled=False)

    def trade(array, reach):
        return lax.ppermute(array, "seq", [(d, d ^ reach) for d in range(n_seq)])

    pair = send_on((features, features))

    spread = [((q % n_seq) * n_ch + q // n_seq, q) for q in range(n_seq * n_ch)]
    gather_back = [(b, a) for a, b in spread]
    packed = jnp.concatenate([residues, log_rates, skip_gain[:, None]], 1)
    (poles,) = call(
        functools.partial(poles_kernel, rows=rows, n_ch=n_ch),
        (jax.ShapeDtypeStruct((part, packed.shape[1]), F32),), 0, 0, place, packed, indexed=True,
    )
    poles = lax.ppermute(poles, ("seq", "ch"), spread)
    hc, hs = call(
        functools.partial(taps_kernel, order=order), (spectrum, spectrum),
        8 * square, part * tokens * order, poles, cos_table, sin_table, twist,
    )

    low, high = call(
        functools.partial(pieces_kernel, rows=rows, n_ch=n_ch),
        [jax.ShapeDtypeStruct((n_seq // 2, part, block_len), BF16)] * 2, 0, 0, place, grad_out,
        scratch=[pltpu.VMEM(grad_out.shape, F32)], indexed=True,
    )
    high = trade(high, n_seq // 2)
    pair, hc, high = lax.optimization_barrier((pair, hc, high))
    upper = jnp.concatenate([low, high], 0)

    pieces = [features, *pair]
    group_slots = [3]
    next_pair = send_on(pair)
    sums = early(pieces)
    partials = [to_owners(sums)]
    reach = n_seq // 4
    while reach:
        shaped = upper.reshape(-1, 2, reach, part, block_len)
        moved = trade(shaped[:, 1], reach)
        upper = jnp.stack([shaped[:, 0], moved], 1).reshape(n_seq, part, block_len)
        reach //= 2
    for step in range(2, n_seq // 2):
        pair = next_pair
        if step == 2:
            pair, upper, sums = lax.optimization_barrier((pair, upper, sums))
            upper = lax.ppermute(upper, ("seq", "ch"), spread)
        pieces += pair
        if step < n_seq // 2 - 1:
            next_pair = send_on(pair)
        else:
            half = block_len // 2
            halves, pair = lax.optimization_barrier(((pair[0][:half], pair[1][half:]), pair))
            next_pair = send_on(halves)
        partials.append(to_owners(early(list(pair))))
        group_slots.append(2)
    pair = next_pair
    pieces += pair
    last = project(
        list(pair),
        [
            jax.ShapeDtypeStruct((gates, part, block_len), F32 if d == 0 else BF16)
            for d in range(n_ch)
        ],
    )
    group_slots.append(1)
    group_shares = [1] * len(partials) + [n_ch]
    partials += [last[0]] + [
        lax.ppermute(last[d], "ch", [(h, (h + d) % n_ch) for h in range(n_ch)])
        for d in range(1, n_ch)
    ]

    grads, tgc, tgs, skip_sum = call(
        functools.partial(
            conv_kernel, order=order, n_ch=n_ch, group_slots=group_slots, group_shares=group_shares
        ),
        (
            jax.ShapeDtypeStruct((gates, part, tokens), BF16),
            spectrum,
            spectrum,
            jax.ShapeDtypeStruct((part, 1), F32),
        ),
        32 * square, 0, place, *partials, upper, poles, hc, hs,
        cos_table, sin_table, twist,
        scratch=[pltpu.VMEM((n_seq, gates, part, block_len), F32)]
        + [pltpu.VMEM(a.shape, a.dtype) for a in partials],
        indexed=True, late=range(1, 1 + len(partials)),
    )

    swap = [(h, h ^ 1) for h in range(n_ch)]
    across = [
        lax.ppermute(grads, "ch", [(h, (h + d) % n_ch) for h in range(n_ch)])
        for d in range(2, n_ch, 2)
    ]
    swapped = lax.ppermute(grads, "ch", swap)
    tgc, swapped = lax.optimization_barrier((tgc, swapped))
    (pole_sums,) = call(
        functools.partial(pole_kernel, order=order),
        (jax.ShapeDtypeStruct((part, 2 * order + 1), F32),),
        8 * square, part * tokens * order, poles, tgc, tgs, cos_table, sin_table, skip_sum,
    )

    held = [grads] + across + [swapped] + [lax.ppermute(a, "ch", swap) for a in across]

    tile = min(512, width)
    weight_grad = pl.pallas_call(
        functools.partial(weight_kernel, shares=n_ch),
        out_shape=jax.ShapeDtypeStruct((gates, rows, width), F32),
        grid=(width // tile,),
        in_specs=[pl.BlockSpec(memory_space=pltpu.SMEM)]
        + [pl.BlockSpec((gates, part, tokens), lambda i: (0, 0, 0))] * n_ch
        + [pl.BlockSpec((piece.shape[0], tile), lambda i: (0, i)) for piece in pieces],
        out_specs=pl.BlockSpec((gates, rows, tile), lambda i: (0, 0, i)),
        scratch_shapes=[
            pltpu.VMEM((gates, rows, tokens), F32),
            pltpu.VMEM((gates, rows, tokens), BF16),
            pltpu.VMEM((tokens, tile), BF16),
        ],
        compiler_params=pltpu.CompilerParams(
            vmem_limit_bytes=min(56 * MIB, 16 * MIB + 12 * gates * rows * tokens + 4 * tokens * tile)
        ),
        cost_estimate=pl.CostEstimate(
            flops=2 * gates * rows * width * tokens,
            bytes_accessed=4 * gates * rows * width + 2 * tokens * (width + gates * rows),
            transcendentals=0,
        ),
    )(place, *held, *pieces)
    weight_grad = weight_grad.transpose(1, 0, 2)

    returned = lax.ppermute(pole_sums, ("seq", "ch"), gather_back)[None]
    reach = 1
    while reach < n_seq:
        returned = jnp.concatenate([returned, trade(returned, reach)], 0)
        reach *= 2
    (sums,) = call(
        functools.partial(assemble_kernel, rows=rows, n_ch=n_ch),
        [jax.ShapeDtypeStruct((residues.shape[0], 2 * order + 1), F32)], 0, 0, place, returned,
        indexed=True,
    )
    return (weight_grad, sums[:, :order], sums[:, order : 2 * order], sums[:, 2 * order])


def solution(mesh):
    placed = (
        P("seq", "ch"),
        P("seq", None, "ch"),
        P("ch", "seq"),
        P("ch", None),
        P("ch", None),
        P("ch"),
    )
    return jax.shard_map(
        local,
        mesh=mesh,
        in_specs=placed,
        out_specs=(P("seq", None, "ch"), P("ch", None), P("ch", None), P("ch")),
        check_vma=False,
    )
```

```python
import functools
import math

import jax
import jax.numpy as jnp
import ml_dtypes
import numpy as np
from jax import lax
from jax.experimental import pallas as pl
from jax.experimental.pallas import tpu as pltpu
from jax.sharding import PartitionSpec as P

F32 = jnp.float32
BF16 = jnp.bfloat16
MIB = 1024 * 1024


def round_up(value, multiple):
    return -(-value // multiple) * multiple


def wave_tables(tokens):
    odd = 2 * np.arange(tokens, dtype=np.int64) + 1
    angles = (odd[:, None] * odd[None, :] % (8 * tokens)) * (math.pi / (4 * tokens))
    twist = odd * (math.pi / (4 * tokens))
    return (
        np.cos(angles).astype(ml_dtypes.bfloat16),
        np.sin(angles).astype(ml_dtypes.bfloat16),
        np.stack([np.cos(twist), np.sin(twist)]).astype(np.float32),
    )


def dot(left, right):
    return jnp.dot(left, right, preferred_element_type=F32)


def two_parts(value):
    high = value.astype(BF16)
    low = (value - high.astype(F32)).astype(BF16)
    return jnp.concatenate([high, low], 0)


def wide_dot(value, table):
    rows = value.shape[0]
    both = dot(two_parts(value), table)
    return both[:rows] + both[rows:]


def taps_kernel(poles_ref, cos_ref, sin_ref, twist_ref, hc_ref, hs_ref, *, order):
    rows, tokens = hc_ref.shape
    steps = lax.broadcasted_iota(jnp.int32, (rows, tokens), 1).astype(F32)
    taps = jnp.zeros((rows, tokens), F32)
    for pole in range(order):
        residue = poles_ref[:, pole : pole + 1]
        rate = jnp.exp(poles_ref[:, order + pole : order + pole + 1])
        taps = taps + residue * jnp.exp(-rate * steps)
    even = wide_dot(taps, cos_ref[...])
    uneven = wide_dot(taps, sin_ref[...])
    cos_half = twist_ref[0:1, :]
    sin_half = twist_ref[1:2, :]
    hc_ref[...] = cos_half * even + sin_half * uneven
    hs_ref[...] = cos_half * uneven - sin_half * even


def part_start(index, part, rows):
    return pl.multiple_of(jnp.minimum(index * part, rows - part), 8)


def pieces_kernel(grad_ref, pieces_ref, *, rows, n_ch):
    part = pieces_ref.shape[1]
    grad = grad_ref[...].astype(F32)
    for piece in range(pieces_ref.shape[0]):
        start = piece // n_ch * rows + min(piece % n_ch * part, rows - part)
        pieces_ref[piece] = grad[start : start + part].astype(BF16)


def poles_kernel(place_ref, packed_ref, poles_ref, *, rows, n_ch):
    part = poles_ref.shape[0]
    own = place_ref[0]
    start = own // n_ch * rows + part_start(own % n_ch, part, rows)
    poles_ref[...] = packed_ref[pl.ds(pl.multiple_of(start, 8), part), :]


def fetch(sources, targets, semaphores):
    copies = [
        pltpu.make_async_copy(source, target, semaphores.at[i])
        for i, (source, target) in enumerate(zip(sources, targets))
    ]
    for copy in copies:
        copy.start()
    for copy in copies:
        copy.wait()


def project_kernel(place_ref, weight_ref, *refs, pieces):
    feature_refs = refs[:pieces]
    out_refs = refs[pieces:-3]
    features_ref, sums_ref, semaphores = refs[-3:]
    gates, _, _ = weight_ref.shape
    part = out_refs[0].shape[-2]
    targets, row = [], 0
    for feature_ref in feature_refs:
        targets.append(features_ref.at[pl.ds(row, feature_ref.shape[0]), :])
        row += feature_ref.shape[0]
    fetch(feature_refs, targets, semaphores)
    for gate in range(gates):
        sums_ref[gate] = lax.dot_general(
            weight_ref[gate], features_ref[...], (((1,), (1,)), ((), ())),
            preferred_element_type=F32,
        )
    rows = weight_ref.shape[1]
    for step, out_ref in enumerate(out_refs):
        start = part_start((place_ref[1] + step) % len(out_refs), part, rows)
        out_ref[...] = sums_ref[:, pl.ds(start, part), :].astype(out_ref.dtype)


def ring_place(index, count):
    return jnp.where(index % 2 == 0, index // 2, count - (index + 1) // 2)


def ring_slot(index, place, count):
    ahead = (ring_place(index, count) - place + count) % count
    near = jnp.where(ahead * 2 < count, 2 * ahead, 2 * (count - ahead) - 1)
    return jnp.where(ahead * 2 == count, count - 1, near)


def conv_kernel(place_ref, *refs, order, group_slots, shares):
    count = len(group_slots) * shares
    partial_refs = refs[:count]
    (
        gout_ref, poles_ref, hc_ref, hs_ref, cos_ref, sin_ref, twist_ref,
        grad_ref, tgc_ref, tgs_ref, skip_ref, proj_ref, *scratch_refs,
    ) = refs[count:]
    *held_refs, semaphores = scratch_refs
    fetch(partial_refs, held_refs, semaphores)
    rows, tokens = hc_ref.shape
    blocks, _, _, block_len = proj_ref.shape
    slot = 0
    for group, count in enumerate(group_slots):
        own_ref, *other_refs = held_refs[group * shares : (group + 1) * shares]
        total = own_ref[...]
        for other_ref in other_refs:
            total = total + other_ref[...].astype(F32)
        total = total.astype(BF16).astype(F32)
        for place in range(count):
            proj_ref[slot] = total[:, :, place * block_len : (place + 1) * block_len]
            slot += 1

    place = ring_place(place_ref[0], blocks)
    slots = [ring_slot(jnp.int32(b), place, blocks) for b in range(blocks)]

    def in_order(gate):
        return jnp.concatenate([proj_ref[slots[b], gate] for b in range(blocks)], 1)

    queries = in_order(0)
    keys = in_order(1)
    values = in_order(2)
    upper = jnp.concatenate([gout_ref[b].astype(F32) for b in range(blocks)], 1)
    product = keys * values
    middle = upper * queries
    signals = jnp.concatenate([product, middle], 0)
    parts = two_parts(signals)
    even = dot(parts, cos_ref[...])
    uneven = dot(parts, sin_ref[...])
    even = even[: 2 * rows] + even[2 * rows :]
    uneven = uneven[: 2 * rows] + uneven[2 * rows :]
    ac, mc = even[:rows], even[rows:]
    as_, ms = uneven[:rows], uneven[rows:]
    hc = hc_ref[...]
    hs = hs_ref[...]
    scale = 1.0 / tokens
    cos_sums = jnp.concatenate([hc * ac - hs * as_, hc * mc + hs * ms], 0) * scale
    sin_sums = jnp.concatenate([hc * as_ + hs * ac, hc * ms - hs * mc], 0) * scale
    tc = (ac * mc + as_ * ms) * scale
    ts = (ac * ms - as_ * mc) * scale
    cos_half = twist_ref[0:1, :]
    sin_half = twist_ref[1:2, :]
    tgc_ref[...] = tc * cos_half - ts * sin_half
    tgs_ref[...] = ts * cos_half + tc * sin_half
    restored = wide_dot(cos_sums, cos_ref[...]) + wide_dot(sin_sums, sin_ref[...])
    skip = poles_ref[:, 2 * order : 2 * order + 1]
    mix = restored[rows:] + skip * middle
    grads = (upper * (restored[:rows] + skip * product), mix * values, mix * keys)
    for gate, grad in enumerate(grads):
        for b in range(blocks):
            column = pl.multiple_of(slots[b] * block_len, block_len)
            grad_ref[gate, :, pl.ds(column, block_len)] = grad[
                :, b * block_len : (b + 1) * block_len
            ].astype(BF16)
    skip_ref[...] = jnp.sum(product * middle, axis=1, keepdims=True)


def pole_kernel(poles_ref, tgc_ref, tgs_ref, cos_ref, sin_ref, skip_ref, out_ref, *, order):
    rows, tokens = tgc_ref.shape
    taps_grad = wide_dot(tgc_ref[...], cos_ref[...]) + wide_dot(tgs_ref[...], sin_ref[...])
    steps = lax.broadcasted_iota(jnp.int32, (rows, tokens), 1).astype(F32)
    for pole in range(order):
        residue = poles_ref[:, pole : pole + 1]
        rate = jnp.exp(poles_ref[:, order + pole : order + pole + 1])
        decayed = taps_grad * jnp.exp(-rate * steps)
        out_ref[:, pole : pole + 1] = jnp.sum(decayed, axis=1, keepdims=True)
        moment = jnp.sum(decayed * steps, axis=1, keepdims=True)
        out_ref[:, order + pole : order + pole + 1] = -residue * rate * moment
    out_ref[:, 2 * order : 2 * order + 1] = skip_ref[...]


def share_start(own, share, shares, part, rows):
    core, step = share // (shares // 2), 2 * (share % (shares // 2))
    owner = own + core * (1 - 2 * (own % 2))
    return part_start((owner - step + shares) % shares, part, rows)


def weight_kernel(place_ref, *refs, shares):
    grad_refs = refs[:shares]
    *feature_refs, out_ref, wide_ref, rows_ref, features_ref = refs[shares:]
    gates = out_ref.shape[0]
    part = grad_refs[0].shape[1]

    @pl.when(pl.program_id(0) == 0)
    def _():
        for share, grad_ref in enumerate(grad_refs):
            start = share_start(place_ref[1], share, shares, part, out_ref.shape[1])
            wide_ref[:, pl.ds(start, part), :] = grad_ref[...].astype(F32)
        rows_ref[...] = wide_ref[...].astype(BF16)

    row = 0
    for feature_ref in feature_refs:
        features_ref[row : row + feature_ref.shape[0], :] = feature_ref[...]
        row += feature_ref.shape[0]
    for gate in range(gates):
        out_ref[gate] = dot(rows_ref[gate], features_ref[...])


def assemble_kernel(place_ref, *refs, rows, order):
    *block_refs, residue_ref, rate_ref, skip_ref, sums_ref = refs
    count = len(block_refs)
    sums_ref[...] = jnp.zeros_like(sums_ref)
    width = block_refs[0].shape[1]
    for turn, block_ref in enumerate(block_refs):
        block = (place_ref[0] + turn) % count
        sums_ref[pl.ds(pl.multiple_of(block * rows, 8), rows), :width] = block_ref[...]
    turned = sums_ref[...].T
    channels = residue_ref.shape[1]
    residue_ref[...] = turned[:order, :channels]
    rate_ref[...] = turned[order : 2 * order, :channels]
    skip_ref[...] = turned[2 * order : 2 * order + 1, :channels]


def gather_kernel(place_ref, *refs):
    *held_refs, out_ref = refs
    for share, held_ref in enumerate(held_refs):
        start = share_start(place_ref[1], share, len(held_refs), held_ref.shape[0], out_ref.shape[0])
        out_ref[pl.ds(start, held_ref.shape[0]), :] = held_ref[...]


def call(kernel, outs, flops, transcendentals, *operands, scratch=(), indexed=False, late=(), grant=0):
    size = sum(a.size * a.dtype.itemsize for a in operands) + sum(
        o.size * o.dtype.itemsize for o in outs
    )
    scratch_size = sum(math.prod(a.shape) * a.dtype.itemsize for a in scratch)
    if late:
        scratch = [*scratch, pltpu.SemaphoreType.DMA((len(late),))]
    limit = max(grant, min(56 * MIB, 2 * (size + scratch_size) + 8 * MIB))
    whole = pl.BlockSpec(memory_space=pltpu.VMEM)
    specs = [whole] * len(operands)
    if indexed:
        specs[0] = pl.BlockSpec(memory_space=pltpu.SMEM)
    for operand in late:
        specs[operand] = pl.BlockSpec(memory_space=pltpu.HBM)
    return pl.pallas_call(
        kernel,
        out_shape=outs,
        in_specs=specs,
        out_specs=[whole] * len(outs),
        scratch_shapes=scratch,
        compiler_params=pltpu.CompilerParams(vmem_limit_bytes=limit),
        cost_estimate=pl.CostEstimate(
            flops=flops, bytes_accessed=size, transcendentals=transcendentals
        ),
    )(*operands)


def ring_routes(ring):
    ahead = [(a, ring[(i + 1) % len(ring)]) for i, a in enumerate(ring)]
    return ahead, [(b, a) for a, b in ahead]


def local(features, qkv_weight, grad_out, residues, log_rates, skip_gain):
    n_seq = lax.axis_size("seq")
    n_ch = lax.axis_size("ch")
    seq_index = lax.axis_index("seq")
    ch_index = lax.axis_index("ch")
    rows, gates, width = qkv_weight.shape
    block_len = features.shape[0]
    tokens = n_seq * block_len
    order = residues.shape[1]
    part = round_up(-(-rows // n_ch), 8)
    cos_table, sin_table, twist = (jnp.asarray(a) for a in wave_tables(tokens))

    place = jnp.stack([seq_index, ch_index]).astype(jnp.int32)

    ring = list(range(0, n_seq, 2)) + list(range(n_seq - 1, 0, -2))
    ahead, behind = ring_routes(ring)

    def send_on(pair):
        return lax.ppermute(pair[0], "seq", ahead), lax.ppermute(pair[1], "seq", behind)

    square = part * tokens * tokens
    spectrum = jax.ShapeDtypeStruct((part, tokens), F32)
    weight = qkv_weight.transpose(1, 0, 2)

    def project(pieces):
        span = sum(piece.shape[0] for piece in pieces)
        sums = call(
            functools.partial(project_kernel, pieces=len(pieces)),
            [
                jax.ShapeDtypeStruct((gates, part, span), F32 if d == 0 else BF16)
                for d in range(n_ch)
            ],
            2 * gates * rows * width * span, 0, place, weight, *pieces,
            scratch=[pltpu.VMEM((span, width), BF16), pltpu.VMEM((gates, rows, span), F32)],
            indexed=True, late=range(2, 2 + len(pieces)),
        )
        return list(sums)

    def to_owners(sums):
        return [sums[0]] + [
            lax.ppermute(sums[d], "ch", [(h, (h + d) % n_ch) for h in range(n_ch)])
            for d in range(1, n_ch)
        ]

    pair = send_on((features, features))

    spread = [((q % n_seq) * n_ch + q // n_seq, q) for q in range(n_seq * n_ch)]
    (upper,) = call(
        functools.partial(pieces_kernel, rows=rows, n_ch=n_ch),
        (jax.ShapeDtypeStruct((n_seq, part, block_len), BF16),), 0, 0, grad_out,
    )
    upper = lax.all_to_all(upper, "seq", split_axis=0, concat_axis=0, tiled=True)
    pair, upper, residues, log_rates, skip_gain = lax.optimization_barrier(
        (pair, upper, residues, log_rates, skip_gain)
    )
    packed = jnp.concatenate([residues, log_rates, skip_gain[:, None]], 1)
    (poles,) = call(
        functools.partial(poles_kernel, rows=rows, n_ch=n_ch),
        (jax.ShapeDtypeStruct((part, packed.shape[1]), F32),), 0, 0, place, packed, indexed=True,
    )

    pieces = [features, *pair]
    group_slots = [3]
    next_pair = send_on(pair)
    sums = project(pieces)
    partials = to_owners(sums)
    for step in range(2, n_seq // 2):
        pair = next_pair
        if step == 2:
            pair, poles, upper, sums[0] = lax.optimization_barrier((pair, poles, upper, sums[0]))
            partials[0] = sums[0]
        pieces += pair
        if step < n_seq // 2 - 1:
            next_pair = send_on(pair)
        else:
            half = block_len // 2
            pair, poles, upper, partials[: n_ch + 1] = lax.optimization_barrier(
                (pair, poles, upper, partials[: n_ch + 1])
            )
            halves, pair = lax.optimization_barrier(((pair[0][:half], pair[1][half:]), pair))
            next_pair = send_on(halves)
        if step == 2:
            poles = lax.ppermute(poles, ("seq", "ch"), spread)
            upper = lax.ppermute(upper, ("seq", "ch"), spread)
        partials += to_owners(project(list(pair)))
        group_slots.append(2)
    pair = next_pair
    pieces += pair
    partials += to_owners(project(list(pair)))
    group_slots.append(1)
    hc, hs = call(
        functools.partial(taps_kernel, order=order), (spectrum, spectrum),
        8 * square, part * tokens * order, poles, cos_table, sin_table, twist,
    )

    grads, tgc, tgs, skip_sum = call(
        functools.partial(conv_kernel, order=order, group_slots=group_slots, shares=n_ch),
        (
            jax.ShapeDtypeStruct((gates, part, tokens), BF16),
            spectrum,
            spectrum,
            jax.ShapeDtypeStruct((part, 1), F32),
        ),
        32 * square, 0, place, *partials, upper, poles, hc, hs,
        cos_table, sin_table, twist,
        scratch=[pltpu.VMEM((n_seq, gates, part, block_len), F32)]
        + [pltpu.VMEM(a.shape, a.dtype) for a in partials],
        indexed=True, late=range(1, 1 + len(partials)), grant=60 * MIB,
    )

    swap = [(h, h ^ 1) for h in range(n_ch)]

    def chips(array):
        return [
            lax.ppermute(array, "ch", [(h, (h + d) % n_ch) for h in range(n_ch)])
            for d in range(2, n_ch, 2)
        ]

    across = chips(grads)
    swapped = lax.ppermute(grads, "ch", swap)
    tgc, swapped = lax.optimization_barrier((tgc, swapped))
    (pole_sums,) = call(
        functools.partial(pole_kernel, order=order),
        (jax.ShapeDtypeStruct((part, 2 * order + 1), F32),),
        8 * square, part * tokens * order, poles, tgc, tgs, cos_table, sin_table, skip_sum,
    )

    held = [grads] + across + [swapped] + [lax.ppermute(a, "ch", swap) for a in across]

    sums = [pole_sums] + chips(pole_sums)
    sums += [lax.ppermute(a, "ch", swap) for a in sums]
    (block_sums,) = call(
        gather_kernel, [jax.ShapeDtypeStruct((rows, 2 * order + 1), F32)], 0, 0, place, *sums,
        indexed=True,
    )
    turns = n_seq // n_ch
    blocks = []
    for turn in range(turns):
        route = [
            ((h * turns + (s + turn) % turns) * n_ch + s // turns, s * n_ch + h)
            for s in range(n_seq)
            for h in range(n_ch)
        ]
        blocks.append(lax.ppermute(block_sums, ("seq", "ch"), route))

    tile = min(512, width)
    weight_grad = pl.pallas_call(
        functools.partial(weight_kernel, shares=n_ch),
        out_shape=jax.ShapeDtypeStruct((gates, rows, width), F32),
        grid=(width // tile,),
        in_specs=[pl.BlockSpec(memory_space=pltpu.SMEM)]
        + [pl.BlockSpec((gates, part, tokens), lambda i: (0, 0, 0))] * n_ch
        + [pl.BlockSpec((piece.shape[0], tile), lambda i: (0, i)) for piece in pieces],
        out_specs=pl.BlockSpec((gates, rows, tile), lambda i: (0, 0, i)),
        scratch_shapes=[
            pltpu.VMEM((gates, rows, tokens), F32),
            pltpu.VMEM((gates, rows, tokens), BF16),
            pltpu.VMEM((tokens, tile), BF16),
        ],
        compiler_params=pltpu.CompilerParams(
            vmem_limit_bytes=60 * MIB
        ),
        cost_estimate=pl.CostEstimate(
            flops=2 * gates * rows * width * tokens,
            bytes_accessed=4 * gates * rows * width + 2 * tokens * (width + gates * rows),
            transcendentals=0,
        ),
    )(place, *held, *pieces)
    weight_grad = weight_grad.transpose(1, 0, 2)

    channels = residues.shape[0]
    by_pole = jax.ShapeDtypeStruct((order, channels), F32)
    residue_grad, rate_grad, skip_grad = call(
        functools.partial(assemble_kernel, rows=rows, order=order),
        [by_pole, by_pole, jax.ShapeDtypeStruct((1, channels), F32)], 0, 0, place, *blocks,
        scratch=[pltpu.VMEM((round_up(channels, 128), 128), F32)], indexed=True,
    )
    return (weight_grad, residue_grad.T, rate_grad.T, skip_grad.reshape(channels))


def solution(mesh):
    placed = (
        P("seq", "ch"),
        P("seq", None, "ch"),
        P("ch", "seq"),
        P("ch", None),
        P("ch", None),
        P("ch"),
    )
    return jax.shard_map(
        local,
        mesh=mesh,
        in_specs=placed,
        out_specs=(P("seq", None, "ch"), P("ch", None), P("ch", None), P("ch")),
        check_vma=False,
    )
```

```python
import functools
import math

import jax
import jax.numpy as jnp
import ml_dtypes
import numpy as np
from jax import lax
from jax.experimental import pallas as pl
from jax.experimental.pallas import tpu as pltpu
from jax.sharding import PartitionSpec as P

F32 = jnp.float32
BF16 = jnp.bfloat16
MIB = 1024 * 1024


def round_up(value, multiple):
    return -(-value // multiple) * multiple


def wave_tables(tokens):
    odd = 2 * np.arange(tokens, dtype=np.int64) + 1
    angles = (odd[:, None] * odd[None, :] % (8 * tokens)) * (math.pi / (4 * tokens))
    twist = odd * (math.pi / (4 * tokens))
    return (
        np.cos(angles).astype(ml_dtypes.bfloat16),
        np.sin(angles).astype(ml_dtypes.bfloat16),
        np.stack([np.cos(twist), np.sin(twist)]).astype(np.float32),
    )


def dot(left, right):
    return jnp.dot(left, right, preferred_element_type=F32)


def two_parts(value):
    high = value.astype(BF16)
    low = (value - high.astype(F32)).astype(BF16)
    return jnp.concatenate([high, low], 0)


def wide_dot(value, table):
    rows = value.shape[0]
    both = dot(two_parts(value), table)
    return both[:rows] + both[rows:]


def taps_kernel(poles_ref, cos_ref, sin_ref, twist_ref, hc_ref, hs_ref, *, order):
    rows, tokens = hc_ref.shape
    steps = lax.broadcasted_iota(jnp.int32, (rows, tokens), 1).astype(F32)
    taps = jnp.zeros((rows, tokens), F32)
    for pole in range(order):
        residue = poles_ref[:, pole : pole + 1]
        rate = jnp.exp(poles_ref[:, order + pole : order + pole + 1])
        taps = taps + residue * jnp.exp(-rate * steps)
    even = wide_dot(taps, cos_ref[...])
    uneven = wide_dot(taps, sin_ref[...])
    cos_half = twist_ref[0:1, :]
    sin_half = twist_ref[1:2, :]
    hc_ref[...] = cos_half * even + sin_half * uneven
    hs_ref[...] = cos_half * uneven - sin_half * even


def part_start(index, part, rows):
    return pl.multiple_of(jnp.minimum(index * part, rows - part), 8)


def pieces_kernel(grad_ref, pieces_ref, *, rows, n_ch):
    part = pieces_ref.shape[1]
    grad = grad_ref[...].astype(F32)
    for piece in range(pieces_ref.shape[0]):
        start = piece // n_ch * rows + min(piece % n_ch * part, rows - part)
        pieces_ref[piece] = grad[start : start + part].astype(BF16)


def poles_kernel(place_ref, packed_ref, poles_ref, *, rows, n_ch):
    part = poles_ref.shape[0]
    own = place_ref[0]
    start = own // n_ch * rows + part_start(own % n_ch, part, rows)
    poles_ref[...] = packed_ref[pl.ds(pl.multiple_of(start, 8), part), :]


def fetch(sources, targets, semaphores):
    copies = [
        pltpu.make_async_copy(source, target, semaphores.at[i])
        for i, (source, target) in enumerate(zip(sources, targets))
    ]
    for copy in copies:
        copy.start()
    return copies


def finish(copies):
    for copy in copies:
        copy.wait()


def project_kernel(place_ref, weight_ref, *refs, pieces):
    feature_refs = refs[:pieces]
    out_refs = refs[pieces:-3]
    features_ref, sums_ref, semaphores = refs[-3:]
    gates, _, _ = weight_ref.shape
    part = out_refs[0].shape[-2]
    targets, row = [], 0
    for feature_ref in feature_refs:
        targets.append(features_ref.at[pl.ds(row, feature_ref.shape[0]), :])
        row += feature_ref.shape[0]
    finish(fetch(feature_refs, targets, semaphores))
    for gate in range(gates):
        sums_ref[gate] = lax.dot_general(
            weight_ref[gate], features_ref[...], (((1,), (1,)), ((), ())),
            preferred_element_type=F32,
        )
    rows = weight_ref.shape[1]
    for step, out_ref in enumerate(out_refs):
        start = part_start((place_ref[1] + step) % len(out_refs), part, rows)
        out_ref[...] = sums_ref[:, pl.ds(start, part), :].astype(out_ref.dtype)


def ring_place(index, count):
    return jnp.where(index % 2 == 0, index // 2, count - (index + 1) // 2)


def ring_slot(index, place, count):
    ahead = (ring_place(index, count) - place + count) % count
    near = jnp.where(ahead * 2 < count, 2 * ahead, 2 * (count - ahead) - 1)
    return jnp.where(ahead * 2 == count, count - 1, near)


def conv_kernel(place_ref, *refs, order, group_slots, shares):
    count = len(group_slots) * shares
    partial_refs = refs[:count]
    (
        poles_ref, twist_ref, gout_from, hc_from, hs_from, cos_from, sin_from, grad_ref,
        tgc_ref, tgs_ref, skip_ref, proj_ref, *scratch_refs,
    ) = refs[count:]
    *held_refs, gout_ref, hc_ref, hs_ref, cos_ref, sin_ref, semaphores = scratch_refs
    copies = fetch(
        (*partial_refs, gout_from, cos_from, sin_from, hc_from, hs_from),
        (*held_refs, gout_ref, cos_ref, sin_ref, hc_ref, hs_ref),
        semaphores,
    )
    finish(copies[: count + 1])
    rows, tokens = hc_ref.shape
    blocks, _, _, block_len = proj_ref.shape
    slot = 0
    for group, span in enumerate(group_slots):
        own_ref, *other_refs = held_refs[group * shares : (group + 1) * shares]
        total = own_ref[...]
        for other_ref in other_refs:
            total = total + other_ref[...].astype(F32)
        total = total.astype(BF16).astype(F32)
        for place in range(span):
            proj_ref[slot] = total[:, :, place * block_len : (place + 1) * block_len]
            slot += 1

    place = ring_place(place_ref[0], blocks)
    slots = [ring_slot(jnp.int32(b), place, blocks) for b in range(blocks)]

    def in_order(gate):
        return jnp.concatenate([proj_ref[slots[b], gate] for b in range(blocks)], 1)

    queries = in_order(0)
    keys = in_order(1)
    values = in_order(2)
    upper = jnp.concatenate([gout_ref[b].astype(F32) for b in range(blocks)], 1)
    product = keys * values
    middle = upper * queries
    signals = jnp.concatenate([product, middle], 0)
    parts = two_parts(signals)
    finish(copies[count + 1 :])
    even = dot(parts, cos_ref[...])
    uneven = dot(parts, sin_ref[...])
    even = even[: 2 * rows] + even[2 * rows :]
    uneven = uneven[: 2 * rows] + uneven[2 * rows :]
    ac, mc = even[:rows], even[rows:]
    as_, ms = uneven[:rows], uneven[rows:]
    hc = hc_ref[...]
    hs = hs_ref[...]
    scale = 1.0 / tokens
    cos_sums = jnp.concatenate([hc * ac - hs * as_, hc * mc + hs * ms], 0) * scale
    sin_sums = jnp.concatenate([hc * as_ + hs * ac, hc * ms - hs * mc], 0) * scale
    tc = (ac * mc + as_ * ms) * scale
    ts = (ac * ms - as_ * mc) * scale
    cos_half = twist_ref[0:1, :]
    sin_half = twist_ref[1:2, :]
    tgc_ref[...] = tc * cos_half - ts * sin_half
    tgs_ref[...] = ts * cos_half + tc * sin_half
    restored = wide_dot(cos_sums, cos_ref[...]) + wide_dot(sin_sums, sin_ref[...])
    skip = poles_ref[:, 2 * order : 2 * order + 1]
    mix = restored[rows:] + skip * middle
    grads = (upper * (restored[:rows] + skip * product), mix * values, mix * keys)
    for gate, grad in enumerate(grads):
        for b in range(blocks):
            column = pl.multiple_of(slots[b] * block_len, block_len)
            grad_ref[gate, :, pl.ds(column, block_len)] = grad[
                :, b * block_len : (b + 1) * block_len
            ].astype(BF16)
    skip_ref[...] = jnp.sum(product * middle, axis=1, keepdims=True)


def pole_kernel(poles_ref, tgc_ref, tgs_ref, cos_ref, sin_ref, skip_ref, out_ref, *, order):
    rows, tokens = tgc_ref.shape
    taps_grad = wide_dot(tgc_ref[...], cos_ref[...]) + wide_dot(tgs_ref[...], sin_ref[...])
    steps = lax.broadcasted_iota(jnp.int32, (rows, tokens), 1).astype(F32)
    for pole in range(order):
        residue = poles_ref[:, pole : pole + 1]
        rate = jnp.exp(poles_ref[:, order + pole : order + pole + 1])
        decayed = taps_grad * jnp.exp(-rate * steps)
        out_ref[:, pole : pole + 1] = jnp.sum(decayed, axis=1, keepdims=True)
        moment = jnp.sum(decayed * steps, axis=1, keepdims=True)
        out_ref[:, order + pole : order + pole + 1] = -residue * rate * moment
    out_ref[:, 2 * order : 2 * order + 1] = skip_ref[...]


def share_start(own, share, shares, part, rows):
    core, step = share // (shares // 2), 2 * (share % (shares // 2))
    owner = own + core * (1 - 2 * (own % 2))
    return part_start((owner - step + shares) % shares, part, rows)


def weight_kernel(place_ref, *refs, shares):
    grad_refs = refs[:shares]
    *feature_refs, out_ref, wide_ref, rows_ref, features_ref = refs[shares:]
    gates = out_ref.shape[0]
    part = grad_refs[0].shape[1]

    @pl.when(pl.program_id(0) == 0)
    def _():
        for share, grad_ref in enumerate(grad_refs):
            start = share_start(place_ref[1], share, shares, part, out_ref.shape[1])
            wide_ref[:, pl.ds(start, part), :] = grad_ref[...].astype(F32)
        rows_ref[...] = wide_ref[...].astype(BF16)

    row = 0
    for feature_ref in feature_refs:
        features_ref[row : row + feature_ref.shape[0], :] = feature_ref[...]
        row += feature_ref.shape[0]
    for gate in range(gates):
        out_ref[gate] = dot(rows_ref[gate], features_ref[...])


def assemble_kernel(place_ref, *refs, rows, order):
    *block_refs, residue_ref, rate_ref, skip_ref, sums_ref = refs
    count = len(block_refs)
    sums_ref[...] = jnp.zeros_like(sums_ref)
    width = block_refs[0].shape[1]
    for turn, block_ref in enumerate(block_refs):
        block = (place_ref[0] + turn) % count
        sums_ref[pl.ds(pl.multiple_of(block * rows, 8), rows), :width] = block_ref[...]
    turned = sums_ref[...].T
    channels = residue_ref.shape[1]
    residue_ref[...] = turned[:order, :channels]
    rate_ref[...] = turned[order : 2 * order, :channels]
    skip_ref[...] = turned[2 * order : 2 * order + 1, :channels]


def gather_kernel(place_ref, *refs):
    *held_refs, out_ref = refs
    for share, held_ref in enumerate(held_refs):
        start = share_start(place_ref[1], share, len(held_refs), held_ref.shape[0], out_ref.shape[0])
        out_ref[pl.ds(start, held_ref.shape[0]), :] = held_ref[...]


def call(kernel, outs, flops, transcendentals, *operands, scratch=(), indexed=False, late=(), grant=0):
    size = sum(a.size * a.dtype.itemsize for a in operands) + sum(
        o.size * o.dtype.itemsize for o in outs
    )
    scratch_size = sum(math.prod(a.shape) * a.dtype.itemsize for a in scratch)
    if late:
        scratch = [*scratch, pltpu.SemaphoreType.DMA((len(late),))]
    limit = max(grant, min(56 * MIB, 2 * (size + scratch_size) + 8 * MIB))
    whole = pl.BlockSpec(memory_space=pltpu.VMEM)
    specs = [whole] * len(operands)
    if indexed:
        specs[0] = pl.BlockSpec(memory_space=pltpu.SMEM)
    for operand in late:
        specs[operand] = pl.BlockSpec(memory_space=pl.ANY)
    return pl.pallas_call(
        kernel,
        out_shape=outs,
        in_specs=specs,
        out_specs=[whole] * len(outs),
        scratch_shapes=scratch,
        compiler_params=pltpu.CompilerParams(vmem_limit_bytes=limit),
        cost_estimate=pl.CostEstimate(
            flops=flops, bytes_accessed=size, transcendentals=transcendentals
        ),
    )(*operands)


def ring_routes(ring):
    ahead = [(a, ring[(i + 1) % len(ring)]) for i, a in enumerate(ring)]
    return ahead, [(b, a) for a, b in ahead]


def local(features, qkv_weight, grad_out, residues, log_rates, skip_gain):
    n_seq = lax.axis_size("seq")
    n_ch = lax.axis_size("ch")
    seq_index = lax.axis_index("seq")
    ch_index = lax.axis_index("ch")
    rows, gates, width = qkv_weight.shape
    block_len = features.shape[0]
    tokens = n_seq * block_len
    order = residues.shape[1]
    part = round_up(-(-rows // n_ch), 8)
    cos_table, sin_table, twist = (jnp.asarray(a) for a in wave_tables(tokens))

    place = jnp.stack([seq_index, ch_index]).astype(jnp.int32)

    ring = list(range(0, n_seq, 2)) + list(range(n_seq - 1, 0, -2))
    ahead, behind = ring_routes(ring)

    def send_on(pair):
        return lax.ppermute(pair[0], "seq", ahead), lax.ppermute(pair[1], "seq", behind)

    square = part * tokens * tokens
    spectrum = jax.ShapeDtypeStruct((part, tokens), F32)
    weight = qkv_weight.transpose(1, 0, 2)

    def project(pieces):
        span = sum(piece.shape[0] for piece in pieces)
        sums = call(
            functools.partial(project_kernel, pieces=len(pieces)),
            [
                jax.ShapeDtypeStruct((gates, part, span), F32 if d == 0 else BF16)
                for d in range(n_ch)
            ],
            2 * gates * rows * width * span, 0, place, weight, *pieces,
            scratch=[pltpu.VMEM((span, width), BF16), pltpu.VMEM((gates, rows, span), F32)],
            indexed=True, late=range(2, 2 + len(pieces)),
        )
        return list(sums)

    def to_owners(sums):
        return [sums[0]] + [
            lax.ppermute(sums[d], "ch", [(h, (h + d) % n_ch) for h in range(n_ch)])
            for d in range(1, n_ch)
        ]

    pair = send_on((features, features))

    spread = [((q % n_seq) * n_ch + q // n_seq, q) for q in range(n_seq * n_ch)]
    packed = jnp.concatenate([residues, log_rates, skip_gain[:, None]], 1)
    (poles,) = call(
        functools.partial(poles_kernel, rows=rows, n_ch=n_ch),
        (jax.ShapeDtypeStruct((part, packed.shape[1]), F32),), 0, 0, place, packed, indexed=True,
    )
    grad_out, poles = lax.optimization_barrier((grad_out, poles))
    poles = lax.ppermute(poles, ("seq", "ch"), spread)
    (upper,) = call(
        functools.partial(pieces_kernel, rows=rows, n_ch=n_ch),
        (jax.ShapeDtypeStruct((n_seq, part, block_len), BF16),), 0, 0, grad_out,
    )
    upper = lax.all_to_all(upper, "seq", split_axis=0, concat_axis=0, tiled=True)
    pair, upper, poles = lax.optimization_barrier((pair, upper, poles))
    upper = lax.ppermute(upper, ("seq", "ch"), spread)

    pieces, group_slots, partials = [features, *pair], [], []
    waiting = list(pieces)
    next_pair = send_on(pair)
    for step in range(2, n_seq // 2):
        pair = next_pair
        if step == 2:
            pair, upper = lax.optimization_barrier((pair, upper))
        else:
            pair, sums[0] = lax.optimization_barrier((pair, sums[0]))
            partials[-n_ch] = sums[0]
        pieces += pair
        waiting += pair
        if step < n_seq // 2 - 1:
            next_pair = send_on(pair)
        else:
            half = block_len // 2
            halves, waiting = lax.optimization_barrier(((pair[0][:half], pair[1][half:]), waiting))
            next_pair = send_on(halves)
        sums = project(waiting)
        partials += to_owners(sums)
        group_slots.append(len(waiting))
        waiting = []
    pair = next_pair
    pieces += pair
    partials += to_owners(project(list(pair)))
    group_slots.append(1)
    hc, hs = call(
        functools.partial(taps_kernel, order=order), (spectrum, spectrum),
        8 * square, part * tokens * order, poles, cos_table, sin_table, twist,
    )

    tables = (upper, hc, hs, cos_table, sin_table)
    grads, tgc, tgs, skip_sum = call(
        functools.partial(conv_kernel, order=order, group_slots=group_slots, shares=n_ch),
        (
            jax.ShapeDtypeStruct((gates, part, tokens), BF16),
            spectrum,
            spectrum,
            jax.ShapeDtypeStruct((part, 1), F32),
        ),
        32 * square, 0, place, *partials, poles, twist, *tables,
        scratch=[pltpu.VMEM((n_seq, gates, part, block_len), F32)]
        + [pltpu.VMEM(a.shape, a.dtype) for a in (*partials, *tables)],
        indexed=True, grant=60 * MIB,
        late=[
            *range(1, 1 + len(partials)),
            *range(3 + len(partials), 3 + len(partials) + len(tables)),
        ],
    )

    swap = [(h, h ^ 1) for h in range(n_ch)]

    def chips(array):
        return [
            lax.ppermute(array, "ch", [(h, (h + d) % n_ch) for h in range(n_ch)])
            for d in range(2, n_ch, 2)
        ]

    across = chips(grads)
    swapped = lax.ppermute(grads, "ch", swap)
    (pole_sums,) = call(
        functools.partial(pole_kernel, order=order),
        (jax.ShapeDtypeStruct((part, 2 * order + 1), F32),),
        8 * square, part * tokens * order, poles, tgc, tgs, cos_table, sin_table, skip_sum,
    )

    across, pole_sums = lax.optimization_barrier((across, pole_sums))
    held = [grads] + across + [swapped] + [lax.ppermute(a, "ch", swap) for a in across]

    sums = [pole_sums] + chips(pole_sums)
    sums += [lax.ppermute(a, "ch", swap) for a in sums]
    (block_sums,) = call(
        gather_kernel, [jax.ShapeDtypeStruct((rows, 2 * order + 1), F32)], 0, 0, place, *sums,
        indexed=True,
    )
    turns = n_seq // n_ch
    blocks = []
    for turn in range(turns):
        route = [
            ((h * turns + (s + turn) % turns) * n_ch + s // turns, s * n_ch + h)
            for s in range(n_seq)
            for h in range(n_ch)
        ]
        blocks.append(lax.ppermute(block_sums, ("seq", "ch"), route))

    tile = min(512, width)
    weight_grad = pl.pallas_call(
        functools.partial(weight_kernel, shares=n_ch),
        out_shape=jax.ShapeDtypeStruct((gates, rows, width), F32),
        grid=(width // tile,),
        in_specs=[pl.BlockSpec(memory_space=pltpu.SMEM)]
        + [pl.BlockSpec((gates, part, tokens), lambda i: (0, 0, 0))] * n_ch
        + [pl.BlockSpec((piece.shape[0], tile), lambda i: (0, i)) for piece in pieces],
        out_specs=pl.BlockSpec((gates, rows, tile), lambda i: (0, 0, i)),
        scratch_shapes=[
            pltpu.VMEM((gates, rows, tokens), F32),
            pltpu.VMEM((gates, rows, tokens), BF16),
            pltpu.VMEM((tokens, tile), BF16),
        ],
        compiler_params=pltpu.CompilerParams(
            vmem_limit_bytes=60 * MIB
        ),
        cost_estimate=pl.CostEstimate(
            flops=2 * gates * rows * width * tokens,
            bytes_accessed=4 * gates * rows * width + 2 * tokens * (width + gates * rows),
            transcendentals=0,
        ),
    )(place, *held, *pieces)
    weight_grad, blocks = lax.optimization_barrier((weight_grad, blocks))
    weight_grad = weight_grad.transpose(1, 0, 2)

    channels = residues.shape[0]
    by_pole = jax.ShapeDtypeStruct((order, channels), F32)
    residue_grad, rate_grad, skip_grad = call(
        functools.partial(assemble_kernel, rows=rows, order=order),
        [by_pole, by_pole, jax.ShapeDtypeStruct((1, channels), F32)], 0, 0, place, *blocks,
        scratch=[pltpu.VMEM((round_up(channels, 128), 128), F32)], indexed=True,
    )
    return (weight_grad, residue_grad.T, rate_grad.T, skip_grad.reshape(channels))


def solution(mesh):
    placed = (
        P("seq", "ch"),
        P("seq", None, "ch"),
        P("ch", "seq"),
        P("ch", None),
        P("ch", None),
        P("ch"),
    )
    return jax.shard_map(
        local,
        mesh=mesh,
        in_specs=placed,
        out_specs=(P("seq", None, "ch"), P("ch", None), P("ch", None), P("ch")),
        check_vma=False,
    )
```

```python
import functools
import math

import jax
import jax.numpy as jnp
import ml_dtypes
import numpy as np
from jax import lax
from jax.experimental import pallas as pl
from jax.experimental.pallas import tpu as pltpu
from jax.sharding import PartitionSpec as P

F32 = jnp.float32
BF16 = jnp.bfloat16
MIB = 1024 * 1024


def round_up(value, multiple):
    return -(-value // multiple) * multiple


def wave_tables(tokens):
    odd = 2 * np.arange(tokens, dtype=np.int64) + 1
    angles = (odd[:, None] * odd[None, :] % (8 * tokens)) * (math.pi / (4 * tokens))
    twist = odd * (math.pi / (4 * tokens))
    return (
        np.cos(angles).astype(ml_dtypes.bfloat16),
        np.sin(angles).astype(ml_dtypes.bfloat16),
        np.stack([np.cos(twist), np.sin(twist)]).astype(np.float32),
    )


def dot(left, right):
    return jnp.dot(left, right, preferred_element_type=F32)


def two_parts(value):
    high = value.astype(BF16)
    low = (value - high.astype(F32)).astype(BF16)
    return jnp.concatenate([high, low], 0)


def wide_dot(value, table):
    rows = value.shape[0]
    both = dot(two_parts(value), table)
    return both[:rows] + both[rows:]


def taps_kernel(poles_ref, cos_ref, sin_ref, twist_ref, hc_ref, hs_ref, *, order):
    rows, tokens = hc_ref.shape
    steps = lax.broadcasted_iota(jnp.int32, (rows, tokens), 1).astype(F32)
    taps = jnp.zeros((rows, tokens), F32)
    for pole in range(order):
        residue = poles_ref[:, pole : pole + 1]
        rate = jnp.exp(poles_ref[:, order + pole : order + pole + 1])
        taps = taps + residue * jnp.exp(-rate * steps)
    even = wide_dot(taps, cos_ref[...])
    uneven = wide_dot(taps, sin_ref[...])
    cos_half = twist_ref[0:1, :]
    sin_half = twist_ref[1:2, :]
    hc_ref[...] = cos_half * even + sin_half * uneven
    hs_ref[...] = cos_half * uneven - sin_half * even


def part_start(index, part, rows):
    return pl.multiple_of(jnp.minimum(index * part, rows - part), 8)


def pieces_kernel(grad_ref, pieces_ref, *, rows):
    n_ch, blocks, part, _ = pieces_ref.shape
    grad = grad_ref[...].astype(F32)
    for owner in range(n_ch):
        for block in range(blocks):
            start = block * rows + min(owner * part, rows - part)
            pieces_ref[owner, block] = grad[start : start + part].astype(BF16)


def poles_kernel(place_ref, packed_ref, poles_ref, *, rows, n_ch):
    part = poles_ref.shape[0]
    own = place_ref[0]
    start = own // n_ch * rows + part_start(own % n_ch, part, rows)
    poles_ref[...] = packed_ref[pl.ds(pl.multiple_of(start, 8), part), :]


def fetch(sources, targets, semaphores):
    copies = [
        pltpu.make_async_copy(source, target, semaphores.at[i])
        for i, (source, target) in enumerate(zip(sources, targets))
    ]
    for copy in copies:
        copy.start()
    return copies


def finish(copies):
    for copy in copies:
        copy.wait()


def project_kernel(place_ref, weight_ref, *refs, pieces):
    feature_refs = refs[:pieces]
    out_refs = refs[pieces:-3]
    features_ref, sums_ref, semaphores = refs[-3:]
    gates, _, _ = weight_ref.shape
    part = out_refs[0].shape[-2]
    targets, row = [], 0
    for feature_ref in feature_refs:
        targets.append(features_ref.at[pl.ds(row, feature_ref.shape[0]), :])
        row += feature_ref.shape[0]
    finish(fetch(feature_refs, targets, semaphores))
    for gate in range(gates):
        sums_ref[gate] = lax.dot_general(
            weight_ref[gate], features_ref[...], (((1,), (1,)), ((), ())),
            preferred_element_type=F32,
        )
    rows = weight_ref.shape[1]
    for step, out_ref in enumerate(out_refs):
        start = part_start((place_ref[1] + step) % len(out_refs), part, rows)
        out_ref[...] = sums_ref[:, pl.ds(start, part), :].astype(out_ref.dtype)


def ring_place(index, count):
    return jnp.where(index % 2 == 0, index // 2, count - (index + 1) // 2)


def ring_slot(index, place, count):
    ahead = (ring_place(index, count) - place + count) % count
    near = jnp.where(ahead * 2 < count, 2 * ahead, 2 * (count - ahead) - 1)
    return jnp.where(ahead * 2 == count, count - 1, near)


def conv_kernel(place_ref, *refs, order, group_slots, shares):
    count = len(group_slots) * shares
    partial_refs = refs[:count]
    (
        gout_ref, poles_ref, hc_ref, hs_ref, cos_ref, sin_ref, twist_ref, grad_ref,
        tgc_ref, tgs_ref, skip_ref, proj_ref, *scratch_refs,
    ) = refs[count:]
    *held_refs, semaphores = scratch_refs
    finish(fetch(partial_refs, held_refs, semaphores))
    rows, tokens = hc_ref.shape
    blocks, _, _, block_len = proj_ref.shape
    slot = 0
    for group, span in enumerate(group_slots):
        own_ref, *other_refs = held_refs[group * shares : (group + 1) * shares]
        total = own_ref[...]
        for other_ref in other_refs:
            total = total + other_ref[...].astype(F32)
        total = total.astype(BF16).astype(F32)
        for place in range(span):
            proj_ref[slot] = total[:, :, place * block_len : (place + 1) * block_len]
            slot += 1

    place = ring_place(place_ref[0], blocks)
    slots = [ring_slot(jnp.int32(b), place, blocks) for b in range(blocks)]

    def in_order(gate):
        return jnp.concatenate([proj_ref[slots[b], gate] for b in range(blocks)], 1)

    queries = in_order(0)
    keys = in_order(1)
    values = in_order(2)
    upper = jnp.concatenate([gout_ref[b].astype(F32) for b in range(blocks)], 1)
    product = keys * values
    middle = upper * queries
    signals = jnp.concatenate([product, middle], 0)
    parts = two_parts(signals)
    even = dot(parts, cos_ref[...])
    uneven = dot(parts, sin_ref[...])
    even = even[: 2 * rows] + even[2 * rows :]
    uneven = uneven[: 2 * rows] + uneven[2 * rows :]
    ac, mc = even[:rows], even[rows:]
    as_, ms = uneven[:rows], uneven[rows:]
    hc = hc_ref[...]
    hs = hs_ref[...]
    scale = 1.0 / tokens
    cos_sums = jnp.concatenate([hc * ac - hs * as_, hc * mc + hs * ms], 0) * scale
    sin_sums = jnp.concatenate([hc * as_ + hs * ac, hc * ms - hs * mc], 0) * scale
    tc = (ac * mc + as_ * ms) * scale
    ts = (ac * ms - as_ * mc) * scale
    cos_half = twist_ref[0:1, :]
    sin_half = twist_ref[1:2, :]
    tgc_ref[...] = tc * cos_half - ts * sin_half
    tgs_ref[...] = ts * cos_half + tc * sin_half
    restored = wide_dot(cos_sums, cos_ref[...]) + wide_dot(sin_sums, sin_ref[...])
    skip = poles_ref[:, 2 * order : 2 * order + 1]
    mix = restored[rows:] + skip * middle
    grads = (upper * (restored[:rows] + skip * product), mix * values, mix * keys)
    for gate, grad in enumerate(grads):
        for b in range(blocks):
            column = pl.multiple_of(slots[b] * block_len, block_len)
            grad_ref[gate, :, pl.ds(column, block_len)] = grad[
                :, b * block_len : (b + 1) * block_len
            ].astype(BF16)
    skip_ref[...] = jnp.sum(product * middle, axis=1, keepdims=True)


def pole_kernel(poles_ref, tgc_ref, tgs_ref, cos_ref, sin_ref, skip_ref, out_ref, *, order):
    rows, tokens = tgc_ref.shape
    taps_grad = wide_dot(tgc_ref[...], cos_ref[...]) + wide_dot(tgs_ref[...], sin_ref[...])
    steps = lax.broadcasted_iota(jnp.int32, (rows, tokens), 1).astype(F32)
    for pole in range(order):
        residue = poles_ref[:, pole : pole + 1]
        rate = jnp.exp(poles_ref[:, order + pole : order + pole + 1])
        decayed = taps_grad * jnp.exp(-rate * steps)
        out_ref[:, pole : pole + 1] = jnp.sum(decayed, axis=1, keepdims=True)
        moment = jnp.sum(decayed * steps, axis=1, keepdims=True)
        out_ref[:, order + pole : order + pole + 1] = -residue * rate * moment
    out_ref[:, 2 * order : 2 * order + 1] = skip_ref[...]


def share_start(own, share, shares, part, rows):
    core, step = share // (shares // 2), 2 * (share % (shares // 2))
    owner = own + core * (1 - 2 * (own % 2))
    return part_start((owner - step + shares) % shares, part, rows)


def weight_kernel(place_ref, *refs, shares):
    grad_refs = refs[:shares]
    *feature_refs, out_ref, wide_ref, rows_ref, features_ref = refs[shares:]
    gates = out_ref.shape[0]
    part = grad_refs[0].shape[1]

    @pl.when(pl.program_id(0) == 0)
    def _():
        for share, grad_ref in enumerate(grad_refs):
            start = share_start(place_ref[1], share, shares, part, out_ref.shape[1])
            wide_ref[:, pl.ds(start, part), :] = grad_ref[...].astype(F32)
        rows_ref[...] = wide_ref[...].astype(BF16)

    row = 0
    for feature_ref in feature_refs:
        features_ref[row : row + feature_ref.shape[0], :] = feature_ref[...]
        row += feature_ref.shape[0]
    rows = out_ref.shape[1]
    if rows % 16 == 0:
        every = dot(rows_ref[...].reshape(gates * rows, -1), features_ref[...])
        out_ref[...] = every.reshape(out_ref.shape)
    else:
        for gate in range(gates):
            out_ref[gate] = dot(rows_ref[gate], features_ref[...])


def assemble_kernel(place_ref, *refs, rows, order):
    *block_refs, residue_ref, rate_ref, skip_ref, sums_ref = refs
    count = len(block_refs)
    sums_ref[...] = jnp.zeros_like(sums_ref)
    width = block_refs[0].shape[1]
    for turn, block_ref in enumerate(block_refs):
        block = (place_ref[0] + turn) % count
        sums_ref[pl.ds(pl.multiple_of(block * rows, 8), rows), :width] = block_ref[...]
    turned = sums_ref[...].T
    channels = residue_ref.shape[1]
    residue_ref[...] = turned[:order, :channels]
    rate_ref[...] = turned[order : 2 * order, :channels]
    skip_ref[...] = turned[2 * order : 2 * order + 1, :channels]


def gather_kernel(place_ref, *refs):
    *held_refs, out_ref = refs
    for share, held_ref in enumerate(held_refs):
        start = share_start(place_ref[1], share, len(held_refs), held_ref.shape[0], out_ref.shape[0])
        out_ref[pl.ds(start, held_ref.shape[0]), :] = held_ref[...]


def call(kernel, outs, flops, transcendentals, *operands, scratch=(), indexed=False, late=()):
    size = sum(a.size * a.dtype.itemsize for a in operands) + sum(
        o.size * o.dtype.itemsize for o in outs
    )
    scratch_size = sum(math.prod(a.shape) * a.dtype.itemsize for a in scratch)
    if late:
        scratch = [*scratch, pltpu.SemaphoreType.DMA((len(late),))]
    limit = min(56 * MIB, 2 * (size + scratch_size) + 8 * MIB)
    whole = pl.BlockSpec(memory_space=pltpu.VMEM)
    specs = [whole] * len(operands)
    if indexed:
        specs[0] = pl.BlockSpec(memory_space=pltpu.SMEM)
    for operand in late:
        specs[operand] = pl.BlockSpec(memory_space=pltpu.HBM)
    return pl.pallas_call(
        kernel,
        out_shape=outs,
        in_specs=specs,
        out_specs=[whole] * len(outs),
        scratch_shapes=scratch,
        compiler_params=pltpu.CompilerParams(vmem_limit_bytes=limit),
        cost_estimate=pl.CostEstimate(
            flops=flops, bytes_accessed=size, transcendentals=transcendentals
        ),
    )(*operands)


def ring_routes(ring):
    ahead = [(a, ring[(i + 1) % len(ring)]) for i, a in enumerate(ring)]
    return ahead, [(b, a) for a, b in ahead]


def local(features, qkv_weight, grad_out, residues, log_rates, skip_gain):
    n_seq = lax.axis_size("seq")
    n_ch = lax.axis_size("ch")
    seq_index = lax.axis_index("seq")
    ch_index = lax.axis_index("ch")
    rows, gates, width = qkv_weight.shape
    block_len = features.shape[0]
    tokens = n_seq * block_len
    order = residues.shape[1]
    part = round_up(-(-rows // n_ch), 8)
    cos_table, sin_table, twist = (jnp.asarray(a) for a in wave_tables(tokens))

    place = jnp.stack([seq_index, ch_index]).astype(jnp.int32)

    ring = list(range(0, n_seq, 2)) + list(range(n_seq - 1, 0, -2))
    ahead, behind = ring_routes(ring)

    def send_on(pair):
        return lax.ppermute(pair[0], "seq", ahead), lax.ppermute(pair[1], "seq", behind)

    square = part * tokens * tokens
    spectrum = jax.ShapeDtypeStruct((part, tokens), F32)
    weight = qkv_weight.transpose(1, 0, 2)

    def project(pieces):
        span = sum(piece.shape[0] for piece in pieces)
        sums = call(
            functools.partial(project_kernel, pieces=len(pieces)),
            [
                jax.ShapeDtypeStruct((gates, part, span), F32 if d == 0 else BF16)
                for d in range(n_ch)
            ],
            2 * gates * rows * width * span, 0, place, weight, *pieces,
            scratch=[pltpu.VMEM((span, width), BF16), pltpu.VMEM((gates, rows, span), F32)],
            indexed=True, late=range(2, 2 + len(pieces)),
        )
        return list(sums)

    def to_owners(sums):
        return [sums[0]] + [
            lax.ppermute(sums[d], "ch", [(h, (h + d) % n_ch) for h in range(n_ch)])
            for d in range(1, n_ch)
        ]

    pair = send_on((features, features))

    spread = [((q % n_seq) * n_ch + q // n_seq, q) for q in range(n_seq * n_ch)]
    packed = jnp.concatenate([residues, log_rates, skip_gain[:, None]], 1)
    (poles,) = call(
        functools.partial(poles_kernel, rows=rows, n_ch=n_ch),
        (jax.ShapeDtypeStruct((part, packed.shape[1]), F32),), 0, 0, place, packed, indexed=True,
    )
    grad_out, poles = lax.optimization_barrier((grad_out, poles))
    poles = lax.ppermute(poles, ("seq", "ch"), spread)
    (upper,) = call(
        functools.partial(pieces_kernel, rows=rows),
        (jax.ShapeDtypeStruct((n_ch, n_seq // n_ch, part, block_len), BF16),), 0, 0, grad_out,
    )
    upper = lax.all_to_all(upper, "ch", split_axis=0, concat_axis=0, tiled=True)
    pair, upper, poles = lax.optimization_barrier((pair, upper, poles))
    upper = upper.reshape(n_seq, part, block_len)
    upper = lax.all_to_all(upper, "seq", split_axis=0, concat_axis=0, tiled=True)

    pieces, group_slots, partials = [features, *pair], [], []
    waiting = list(pieces)
    next_pair = send_on(pair)
    for step in range(2, n_seq // 2):
        pair = next_pair
        if step == 2:
            pair, upper = lax.optimization_barrier((pair, upper))
        else:
            pair, sums[0] = lax.optimization_barrier((pair, sums[0]))
            partials[-n_ch] = sums[0]
        pieces += pair
        waiting += pair
        if step < n_seq // 2 - 1:
            next_pair = send_on(pair)
        else:
            half = block_len // 2
            halves, waiting = lax.optimization_barrier(((pair[0][:half], pair[1][half:]), waiting))
            next_pair = send_on(halves)
        sums = project(waiting)
        partials += to_owners(sums)
        group_slots.append(len(waiting))
        waiting = []
    pair = next_pair
    pieces += pair
    partials += to_owners(project(list(pair)))
    group_slots.append(1)
    hc, hs = call(
        functools.partial(taps_kernel, order=order), (spectrum, spectrum),
        8 * square, part * tokens * order, poles, cos_table, sin_table, twist,
    )

    grads, tgc, tgs, skip_sum = call(
        functools.partial(conv_kernel, order=order, group_slots=group_slots, shares=n_ch),
        (
            jax.ShapeDtypeStruct((gates, part, tokens), BF16),
            spectrum,
            spectrum,
            jax.ShapeDtypeStruct((part, 1), F32),
        ),
        32 * square, 0, place, *partials, upper, poles, hc, hs, cos_table, sin_table, twist,
        scratch=[pltpu.VMEM((n_seq, gates, part, block_len), F32)]
        + [pltpu.VMEM(a.shape, a.dtype) for a in partials],
        indexed=True, late=range(1, 1 + len(partials)),
    )

    swap = [(h, h ^ 1) for h in range(n_ch)]

    def chips(array):
        return [
            lax.ppermute(array, "ch", [(h, (h + d) % n_ch) for h in range(n_ch)])
            for d in range(2, n_ch, 2)
        ]

    across = chips(grads)
    swapped = lax.ppermute(grads, "ch", swap)
    (pole_sums,) = call(
        functools.partial(pole_kernel, order=order),
        (jax.ShapeDtypeStruct((part, 2 * order + 1), F32),),
        8 * square, part * tokens * order, poles, tgc, tgs, cos_table, sin_table, skip_sum,
    )

    sums = [pole_sums] + chips(pole_sums)
    across, sums = lax.optimization_barrier((across, sums))
    held = [grads] + across + [swapped] + [lax.ppermute(a, "ch", swap) for a in across]
    sums += [lax.ppermute(a, "ch", swap) for a in sums]
    (block_sums,) = call(
        gather_kernel, [jax.ShapeDtypeStruct((rows, 2 * order + 1), F32)], 0, 0, place, *sums,
        indexed=True,
    )
    turns = n_seq // n_ch
    blocks = []
    for turn in range(turns):
        route = [
            ((h * turns + (s + turn) % turns) * n_ch + s // turns, s * n_ch + h)
            for s in range(n_seq)
            for h in range(n_ch)
        ]
        blocks.append(lax.ppermute(block_sums, ("seq", "ch"), route))

    tile = min(512, width)
    weight_grad = pl.pallas_call(
        functools.partial(weight_kernel, shares=n_ch),
        out_shape=jax.ShapeDtypeStruct((gates, rows, width), F32),
        grid=(width // tile,),
        in_specs=[pl.BlockSpec(memory_space=pltpu.SMEM)]
        + [pl.BlockSpec((gates, part, tokens), lambda i: (0, 0, 0))] * n_ch
        + [pl.BlockSpec((piece.shape[0], tile), lambda i: (0, i)) for piece in pieces],
        out_specs=pl.BlockSpec((gates, rows, tile), lambda i: (0, 0, i)),
        scratch_shapes=[
            pltpu.VMEM((gates, rows, tokens), F32),
            pltpu.VMEM((gates, rows, tokens), BF16),
            pltpu.VMEM((tokens, tile), BF16),
        ],
        compiler_params=pltpu.CompilerParams(
            vmem_limit_bytes=min(56 * MIB, 16 * MIB + 12 * gates * rows * tokens + 4 * tokens * tile)
        ),
        cost_estimate=pl.CostEstimate(
            flops=2 * gates * rows * width * tokens,
            bytes_accessed=4 * gates * rows * width + 2 * tokens * (width + gates * rows),
            transcendentals=0,
        ),
    )(place, *held, *pieces)
    weight_grad, blocks = lax.optimization_barrier((weight_grad, blocks))
    weight_grad = weight_grad.transpose(1, 0, 2)

    channels = residues.shape[0]
    by_pole = jax.ShapeDtypeStruct((order, channels), F32)
    residue_grad, rate_grad, skip_grad = call(
        functools.partial(assemble_kernel, rows=rows, order=order),
        [by_pole, by_pole, jax.ShapeDtypeStruct((1, channels), F32)], 0, 0, place, *blocks,
        scratch=[pltpu.VMEM((round_up(channels, 128), 128), F32)], indexed=True,
    )
    return (weight_grad, residue_grad.T, rate_grad.T, skip_grad.reshape(channels))


def solution(mesh):
    placed = (
        P("seq", "ch"),
        P("seq", None, "ch"),
        P("ch", "seq"),
        P("ch", None),
        P("ch", None),
        P("ch"),
    )
    return jax.shard_map(
        local,
        mesh=mesh,
        in_specs=placed,
        out_specs=(P("seq", None, "ch"), P("ch", None), P("ch", None), P("ch")),
        check_vma=False,
    )
```

```python
import functools
import math

import jax
import jax.numpy as jnp
import ml_dtypes
import numpy as np
from jax import lax
from jax.experimental import pallas as pl
from jax.experimental.pallas import tpu as pltpu
from jax.sharding import PartitionSpec as P

F32 = jnp.float32
BF16 = jnp.bfloat16
MIB = 1024 * 1024


def round_up(value, multiple):
    return -(-value // multiple) * multiple


def wave_tables(tokens):
    odd = 2 * np.arange(tokens, dtype=np.int64) + 1
    angles = (odd[:, None] * odd[None, :] % (8 * tokens)) * (math.pi / (4 * tokens))
    twist = odd * (math.pi / (4 * tokens))
    return (
        np.cos(angles).astype(ml_dtypes.bfloat16),
        np.sin(angles).astype(ml_dtypes.bfloat16),
        np.stack([np.cos(twist), np.sin(twist)]).astype(np.float32),
    )


def dot(left, right):
    return jnp.dot(left, right, preferred_element_type=F32)


def two_parts(value):
    high = value.astype(BF16)
    low = (value - high.astype(F32)).astype(BF16)
    return jnp.concatenate([high, low], 0)


def wide_dot(value, table):
    rows = value.shape[0]
    both = dot(two_parts(value), table)
    return both[:rows] + both[rows:]


def taps_kernel(poles_ref, cos_ref, sin_ref, twist_ref, hc_ref, hs_ref, *, order):
    rows, tokens = hc_ref.shape
    steps = lax.broadcasted_iota(jnp.int32, (rows, tokens), 1).astype(F32)
    taps = jnp.zeros((rows, tokens), F32)
    for pole in range(order):
        residue = poles_ref[:, pole : pole + 1]
        rate = jnp.exp(poles_ref[:, order + pole : order + pole + 1])
        taps = taps + residue * jnp.exp(-rate * steps)
    even = wide_dot(taps, cos_ref[...])
    uneven = wide_dot(taps, sin_ref[...])
    cos_half = twist_ref[0:1, :]
    sin_half = twist_ref[1:2, :]
    hc_ref[...] = cos_half * even + sin_half * uneven
    hs_ref[...] = cos_half * uneven - sin_half * even


def part_start(index, part, rows):
    return pl.multiple_of(jnp.minimum(index * part, rows - part), 8)


def pieces_kernel(grad_ref, pieces_ref, *, rows):
    n_ch, blocks, part, _ = pieces_ref.shape
    grad = grad_ref[...].astype(F32)
    for owner in range(n_ch):
        for block in range(blocks):
            start = block * rows + min(owner * part, rows - part)
            pieces_ref[owner, block] = grad[start : start + part].astype(BF16)


def poles_kernel(place_ref, packed_ref, poles_ref, *, rows, n_ch):
    part = poles_ref.shape[0]
    own = place_ref[0]
    start = own // n_ch * rows + part_start(own % n_ch, part, rows)
    poles_ref[...] = packed_ref[pl.ds(pl.multiple_of(start, 8), part), :]


def fetch(sources, targets, semaphores):
    copies = [
        pltpu.make_async_copy(source, target, semaphores.at[i])
        for i, (source, target) in enumerate(zip(sources, targets))
    ]
    for copy in copies:
        copy.start()
    return copies


def finish(copies):
    for copy in copies:
        copy.wait()


def project_kernel(place_ref, weight_ref, *refs, pieces):
    feature_refs = refs[:pieces]
    out_refs = refs[pieces:-3]
    features_ref, sums_ref, semaphores = refs[-3:]
    gates, _, _ = weight_ref.shape
    part = out_refs[0].shape[-2]
    targets, row = [], 0
    for feature_ref in feature_refs:
        targets.append(features_ref.at[pl.ds(row, feature_ref.shape[0]), :])
        row += feature_ref.shape[0]
    finish(fetch(feature_refs, targets, semaphores))
    for gate in range(gates):
        sums_ref[gate] = lax.dot_general(
            weight_ref[gate], features_ref[...], (((1,), (1,)), ((), ())),
            preferred_element_type=F32,
        )
    rows = weight_ref.shape[1]
    for step, out_ref in enumerate(out_refs):
        start = part_start(place_ref[1] ^ step, part, rows)
        out_ref[...] = sums_ref[:, pl.ds(start, part), :].astype(out_ref.dtype)


def ring_place(index, count):
    return jnp.where(index % 2 == 0, index // 2, count - (index + 1) // 2)


def ring_slot(index, place, count):
    ahead = (ring_place(index, count) - place + count) % count
    near = jnp.where(ahead * 2 < count, 2 * ahead, 2 * (count - ahead) - 1)
    return jnp.where(ahead * 2 == count, count - 1, near)


def conv_kernel(place_ref, *refs, order, group_slots, shares):
    count = len(group_slots) * shares
    partial_refs = refs[:count]
    (
        gout_ref, poles_ref, hc_ref, hs_ref, cos_ref, sin_ref, twist_ref, grad_ref,
        tgc_ref, tgs_ref, skip_ref, proj_ref, *scratch_refs,
    ) = refs[count:]
    *held_refs, semaphores = scratch_refs
    finish(fetch(partial_refs, held_refs, semaphores))
    rows, tokens = hc_ref.shape
    blocks, _, _, block_len = proj_ref.shape
    slot = 0
    for group, span in enumerate(group_slots):
        own_ref, *other_refs = held_refs[group * shares : (group + 1) * shares]
        total = own_ref[...]
        for other_ref in other_refs:
            total = total + other_ref[...].astype(F32)
        total = total.astype(BF16).astype(F32)
        for place in range(span):
            proj_ref[slot] = total[:, :, place * block_len : (place + 1) * block_len]
            slot += 1

    place = ring_place(place_ref[0], blocks)
    slots = [ring_slot(jnp.int32(b), place, blocks) for b in range(blocks)]

    def in_order(gate):
        return jnp.concatenate([proj_ref[slots[b], gate] for b in range(blocks)], 1)

    queries = in_order(0)
    keys = in_order(1)
    values = in_order(2)
    upper = jnp.concatenate([gout_ref[b].astype(F32) for b in range(blocks)], 1)
    product = keys * values
    middle = upper * queries
    signals = jnp.concatenate([product, middle], 0)
    parts = two_parts(signals)
    even = dot(parts, cos_ref[...])
    uneven = dot(parts, sin_ref[...])
    even = even[: 2 * rows] + even[2 * rows :]
    uneven = uneven[: 2 * rows] + uneven[2 * rows :]
    ac, mc = even[:rows], even[rows:]
    as_, ms = uneven[:rows], uneven[rows:]
    hc = hc_ref[...]
    hs = hs_ref[...]
    scale = 1.0 / tokens
    cos_sums = jnp.concatenate([hc * ac - hs * as_, hc * mc + hs * ms], 0) * scale
    sin_sums = jnp.concatenate([hc * as_ + hs * ac, hc * ms - hs * mc], 0) * scale
    tc = (ac * mc + as_ * ms) * scale
    ts = (ac * ms - as_ * mc) * scale
    cos_half = twist_ref[0:1, :]
    sin_half = twist_ref[1:2, :]
    tgc_ref[...] = tc * cos_half - ts * sin_half
    tgs_ref[...] = ts * cos_half + tc * sin_half
    restored = wide_dot(cos_sums, cos_ref[...]) + wide_dot(sin_sums, sin_ref[...])
    skip = poles_ref[:, 2 * order : 2 * order + 1]
    mix = restored[rows:] + skip * middle
    grads = (upper * (restored[:rows] + skip * product), mix * values, mix * keys)
    for gate, grad in enumerate(grads):
        for b in range(blocks):
            column = pl.multiple_of(slots[b] * block_len, block_len)
            grad_ref[gate, :, pl.ds(column, block_len)] = grad[
                :, b * block_len : (b + 1) * block_len
            ].astype(BF16)
    skip_ref[...] = jnp.sum(product * middle, axis=1, keepdims=True)


def pole_kernel(poles_ref, tgc_ref, tgs_ref, cos_ref, sin_ref, skip_ref, out_ref, *, order):
    rows, tokens = tgc_ref.shape
    taps_grad = wide_dot(tgc_ref[...], cos_ref[...]) + wide_dot(tgs_ref[...], sin_ref[...])
    out_ref[...] = jnp.zeros_like(out_ref)
    steps = lax.broadcasted_iota(jnp.int32, (rows, tokens), 1).astype(F32)
    for pole in range(order):
        residue = poles_ref[:, pole : pole + 1]
        rate = jnp.exp(poles_ref[:, order + pole : order + pole + 1])
        decayed = taps_grad * jnp.exp(-rate * steps)
        out_ref[:, pole : pole + 1] = jnp.sum(decayed, axis=1, keepdims=True)
        moment = jnp.sum(decayed * steps, axis=1, keepdims=True)
        out_ref[:, order + pole : order + pole + 1] = -residue * rate * moment
    out_ref[:, 2 * order : 2 * order + 1] = skip_ref[...]


def share_start(own, share, shares, part, rows):
    core, step = share // (shares // 2), 2 * (share % (shares // 2))
    return part_start(own ^ core ^ step, part, rows)


def weight_kernel(place_ref, *refs, shares):
    grad_refs = refs[:shares]
    *feature_refs, out_ref, wide_ref, rows_ref, features_ref = refs[shares:]
    gates = out_ref.shape[0]
    part = grad_refs[0].shape[1]

    @pl.when(pl.program_id(0) == 0)
    def _():
        for share, grad_ref in enumerate(grad_refs):
            start = share_start(place_ref[1], share, shares, part, out_ref.shape[1])
            wide_ref[:, pl.ds(start, part), :] = grad_ref[...].astype(F32)
        rows_ref[...] = wide_ref[...].astype(BF16)

    row = 0
    for feature_ref in feature_refs:
        features_ref[row : row + feature_ref.shape[0], :] = feature_ref[...]
        row += feature_ref.shape[0]
    rows = out_ref.shape[1]
    if rows % 16 == 0:
        every = dot(rows_ref[...].reshape(gates * rows, -1), features_ref[...])
        out_ref[...] = every.reshape(out_ref.shape)
    else:
        for gate in range(gates):
            out_ref[gate] = dot(rows_ref[gate], features_ref[...])


def split_kernel(place_ref, held_ref, *out_refs):
    for step, out_ref in enumerate(out_refs):
        out_ref[...] = held_ref[place_ref[1] ^ step]


def assemble_kernel(place_ref, *refs, rows, order):
    *piece_refs, residue_ref, rate_ref, skip_ref, sums_ref = refs
    blocks, part, _ = piece_refs[0].shape
    sums_ref[...] = jnp.zeros_like(sums_ref)
    for step, piece_ref in enumerate(piece_refs):
        start = part_start(place_ref[1] ^ step, part, rows)
        for block in range(blocks):
            row = pl.multiple_of(block * rows + start, 8)
            sums_ref[pl.ds(row, part), :] = piece_ref[block]
    turned = sums_ref[...].T
    channels = residue_ref.shape[1]
    residue_ref[...] = turned[:order, :channels]
    rate_ref[...] = turned[order : 2 * order, :channels]
    skip_ref[...] = turned[2 * order : 2 * order + 1, :channels]


def call(kernel, outs, flops, transcendentals, *operands, scratch=(), indexed=False, late=()):
    size = sum(a.size * a.dtype.itemsize for a in operands) + sum(
        o.size * o.dtype.itemsize for o in outs
    )
    scratch_size = sum(math.prod(a.shape) * a.dtype.itemsize for a in scratch)
    if late:
        scratch = [*scratch, pltpu.SemaphoreType.DMA((len(late),))]
    limit = min(56 * MIB, 2 * (size + scratch_size) + 8 * MIB)
    whole = pl.BlockSpec(memory_space=pltpu.VMEM)
    specs = [whole] * len(operands)
    if indexed:
        specs[0] = pl.BlockSpec(memory_space=pltpu.SMEM)
    for operand in late:
        specs[operand] = pl.BlockSpec(memory_space=pltpu.HBM)
    return pl.pallas_call(
        kernel,
        out_shape=outs,
        in_specs=specs,
        out_specs=[whole] * len(outs),
        scratch_shapes=scratch,
        compiler_params=pltpu.CompilerParams(vmem_limit_bytes=limit),
        cost_estimate=pl.CostEstimate(
            flops=flops, bytes_accessed=size, transcendentals=transcendentals
        ),
    )(*operands)


def ring_routes(ring):
    ahead = [(a, ring[(i + 1) % len(ring)]) for i, a in enumerate(ring)]
    return ahead, [(b, a) for a, b in ahead]


def local(features, qkv_weight, grad_out, residues, log_rates, skip_gain):
    n_seq = lax.axis_size("seq")
    n_ch = lax.axis_size("ch")
    seq_index = lax.axis_index("seq")
    ch_index = lax.axis_index("ch")
    rows, gates, width = qkv_weight.shape
    block_len = features.shape[0]
    tokens = n_seq * block_len
    order = residues.shape[1]
    part = round_up(-(-rows // n_ch), 8)
    cos_table, sin_table, twist = (jnp.asarray(a) for a in wave_tables(tokens))

    place = jnp.stack([seq_index, ch_index]).astype(jnp.int32)

    ring = list(range(0, n_seq, 2)) + list(range(n_seq - 1, 0, -2))
    ahead, behind = ring_routes(ring)

    def send_on(pair):
        return lax.ppermute(pair[0], "seq", ahead), lax.ppermute(pair[1], "seq", behind)

    square = part * tokens * tokens
    spectrum = jax.ShapeDtypeStruct((part, tokens), F32)
    weight = qkv_weight.transpose(1, 0, 2)

    def project(pieces):
        span = sum(piece.shape[0] for piece in pieces)
        sums = call(
            functools.partial(project_kernel, pieces=len(pieces)),
            [
                jax.ShapeDtypeStruct((gates, part, span), F32 if d == 0 else BF16)
                for d in range(n_ch)
            ],
            2 * gates * rows * width * span, 0, place, weight, *pieces,
            scratch=[pltpu.VMEM((span, width), BF16), pltpu.VMEM((gates, rows, span), F32)],
            indexed=True, late=range(2, 2 + len(pieces)),
        )
        return list(sums)

    def to_owners(sums):
        return [sums[0]] + [
            lax.ppermute(sums[d], "ch", [(h, h ^ d) for h in range(n_ch)])
            for d in range(1, n_ch)
        ]

    pair = send_on((features, features))

    spread = [((q % n_seq) * n_ch + q // n_seq, q) for q in range(n_seq * n_ch)]
    packed = jnp.concatenate([residues, log_rates, skip_gain[:, None]], 1)
    (poles,) = call(
        functools.partial(poles_kernel, rows=rows, n_ch=n_ch),
        (jax.ShapeDtypeStruct((part, packed.shape[1]), F32),), 0, 0, place, packed, indexed=True,
    )
    grad_out, poles = lax.optimization_barrier((grad_out, poles))
    poles = lax.ppermute(poles, ("seq", "ch"), spread)
    (upper,) = call(
        functools.partial(pieces_kernel, rows=rows),
        (jax.ShapeDtypeStruct((n_ch, n_seq // n_ch, part, block_len), BF16),), 0, 0, grad_out,
    )
    upper = lax.all_to_all(upper, "ch", split_axis=0, concat_axis=0, tiled=True)
    pair, upper, poles = lax.optimization_barrier((pair, upper, poles))
    upper = upper.reshape(n_seq, part, block_len)
    upper = lax.all_to_all(upper, "seq", split_axis=0, concat_axis=0, tiled=True)

    pieces, group_slots, partials = [features, *pair], [], []
    waiting = list(pieces)
    next_pair = send_on(pair)
    for step in range(2, n_seq // 2):
        pair = next_pair
        if step == 2:
            pair, upper = lax.optimization_barrier((pair, upper))
        else:
            pair, near = lax.optimization_barrier((pair, partials[1 - n_ch]))
            partials[1 - n_ch] = near
        pieces += pair
        waiting += pair
        if step < n_seq // 2 - 1:
            next_pair = send_on(pair)
        else:
            half = block_len // 2
            halves, waiting = lax.optimization_barrier(((pair[0][:half], pair[1][half:]), waiting))
            next_pair = send_on(halves)
        sums = project(waiting)
        partials += to_owners(sums)
        group_slots.append(len(waiting))
        waiting = []
    pair = next_pair
    pieces += pair
    partials += to_owners(project(list(pair)))
    group_slots.append(1)
    hc, hs = call(
        functools.partial(taps_kernel, order=order), (spectrum, spectrum),
        8 * square, part * tokens * order, poles, cos_table, sin_table, twist,
    )

    grads, tgc, tgs, skip_sum = call(
        functools.partial(conv_kernel, order=order, group_slots=group_slots, shares=n_ch),
        (
            jax.ShapeDtypeStruct((gates, part, tokens), BF16),
            spectrum,
            spectrum,
            jax.ShapeDtypeStruct((part, 1), F32),
        ),
        32 * square, 0, place, *partials, upper, poles, hc, hs, cos_table, sin_table, twist,
        scratch=[pltpu.VMEM((n_seq, gates, part, block_len), F32)]
        + [pltpu.VMEM(a.shape, a.dtype) for a in partials],
        indexed=True, late=range(1, 1 + len(partials)),
    )

    swap = [(h, h ^ 1) for h in range(n_ch)]

    def chips(array):
        return [
            lax.ppermute(array, "ch", [(h, h ^ d) for h in range(n_ch)])
            for d in range(2, n_ch, 2)
        ]

    across = chips(grads)
    swapped = lax.ppermute(grads, "ch", swap)
    lanes = round_up(2 * order + 1, 128)
    (pole_sums,) = call(
        functools.partial(pole_kernel, order=order),
        (jax.ShapeDtypeStruct((part, lanes), F32),),
        8 * square, part * tokens * order, poles, tgc, tgs, cos_table, sin_table, skip_sum,
    )

    every = jnp.broadcast_to(pole_sums[None], (n_seq,) + pole_sums.shape)
    every = lax.all_to_all(every, "seq", split_axis=0, concat_axis=0, tiled=True)
    every = every.reshape(n_ch, n_seq // n_ch, part, pole_sums.shape[1])
    sums = call(
        split_kernel, [jax.ShapeDtypeStruct(every.shape[1:], F32)] * n_ch, 0, 0, place, every,
        indexed=True,
    )
    across, sums = lax.optimization_barrier((across, list(sums)))
    held = [grads] + across + [swapped] + [lax.ppermute(a, "ch", swap) for a in across]
    blocks = [sums[0]] + [
        lax.ppermute(sums[d], "ch", [(h, h ^ d) for h in range(n_ch)]) for d in range(1, n_ch)
    ]

    tile = min(512, width)
    weight_grad = pl.pallas_call(
        functools.partial(weight_kernel, shares=n_ch),
        out_shape=jax.ShapeDtypeStruct((gates, rows, width), F32),
        grid=(width // tile,),
        in_specs=[pl.BlockSpec(memory_space=pltpu.SMEM)]
        + [pl.BlockSpec((gates, part, tokens), lambda i: (0, 0, 0))] * n_ch
        + [pl.BlockSpec((piece.shape[0], tile), lambda i: (0, i)) for piece in pieces],
        out_specs=pl.BlockSpec((gates, rows, tile), lambda i: (0, 0, i)),
        scratch_shapes=[
            pltpu.VMEM((gates, rows, tokens), F32),
            pltpu.VMEM((gates, rows, tokens), BF16),
            pltpu.VMEM((tokens, tile), BF16),
        ],
        compiler_params=pltpu.CompilerParams(
            vmem_limit_bytes=min(56 * MIB, 16 * MIB + 12 * gates * rows * tokens + 4 * tokens * tile)
        ),
        cost_estimate=pl.CostEstimate(
            flops=2 * gates * rows * width * tokens,
            bytes_accessed=4 * gates * rows * width + 2 * tokens * (width + gates * rows),
            transcendentals=0,
        ),
    )(place, *held, *pieces)
    weight_grad, blocks = lax.optimization_barrier((weight_grad, blocks))
    weight_grad = weight_grad.transpose(1, 0, 2)

    channels = residues.shape[0]
    by_pole = jax.ShapeDtypeStruct((order, channels), F32)
    residue_grad, rate_grad, skip_grad = call(
        functools.partial(assemble_kernel, rows=rows, order=order),
        [by_pole, by_pole, jax.ShapeDtypeStruct((1, channels), F32)], 0, 0, place, *blocks,
        scratch=[pltpu.VMEM((round_up(channels, 128), lanes), F32)], indexed=True,
    )
    return (weight_grad, residue_grad.T, rate_grad.T, skip_grad.reshape(channels))


def solution(mesh):
    placed = (
        P("seq", "ch"),
        P("seq", None, "ch"),
        P("ch", "seq"),
        P("ch", None),
        P("ch", None),
        P("ch"),
    )
    return jax.shard_map(
        local,
        mesh=mesh,
        in_specs=placed,
        out_specs=(P("seq", None, "ch"), P("ch", None), P("ch", None), P("ch")),
        check_vma=False,
    )
```

```python
import functools
import math

import jax
import jax.numpy as jnp
import ml_dtypes
import numpy as np
from jax import lax
from jax.experimental import pallas as pl
from jax.experimental.pallas import tpu as pltpu
from jax.sharding import PartitionSpec as P

F32 = jnp.float32
BF16 = jnp.bfloat16
MIB = 1024 * 1024


def round_up(value, multiple):
    return -(-value // multiple) * multiple


def wave_tables(tokens):
    odd = 2 * np.arange(tokens, dtype=np.int64) + 1
    angles = (odd[:, None] * odd[None, :] % (8 * tokens)) * (math.pi / (4 * tokens))
    twist = odd * (math.pi / (4 * tokens))
    return (
        np.cos(angles).astype(ml_dtypes.bfloat16),
        np.sin(angles).astype(ml_dtypes.bfloat16),
        np.stack([np.cos(twist), np.sin(twist)]).astype(np.float32),
    )


def dot(left, right):
    return jnp.dot(left, right, preferred_element_type=F32)


def two_parts(value):
    high = value.astype(BF16)
    low = (value - high.astype(F32)).astype(BF16)
    return jnp.concatenate([high, low], 0)


def wide_dot(value, table):
    rows = value.shape[0]
    both = dot(two_parts(value), table)
    return both[:rows] + both[rows:]


def taps_kernel(poles_ref, cos_ref, sin_ref, twist_ref, hc_ref, hs_ref, *, order):
    rows, tokens = hc_ref.shape
    steps = lax.broadcasted_iota(jnp.int32, (rows, tokens), 1).astype(F32)
    taps = jnp.zeros((rows, tokens), F32)
    for pole in range(order):
        residue = poles_ref[:, pole : pole + 1]
        rate = jnp.exp(poles_ref[:, order + pole : order + pole + 1])
        taps = taps + residue * jnp.exp(-rate * steps)
    even = wide_dot(taps, cos_ref[...])
    uneven = wide_dot(taps, sin_ref[...])
    cos_half = twist_ref[0:1, :]
    sin_half = twist_ref[1:2, :]
    hc_ref[...] = cos_half * even + sin_half * uneven
    hs_ref[...] = cos_half * uneven - sin_half * even


def part_start(index, part, rows):
    return pl.multiple_of(jnp.minimum(index * part, rows - part), 8)


def pieces_kernel(grad_ref, pieces_ref, *, rows):
    n_ch, blocks, part, _ = pieces_ref.shape
    grad = grad_ref[...].astype(F32)
    for owner in range(n_ch):
        for block in range(blocks):
            start = block * rows + min(owner * part, rows - part)
            pieces_ref[owner, block] = grad[start : start + part].astype(BF16)


def turn_kernel(place_ref, held_ref, *out_refs):
    count = out_refs[0].shape[0]
    for half, out_ref in enumerate(out_refs):
        for slot in range(count):
            out_ref[slot] = held_ref[place_ref[0] ^ (half * count + slot)]


def poles_kernel(place_ref, packed_ref, poles_ref, *, rows, n_ch):
    part = poles_ref.shape[0]
    own = place_ref[0]
    start = own // n_ch * rows + part_start(own % n_ch, part, rows)
    poles_ref[...] = packed_ref[pl.ds(pl.multiple_of(start, 8), part), :]


def fetch(sources, targets, semaphores):
    copies = [
        pltpu.make_async_copy(source, target, semaphores.at[i])
        for i, (source, target) in enumerate(zip(sources, targets))
    ]
    for copy in copies:
        copy.start()
    return copies


def finish(copies):
    for copy in copies:
        copy.wait()


def project_kernel(place_ref, weight_ref, *refs, pieces):
    feature_refs = refs[:pieces]
    out_refs = refs[pieces:-3]
    features_ref, sums_ref, semaphores = refs[-3:]
    gates, _, _ = weight_ref.shape
    part = out_refs[0].shape[-2]
    targets, row = [], 0
    for feature_ref in feature_refs:
        targets.append(features_ref.at[pl.ds(row, feature_ref.shape[0]), :])
        row += feature_ref.shape[0]
    finish(fetch(feature_refs, targets, semaphores))
    for gate in range(gates):
        sums_ref[gate] = lax.dot_general(
            weight_ref[gate], features_ref[...], (((1,), (1,)), ((), ())),
            preferred_element_type=F32,
        )
    rows = weight_ref.shape[1]
    for step, out_ref in enumerate(out_refs):
        start = part_start(place_ref[1] ^ step, part, rows)
        out_ref[...] = sums_ref[:, pl.ds(start, part), :].astype(out_ref.dtype)


def ring_place(index, count):
    return jnp.where(index % 2 == 0, index // 2, count - (index + 1) // 2)


def ring_slot(index, place, count):
    ahead = (ring_place(index, count) - place + count) % count
    near = jnp.where(ahead * 2 < count, 2 * ahead, 2 * (count - ahead) - 1)
    return jnp.where(ahead * 2 == count, count - 1, near)


def conv_kernel(place_ref, *refs, order, group_slots, shares):
    count = len(group_slots) * shares
    partial_refs = refs[:count]
    (
        gout_ref, poles_ref, hc_ref, hs_ref, cos_ref, sin_ref, twist_ref, grad_ref,
        tgc_ref, tgs_ref, skip_ref, proj_ref, *scratch_refs,
    ) = refs[count:]
    *held_refs, semaphores = scratch_refs
    finish(fetch(partial_refs, held_refs, semaphores))
    rows, tokens = hc_ref.shape
    blocks, _, _, block_len = proj_ref.shape
    slot = 0
    for group, span in enumerate(group_slots):
        own_ref, *other_refs = held_refs[group * shares : (group + 1) * shares]
        total = own_ref[...]
        for other_ref in other_refs:
            total = total + other_ref[...].astype(F32)
        total = total.astype(BF16).astype(F32)
        for place in range(span):
            proj_ref[slot] = total[:, :, place * block_len : (place + 1) * block_len]
            slot += 1

    place = ring_place(place_ref[0], blocks)
    slots = [ring_slot(jnp.int32(b), place, blocks) for b in range(blocks)]

    def in_order(gate):
        return jnp.concatenate([proj_ref[slots[b], gate] for b in range(blocks)], 1)

    queries = in_order(0)
    keys = in_order(1)
    values = in_order(2)
    upper = jnp.concatenate([gout_ref[b ^ place_ref[0]].astype(F32) for b in range(blocks)], 1)
    product = keys * values
    middle = upper * queries
    signals = jnp.concatenate([product, middle], 0)
    parts = two_parts(signals)
    even = dot(parts, cos_ref[...])
    uneven = dot(parts, sin_ref[...])
    even = even[: 2 * rows] + even[2 * rows :]
    uneven = uneven[: 2 * rows] + uneven[2 * rows :]
    ac, mc = even[:rows], even[rows:]
    as_, ms = uneven[:rows], uneven[rows:]
    hc = hc_ref[...]
    hs = hs_ref[...]
    scale = 1.0 / tokens
    cos_sums = jnp.concatenate([hc * ac - hs * as_, hc * mc + hs * ms], 0) * scale
    sin_sums = jnp.concatenate([hc * as_ + hs * ac, hc * ms - hs * mc], 0) * scale
    tc = (ac * mc + as_ * ms) * scale
    ts = (ac * ms - as_ * mc) * scale
    cos_half = twist_ref[0:1, :]
    sin_half = twist_ref[1:2, :]
    tgc_ref[...] = tc * cos_half - ts * sin_half
    tgs_ref[...] = ts * cos_half + tc * sin_half
    restored = wide_dot(cos_sums, cos_ref[...]) + wide_dot(sin_sums, sin_ref[...])
    skip = poles_ref[:, 2 * order : 2 * order + 1]
    mix = restored[rows:] + skip * middle
    grads = (upper * (restored[:rows] + skip * product), mix * values, mix * keys)
    for gate, grad in enumerate(grads):
        for b in range(blocks):
            column = pl.multiple_of(slots[b] * block_len, block_len)
            grad_ref[gate, :, pl.ds(column, block_len)] = grad[
                :, b * block_len : (b + 1) * block_len
            ].astype(BF16)
    skip_ref[...] = jnp.sum(product * middle, axis=1, keepdims=True)


def pole_kernel(poles_ref, tgc_ref, tgs_ref, cos_ref, sin_ref, skip_ref, out_ref, *, order):
    rows, tokens = tgc_ref.shape
    taps_grad = wide_dot(tgc_ref[...], cos_ref[...]) + wide_dot(tgs_ref[...], sin_ref[...])
    out_ref[...] = jnp.zeros_like(out_ref)
    steps = lax.broadcasted_iota(jnp.int32, (rows, tokens), 1).astype(F32)
    for pole in range(order):
        residue = poles_ref[:, pole : pole + 1]
        rate = jnp.exp(poles_ref[:, order + pole : order + pole + 1])
        decayed = taps_grad * jnp.exp(-rate * steps)
        out_ref[:, pole : pole + 1] = jnp.sum(decayed, axis=1, keepdims=True)
        moment = jnp.sum(decayed * steps, axis=1, keepdims=True)
        out_ref[:, order + pole : order + pole + 1] = -residue * rate * moment
    out_ref[:, 2 * order : 2 * order + 1] = skip_ref[...]


def share_start(own, share, shares, part, rows):
    core, step = share // (shares // 2), 2 * (share % (shares // 2))
    return part_start(own ^ core ^ step, part, rows)


def weight_kernel(place_ref, *refs, shares):
    grad_refs = refs[:shares]
    *feature_refs, out_ref, wide_ref, rows_ref, features_ref, semaphores = refs[shares:]
    gates = out_ref.shape[0]
    part = grad_refs[0].shape[1]
    tiles, _, width = features_ref.shape

    def copy(tile, piece):
        row = sum(feature_ref.shape[0] for feature_ref in feature_refs[:piece])
        feature_ref = feature_refs[piece]
        return pltpu.make_async_copy(
            feature_ref.at[:, pl.ds(pl.multiple_of(tile * width, width), width)],
            features_ref.at[tile, pl.ds(row, feature_ref.shape[0]), :],
            semaphores.at[tile, piece],
        )

    @pl.when(pl.program_id(0) == 0)
    def _():
        for tile in range(tiles):
            for piece in range(len(feature_refs)):
                copy(tile, piece).start()
        for share, grad_ref in enumerate(grad_refs):
            start = share_start(place_ref[1], share, shares, part, out_ref.shape[1])
            wide_ref[:, pl.ds(start, part), :] = grad_ref[...].astype(F32)
        rows_ref[...] = wide_ref[...].astype(BF16)

    tile = pl.program_id(0)
    for piece in range(len(feature_refs)):
        copy(tile, piece).wait()
    rows = out_ref.shape[1]
    if rows % 16 == 0:
        every = dot(rows_ref[...].reshape(gates * rows, -1), features_ref[tile])
        out_ref[...] = every.reshape(out_ref.shape)
    else:
        for gate in range(gates):
            out_ref[gate] = dot(rows_ref[gate], features_ref[tile])


def split_kernel(place_ref, held_ref, *out_refs):
    for step, out_ref in enumerate(out_refs):
        out_ref[...] = held_ref[place_ref[1] ^ step]


def assemble_kernel(place_ref, *refs, rows, order):
    *piece_refs, residue_ref, rate_ref, skip_ref, sums_ref = refs
    blocks, part, _ = piece_refs[0].shape
    sums_ref[...] = jnp.zeros_like(sums_ref)
    for step, piece_ref in enumerate(piece_refs):
        start = part_start(place_ref[1] ^ step, part, rows)
        for block in range(blocks):
            row = pl.multiple_of(block * rows + start, 8)
            sums_ref[pl.ds(row, part), :] = piece_ref[block]
    turned = sums_ref[...].T
    channels = residue_ref.shape[1]
    residue_ref[...] = turned[:order, :channels]
    rate_ref[...] = turned[order : 2 * order, :channels]
    skip_ref[...] = turned[2 * order : 2 * order + 1, :channels]


def call(kernel, outs, flops, transcendentals, *operands, scratch=(), indexed=False, late=()):
    size = sum(a.size * a.dtype.itemsize for a in operands) + sum(
        o.size * o.dtype.itemsize for o in outs
    )
    scratch_size = sum(math.prod(a.shape) * a.dtype.itemsize for a in scratch)
    if late:
        scratch = [*scratch, pltpu.SemaphoreType.DMA((len(late),))]
    limit = min(56 * MIB, 2 * (size + scratch_size) + 8 * MIB)
    whole = pl.BlockSpec(memory_space=pltpu.VMEM)
    specs = [whole] * len(operands)
    if indexed:
        specs[0] = pl.BlockSpec(memory_space=pltpu.SMEM)
    for operand in late:
        specs[operand] = pl.BlockSpec(memory_space=pltpu.HBM)
    return pl.pallas_call(
        kernel,
        out_shape=outs,
        in_specs=specs,
        out_specs=[whole] * len(outs),
        scratch_shapes=scratch,
        compiler_params=pltpu.CompilerParams(vmem_limit_bytes=limit),
        cost_estimate=pl.CostEstimate(
            flops=flops, bytes_accessed=size, transcendentals=transcendentals
        ),
    )(*operands)


def ring_routes(ring):
    ahead = [(a, ring[(i + 1) % len(ring)]) for i, a in enumerate(ring)]
    return ahead, [(b, a) for a, b in ahead]


def local(features, qkv_weight, grad_out, residues, log_rates, skip_gain):
    n_seq = lax.axis_size("seq")
    n_ch = lax.axis_size("ch")
    seq_index = lax.axis_index("seq")
    ch_index = lax.axis_index("ch")
    rows, gates, width = qkv_weight.shape
    block_len = features.shape[0]
    tokens = n_seq * block_len
    order = residues.shape[1]
    part = round_up(-(-rows // n_ch), 8)
    cos_table, sin_table, twist = (jnp.asarray(a) for a in wave_tables(tokens))

    place = jnp.stack([seq_index, ch_index]).astype(jnp.int32)

    ring = list(range(0, n_seq, 2)) + list(range(n_seq - 1, 0, -2))
    ahead, behind = ring_routes(ring)

    def send_on(pair):
        return lax.ppermute(pair[0], "seq", ahead), lax.ppermute(pair[1], "seq", behind)

    square = part * tokens * tokens
    spectrum = jax.ShapeDtypeStruct((part, tokens), F32)
    weight = qkv_weight.transpose(1, 0, 2)

    def project(pieces):
        span = sum(piece.shape[0] for piece in pieces)
        sums = call(
            functools.partial(project_kernel, pieces=len(pieces)),
            [
                jax.ShapeDtypeStruct((gates, part, span), F32 if d == 0 else BF16)
                for d in range(n_ch)
            ],
            2 * gates * rows * width * span, 0, place, weight, *pieces,
            scratch=[pltpu.VMEM((span, width), BF16), pltpu.VMEM((gates, rows, span), F32)],
            indexed=True, late=range(2, 2 + len(pieces)),
        )
        return list(sums)

    def to_owners(sums):
        return [sums[0]] + [
            lax.ppermute(sums[d], "ch", [(h, h ^ d) for h in range(n_ch)])
            for d in range(1, n_ch)
        ]

    pair = send_on((features, features))

    spread = [((q % n_seq) * n_ch + q // n_seq, q) for q in range(n_seq * n_ch)]
    packed = jnp.concatenate([residues, log_rates, skip_gain[:, None]], 1)
    (poles,) = call(
        functools.partial(poles_kernel, rows=rows, n_ch=n_ch),
        (jax.ShapeDtypeStruct((part, packed.shape[1]), F32),), 0, 0, place, packed, indexed=True,
    )
    grad_out, poles = lax.optimization_barrier((grad_out, poles))
    poles = lax.ppermute(poles, ("seq", "ch"), spread)
    (upper,) = call(
        functools.partial(pieces_kernel, rows=rows),
        (jax.ShapeDtypeStruct((n_ch, n_seq // n_ch, part, block_len), BF16),), 0, 0, grad_out,
    )
    upper = lax.all_to_all(upper, "ch", split_axis=0, concat_axis=0, tiled=True)
    pair, upper, poles = lax.optimization_barrier((pair, upper, poles))
    low, high = call(
        turn_kernel, [jax.ShapeDtypeStruct((n_seq // 2, part, block_len), BF16)] * 2, 0, 0,
        place, upper.reshape(n_seq, part, block_len), indexed=True,
    )

    def trade(array, reach):
        return lax.ppermute(array, "seq", [(d, d ^ reach) for d in range(n_seq)])

    def merge(kept, moved):
        return jnp.stack([kept, moved], 1).reshape(n_seq, part, block_len)

    def cut(array, reach):
        array = array.reshape(-1, 2, reach, part, block_len)
        return array[:, 0], array[:, 1]

    reach = n_seq // 2
    kept, moved = low[None], trade(high, reach)[None]

    pieces, group_slots, partials = [features, *pair], [], []
    waiting = list(pieces)
    next_pair = send_on(pair)
    for step in range(2, n_seq // 2):
        pair = next_pair
        if step == 2:
            pair, moved = lax.optimization_barrier((pair, moved))
        else:
            pair, near, moved = lax.optimization_barrier((pair, partials[1 - n_ch], moved))
            partials[1 - n_ch] = near
        pieces += pair
        waiting += pair
        if step < n_seq // 2 - 1:
            next_pair = send_on(pair)
        else:
            half = block_len // 2
            halves, waiting = lax.optimization_barrier(((pair[0][:half], pair[1][half:]), waiting))
            next_pair = send_on(halves)
        sums = project(waiting)
        partials += to_owners(sums)
        group_slots.append(len(waiting))
        waiting = []
        if reach > 1:
            reach //= 2
            kept, moved = cut(merge(kept, moved), reach)
            moved = trade(moved, reach)
    while reach > 1:
        reach //= 2
        kept, moved = cut(merge(kept, moved), reach)
        moved = trade(moved, reach)
    upper = merge(kept, moved)
    pair = next_pair
    pieces += pair
    partials += to_owners(project(list(pair)))
    group_slots.append(1)
    hc, hs = call(
        functools.partial(taps_kernel, order=order), (spectrum, spectrum),
        8 * square, part * tokens * order, poles, cos_table, sin_table, twist,
    )

    grads, tgc, tgs, skip_sum = call(
        functools.partial(conv_kernel, order=order, group_slots=group_slots, shares=n_ch),
        (
            jax.ShapeDtypeStruct((gates, part, tokens), BF16),
            spectrum,
            spectrum,
            jax.ShapeDtypeStruct((part, 1), F32),
        ),
        32 * square, 0, place, *partials, upper, poles, hc, hs, cos_table, sin_table, twist,
        scratch=[pltpu.VMEM((n_seq, gates, part, block_len), F32)]
        + [pltpu.VMEM(a.shape, a.dtype) for a in partials],
        indexed=True, late=range(1, 1 + len(partials)),
    )

    swap = [(h, h ^ 1) for h in range(n_ch)]

    def chips(array):
        return [
            lax.ppermute(array, "ch", [(h, h ^ d) for h in range(n_ch)])
            for d in range(2, n_ch, 2)
        ]

    across = chips(grads)
    swapped = lax.ppermute(grads, "ch", swap)
    tgc, swapped = lax.optimization_barrier((tgc, swapped))
    lanes = round_up(2 * order + 1, 128)
    (pole_sums,) = call(
        functools.partial(pole_kernel, order=order),
        (jax.ShapeDtypeStruct((part, lanes), F32),),
        8 * square, part * tokens * order, poles, tgc, tgs, cos_table, sin_table, skip_sum,
    )

    every = jnp.broadcast_to(pole_sums[None], (n_seq,) + pole_sums.shape)
    every = lax.all_to_all(every, "seq", split_axis=0, concat_axis=0, tiled=True)
    every = every.reshape(n_ch, n_seq // n_ch, part, pole_sums.shape[1])
    sums = call(
        split_kernel, [jax.ShapeDtypeStruct(every.shape[1:], F32)] * n_ch, 0, 0, place, every,
        indexed=True,
    )
    across, sums = lax.optimization_barrier((across, list(sums)))
    held = [grads] + across + [swapped] + [lax.ppermute(a, "ch", swap) for a in across]
    blocks = [sums[0]] + [
        lax.ppermute(sums[d], "ch", [(h, h ^ d) for h in range(n_ch)]) for d in range(1, n_ch)
    ]

    tile = min(512, width)
    weight_grad = pl.pallas_call(
        functools.partial(weight_kernel, shares=n_ch),
        out_shape=jax.ShapeDtypeStruct((gates, rows, width), F32),
        grid=(width // tile,),
        in_specs=[pl.BlockSpec(memory_space=pltpu.SMEM)]
        + [pl.BlockSpec((gates, part, tokens), lambda i: (0, 0, 0))] * n_ch
        + [pl.BlockSpec(memory_space=pltpu.HBM)] * len(pieces),
        out_specs=pl.BlockSpec((gates, rows, tile), lambda i: (0, 0, i)),
        scratch_shapes=[
            pltpu.VMEM((gates, rows, tokens), F32),
            pltpu.VMEM((gates, rows, tokens), BF16),
            pltpu.VMEM((width // tile, tokens, tile), BF16),
            pltpu.SemaphoreType.DMA((width // tile, len(pieces))),
        ],
        compiler_params=pltpu.CompilerParams(
            vmem_limit_bytes=min(56 * MIB, 16 * MIB + 12 * gates * rows * tokens + 2 * tokens * width)
        ),
        cost_estimate=pl.CostEstimate(
            flops=2 * gates * rows * width * tokens,
            bytes_accessed=4 * gates * rows * width + 2 * tokens * (width + gates * rows),
            transcendentals=0,
        ),
    )(place, *held, *pieces)
    weight_grad, blocks = lax.optimization_barrier((weight_grad, blocks))
    weight_grad = weight_grad.transpose(1, 0, 2)

    channels = residues.shape[0]
    by_pole = jax.ShapeDtypeStruct((order, channels), F32)
    residue_grad, rate_grad, skip_grad = call(
        functools.partial(assemble_kernel, rows=rows, order=order),
        [by_pole, by_pole, jax.ShapeDtypeStruct((1, channels), F32)], 0, 0, place, *blocks,
        scratch=[pltpu.VMEM((round_up(channels, 128), lanes), F32)], indexed=True,
    )
    return (weight_grad, residue_grad.T, rate_grad.T, skip_grad.reshape(channels))


def solution(mesh):
    placed = (
        P("seq", "ch"),
        P("seq", None, "ch"),
        P("ch", "seq"),
        P("ch", None),
        P("ch", None),
        P("ch"),
    )
    return jax.shard_map(
        local,
        mesh=mesh,
        in_specs=placed,
        out_specs=(P("seq", None, "ch"), P("ch", None), P("ch", None), P("ch")),
        check_vma=False,
    )
```

```python
import functools
import math

import jax
import jax.numpy as jnp
import ml_dtypes
import numpy as np
from jax import lax
from jax.experimental import pallas as pl
from jax.experimental.pallas import tpu as pltpu
from jax.sharding import PartitionSpec as P

F32 = jnp.float32
BF16 = jnp.bfloat16
MIB = 1024 * 1024


def round_up(value, multiple):
    return -(-value // multiple) * multiple


def wave_tables(tokens):
    odd = 2 * np.arange(tokens, dtype=np.int64) + 1
    angles = (odd[:, None] * odd[None, :] % (8 * tokens)) * (math.pi / (4 * tokens))
    twist = odd * (math.pi / (4 * tokens))
    return (
        np.cos(angles).astype(ml_dtypes.bfloat16),
        np.sin(angles).astype(ml_dtypes.bfloat16),
        np.stack([np.cos(twist), np.sin(twist)]).astype(np.float32),
    )


def dot(left, right):
    return jnp.dot(left, right, preferred_element_type=F32)


def two_parts(value):
    high = value.astype(BF16)
    low = (value - high.astype(F32)).astype(BF16)
    return jnp.concatenate([high, low], 0)


def wide_dot(value, table):
    rows = value.shape[0]
    both = dot(two_parts(value), table)
    return both[:rows] + both[rows:]


def taps_kernel(poles_ref, cos_ref, sin_ref, twist_ref, hc_ref, hs_ref, *, order):
    rows, tokens = hc_ref.shape
    steps = lax.broadcasted_iota(jnp.int32, (rows, tokens), 1).astype(F32)
    taps = jnp.zeros((rows, tokens), F32)
    for pole in range(order):
        residue = poles_ref[:, pole : pole + 1]
        rate = jnp.exp(poles_ref[:, order + pole : order + pole + 1])
        taps = taps + residue * jnp.exp(-rate * steps)
    even = wide_dot(taps, cos_ref[...])
    uneven = wide_dot(taps, sin_ref[...])
    cos_half = twist_ref[0:1, :]
    sin_half = twist_ref[1:2, :]
    hc_ref[...] = cos_half * even + sin_half * uneven
    hs_ref[...] = cos_half * uneven - sin_half * even


def part_start(index, part, rows):
    return pl.multiple_of(jnp.minimum(index * part, rows - part), 8)


def pieces_kernel(grad_ref, pieces_ref, *, rows):
    n_ch, blocks, part, _ = pieces_ref.shape
    grad = grad_ref[...].astype(F32)
    for owner in range(n_ch):
        for block in range(blocks):
            start = block * rows + min(owner * part, rows - part)
            pieces_ref[owner, block] = grad[start : start + part].astype(BF16)


def poles_kernel(place_ref, packed_ref, poles_ref, *, rows, n_ch):
    part = poles_ref.shape[0]
    own = place_ref[0]
    start = own // n_ch * rows + part_start(own % n_ch, part, rows)
    poles_ref[...] = packed_ref[pl.ds(pl.multiple_of(start, 8), part), :]


def fetch(sources, targets, semaphores):
    copies = [
        pltpu.make_async_copy(source, target, semaphores.at[i])
        for i, (source, target) in enumerate(zip(sources, targets))
    ]
    for copy in copies:
        copy.start()
    return copies


def finish(copies):
    for copy in copies:
        copy.wait()


def project_kernel(place_ref, weight_ref, *refs, pieces):
    feature_refs = refs[:pieces]
    out_refs = refs[pieces:-3]
    features_ref, sums_ref, semaphores = refs[-3:]
    gates, _, _ = weight_ref.shape
    part = out_refs[0].shape[-2]
    targets, row = [], 0
    for feature_ref in feature_refs:
        targets.append(features_ref.at[pl.ds(row, feature_ref.shape[0]), :])
        row += feature_ref.shape[0]
    finish(fetch(feature_refs, targets, semaphores))
    for gate in range(gates):
        sums_ref[gate] = lax.dot_general(
            weight_ref[gate], features_ref[...], (((1,), (1,)), ((), ())),
            preferred_element_type=F32,
        )
    rows = weight_ref.shape[1]
    for step, out_ref in enumerate(out_refs):
        start = part_start(place_ref[1] ^ step, part, rows)
        out_ref[...] = sums_ref[:, pl.ds(start, part), :].astype(out_ref.dtype)


def ring_place(index, count):
    return jnp.where(index % 2 == 0, index // 2, count - (index + 1) // 2)


def ring_slot(index, place, count):
    ahead = (ring_place(index, count) - place + count) % count
    near = jnp.where(ahead * 2 < count, 2 * ahead, 2 * (count - ahead) - 1)
    return jnp.where(ahead * 2 == count, count - 1, near)


def conv_kernel(place_ref, *refs, order, group_slots, shares):
    count = len(group_slots) * shares
    partial_refs = refs[:count]
    (
        gout_ref, poles_ref, hc_ref, hs_ref, cos_ref, sin_ref, twist_ref, grad_ref,
        tgc_ref, tgs_ref, skip_ref, proj_ref, *scratch_refs,
    ) = refs[count:]
    *held_refs, semaphores = scratch_refs
    finish(fetch(partial_refs, held_refs, semaphores))
    rows, tokens = hc_ref.shape
    blocks, _, _, block_len = proj_ref.shape
    slot = 0
    for group, span in enumerate(group_slots):
        own_ref, *other_refs = held_refs[group * shares : (group + 1) * shares]
        total = own_ref[...]
        for other_ref in other_refs:
            total = total + other_ref[...].astype(F32)
        total = total.astype(BF16).astype(F32)
        for place in range(span):
            proj_ref[slot] = total[:, :, place * block_len : (place + 1) * block_len]
            slot += 1

    place = ring_place(place_ref[0], blocks)
    slots = [ring_slot(jnp.int32(b), place, blocks) for b in range(blocks)]

    def in_order(gate):
        return jnp.concatenate([proj_ref[slots[b], gate] for b in range(blocks)], 1)

    queries = in_order(0)
    keys = in_order(1)
    values = in_order(2)
    upper = jnp.concatenate([gout_ref[b].astype(F32) for b in range(blocks)], 1)
    product = keys * values
    middle = upper * queries
    signals = jnp.concatenate([product, middle], 0)
    parts = two_parts(signals)
    even = dot(parts, cos_ref[...])
    uneven = dot(parts, sin_ref[...])
    even = even[: 2 * rows] + even[2 * rows :]
    uneven = uneven[: 2 * rows] + uneven[2 * rows :]
    ac, mc = even[:rows], even[rows:]
    as_, ms = uneven[:rows], uneven[rows:]
    hc = hc_ref[...]
    hs = hs_ref[...]
    scale = 1.0 / tokens
    cos_sums = jnp.concatenate([hc * ac - hs * as_, hc * mc + hs * ms], 0) * scale
    sin_sums = jnp.concatenate([hc * as_ + hs * ac, hc * ms - hs * mc], 0) * scale
    tc = (ac * mc + as_ * ms) * scale
    ts = (ac * ms - as_ * mc) * scale
    cos_half = twist_ref[0:1, :]
    sin_half = twist_ref[1:2, :]
    tgc_ref[...] = tc * cos_half - ts * sin_half
    tgs_ref[...] = ts * cos_half + tc * sin_half
    restored = wide_dot(cos_sums, cos_ref[...]) + wide_dot(sin_sums, sin_ref[...])
    skip = poles_ref[:, 2 * order : 2 * order + 1]
    mix = restored[rows:] + skip * middle
    grads = (upper * (restored[:rows] + skip * product), mix * values, mix * keys)
    for gate, grad in enumerate(grads):
        for b in range(blocks):
            column = pl.multiple_of(slots[b] * block_len, block_len)
            grad_ref[gate, :, pl.ds(column, block_len)] = grad[
                :, b * block_len : (b + 1) * block_len
            ].astype(BF16)
    skip_ref[...] = jnp.sum(product * middle, axis=1, keepdims=True)


def pole_kernel(poles_ref, tgc_ref, tgs_ref, cos_ref, sin_ref, skip_ref, out_ref, *, order):
    rows, tokens = tgc_ref.shape
    taps_grad = wide_dot(tgc_ref[...], cos_ref[...]) + wide_dot(tgs_ref[...], sin_ref[...])
    steps = lax.broadcasted_iota(jnp.int32, (rows, tokens), 1).astype(F32)
    for pole in range(order):
        residue = poles_ref[:, pole : pole + 1]
        rate = jnp.exp(poles_ref[:, order + pole : order + pole + 1])
        decayed = taps_grad * jnp.exp(-rate * steps)
        out_ref[:, pole : pole + 1] = jnp.sum(decayed, axis=1, keepdims=True)
        moment = jnp.sum(decayed * steps, axis=1, keepdims=True)
        out_ref[:, order + pole : order + pole + 1] = -residue * rate * moment
    out_ref[:, 2 * order : 2 * order + 1] = skip_ref[...]


def share_start(own, share, shares, part, rows):
    core, step = share // (shares // 2), 2 * (share % (shares // 2))
    return part_start(own ^ core ^ step, part, rows)


def weight_kernel(place_ref, *refs, shares):
    grad_refs = refs[:shares]
    *feature_refs, out_ref, wide_ref, rows_ref, features_ref = refs[shares:]
    gates = out_ref.shape[0]
    part = grad_refs[0].shape[1]

    @pl.when(pl.program_id(0) == 0)
    def _():
        for share, grad_ref in enumerate(grad_refs):
            start = share_start(place_ref[1], share, shares, part, out_ref.shape[1])
            wide_ref[:, pl.ds(start, part), :] = grad_ref[...].astype(F32)
        rows_ref[...] = wide_ref[...].astype(BF16)

    row = 0
    for feature_ref in feature_refs:
        features_ref[row : row + feature_ref.shape[0], :] = feature_ref[...]
        row += feature_ref.shape[0]
    rows = out_ref.shape[1]
    if rows % 16 == 0:
        every = dot(rows_ref[...].reshape(gates * rows, -1), features_ref[...])
        out_ref[...] = every.reshape(out_ref.shape)
    else:
        for gate in range(gates):
            out_ref[gate] = dot(rows_ref[gate], features_ref[...])


def assemble_kernel(place_ref, *refs, rows, order):
    *block_refs, residue_ref, rate_ref, skip_ref, sums_ref = refs
    count = len(block_refs)
    sums_ref[...] = jnp.zeros_like(sums_ref)
    width = block_refs[0].shape[1]
    for turn, block_ref in enumerate(block_refs):
        block = (place_ref[0] + turn) % count
        sums_ref[pl.ds(pl.multiple_of(block * rows, 8), rows), :width] = block_ref[...]
    turned = sums_ref[...].T
    channels = residue_ref.shape[1]
    residue_ref[...] = turned[:order, :channels]
    rate_ref[...] = turned[order : 2 * order, :channels]
    skip_ref[...] = turned[2 * order : 2 * order + 1, :channels]


def gather_kernel(place_ref, *refs):
    *held_refs, out_ref = refs
    for share, held_ref in enumerate(held_refs):
        start = share_start(place_ref[1], share, len(held_refs), held_ref.shape[0], out_ref.shape[0])
        out_ref[pl.ds(start, held_ref.shape[0]), :] = held_ref[...]


def call(kernel, outs, flops, transcendentals, *operands, scratch=(), indexed=False, late=()):
    size = sum(a.size * a.dtype.itemsize for a in operands) + sum(
        o.size * o.dtype.itemsize for o in outs
    )
    scratch_size = sum(math.prod(a.shape) * a.dtype.itemsize for a in scratch)
    if late:
        scratch = [*scratch, pltpu.SemaphoreType.DMA((len(late),))]
    limit = min(56 * MIB, 2 * (size + scratch_size) + 8 * MIB)
    whole = pl.BlockSpec(memory_space=pltpu.VMEM)
    specs = [whole] * len(operands)
    if indexed:
        specs[0] = pl.BlockSpec(memory_space=pltpu.SMEM)
    for operand in late:
        specs[operand] = pl.BlockSpec(memory_space=pltpu.HBM)
    return pl.pallas_call(
        kernel,
        out_shape=outs,
        in_specs=specs,
        out_specs=[whole] * len(outs),
        scratch_shapes=scratch,
        compiler_params=pltpu.CompilerParams(vmem_limit_bytes=limit),
        cost_estimate=pl.CostEstimate(
            flops=flops, bytes_accessed=size, transcendentals=transcendentals
        ),
    )(*operands)


def ring_routes(ring):
    ahead = [(a, ring[(i + 1) % len(ring)]) for i, a in enumerate(ring)]
    return ahead, [(b, a) for a, b in ahead]


def local(features, qkv_weight, grad_out, residues, log_rates, skip_gain):
    n_seq = lax.axis_size("seq")
    n_ch = lax.axis_size("ch")
    seq_index = lax.axis_index("seq")
    ch_index = lax.axis_index("ch")
    rows, gates, width = qkv_weight.shape
    block_len = features.shape[0]
    tokens = n_seq * block_len
    order = residues.shape[1]
    part = round_up(-(-rows // n_ch), 8)
    cos_table, sin_table, twist = (jnp.asarray(a) for a in wave_tables(tokens))

    place = jnp.stack([seq_index, ch_index]).astype(jnp.int32)

    ring = list(range(0, n_seq, 2)) + list(range(n_seq - 1, 0, -2))
    ahead, behind = ring_routes(ring)

    def send_on(pair):
        return lax.ppermute(pair[0], "seq", ahead), lax.ppermute(pair[1], "seq", behind)

    square = part * tokens * tokens
    spectrum = jax.ShapeDtypeStruct((part, tokens), F32)
    weight = qkv_weight.transpose(1, 0, 2)

    def project(pieces):
        span = sum(piece.shape[0] for piece in pieces)
        sums = call(
            functools.partial(project_kernel, pieces=len(pieces)),
            [
                jax.ShapeDtypeStruct((gates, part, span), F32 if d == 0 else BF16)
                for d in range(n_ch)
            ],
            2 * gates * rows * width * span, 0, place, weight, *pieces,
            scratch=[pltpu.VMEM((span, width), BF16), pltpu.VMEM((gates, rows, span), F32)],
            indexed=True, late=range(2, 2 + len(pieces)),
        )
        return list(sums)

    def to_owners(sums):
        return [sums[0]] + [
            lax.ppermute(sums[d], "ch", [(h, h ^ d) for h in range(n_ch)])
            for d in range(1, n_ch)
        ]

    pair = send_on((features, features))

    spread = [((q % n_seq) * n_ch + q // n_seq, q) for q in range(n_seq * n_ch)]
    packed = jnp.concatenate([residues, log_rates, skip_gain[:, None]], 1)
    (poles,) = call(
        functools.partial(poles_kernel, rows=rows, n_ch=n_ch),
        (jax.ShapeDtypeStruct((part, packed.shape[1]), F32),), 0, 0, place, packed, indexed=True,
    )
    grad_out, poles = lax.optimization_barrier((grad_out, poles))
    poles = lax.ppermute(poles, ("seq", "ch"), spread)
    (upper,) = call(
        functools.partial(pieces_kernel, rows=rows),
        (jax.ShapeDtypeStruct((n_ch, n_seq // n_ch, part, block_len), BF16),), 0, 0, grad_out,
    )
    upper = lax.all_to_all(upper, "ch", split_axis=0, concat_axis=0, tiled=True)
    pair, upper, poles = lax.optimization_barrier((pair, upper, poles))
    upper = upper.reshape(n_seq, part, block_len)
    upper = lax.all_to_all(upper, "seq", split_axis=0, concat_axis=0, tiled=True)

    pieces, group_slots, partials = [features, *pair], [], []
    waiting = list(pieces)
    next_pair = send_on(pair)
    for step in range(2, n_seq // 2):
        pair = next_pair
        if step == 2:
            pair, upper = lax.optimization_barrier((pair, upper))
        else:
            pair, near = lax.optimization_barrier((pair, partials[1 - n_ch]))
            partials[1 - n_ch] = near
        pieces += pair
        waiting += pair
        if step < n_seq // 2 - 1:
            next_pair = send_on(pair)
        else:
            half = block_len // 2
            halves, waiting = lax.optimization_barrier(((pair[0][:half], pair[1][half:]), waiting))
            next_pair = send_on(halves)
        sums = project(waiting)
        partials += to_owners(sums)
        group_slots.append(len(waiting))
        waiting = []
    pair = next_pair
    pieces += pair
    partials += to_owners(project(list(pair)))
    group_slots.append(1)
    hc, hs = call(
        functools.partial(taps_kernel, order=order), (spectrum, spectrum),
        8 * square, part * tokens * order, poles, cos_table, sin_table, twist,
    )

    grads, tgc, tgs, skip_sum = call(
        functools.partial(conv_kernel, order=order, group_slots=group_slots, shares=n_ch),
        (
            jax.ShapeDtypeStruct((gates, part, tokens), BF16),
            spectrum,
            spectrum,
            jax.ShapeDtypeStruct((part, 1), F32),
        ),
        32 * square, 0, place, *partials, upper, poles, hc, hs, cos_table, sin_table, twist,
        scratch=[pltpu.VMEM((n_seq, gates, part, block_len), F32)]
        + [pltpu.VMEM(a.shape, a.dtype) for a in partials],
        indexed=True, late=range(1, 1 + len(partials)),
    )

    swap = [(h, h ^ 1) for h in range(n_ch)]

    def chips(array):
        return [
            lax.ppermute(array, "ch", [(h, h ^ d) for h in range(n_ch)])
            for d in range(2, n_ch, 2)
        ]

    across = chips(grads)
    swapped = lax.ppermute(grads, "ch", swap)
    (pole_sums,) = call(
        functools.partial(pole_kernel, order=order),
        (jax.ShapeDtypeStruct((part, 2 * order + 1), F32),),
        8 * square, part * tokens * order, poles, tgc, tgs, cos_table, sin_table, skip_sum,
    )

    sums = [pole_sums] + chips(pole_sums)
    across, sums = lax.optimization_barrier((across, sums))
    held = [grads] + across + [swapped] + [lax.ppermute(a, "ch", swap) for a in across]
    sums += [lax.ppermute(a, "ch", swap) for a in sums]
    (block_sums,) = call(
        gather_kernel, [jax.ShapeDtypeStruct((rows, 2 * order + 1), F32)], 0, 0, place, *sums,
        indexed=True,
    )
    turns = n_seq // n_ch
    blocks = []
    for turn in range(turns):
        route = [
            ((h * turns + (s + turn) % turns) * n_ch + s // turns, s * n_ch + h)
            for s in range(n_seq)
            for h in range(n_ch)
        ]
        blocks.append(lax.ppermute(block_sums, ("seq", "ch"), route))

    tile = min(512, width)
    weight_grad = pl.pallas_call(
        functools.partial(weight_kernel, shares=n_ch),
        out_shape=jax.ShapeDtypeStruct((gates, rows, width), F32),
        grid=(width // tile,),
        in_specs=[pl.BlockSpec(memory_space=pltpu.SMEM)]
        + [pl.BlockSpec((gates, part, tokens), lambda i: (0, 0, 0))] * n_ch
        + [pl.BlockSpec((piece.shape[0], tile), lambda i: (0, i)) for piece in pieces],
        out_specs=pl.BlockSpec((gates, rows, tile), lambda i: (0, 0, i)),
        scratch_shapes=[
            pltpu.VMEM((gates, rows, tokens), F32),
            pltpu.VMEM((gates, rows, tokens), BF16),
            pltpu.VMEM((tokens, tile), BF16),
        ],
        compiler_params=pltpu.CompilerParams(
            vmem_limit_bytes=min(56 * MIB, 16 * MIB + 12 * gates * rows * tokens + 4 * tokens * tile)
        ),
        cost_estimate=pl.CostEstimate(
            flops=2 * gates * rows * width * tokens,
            bytes_accessed=4 * gates * rows * width + 2 * tokens * (width + gates * rows),
            transcendentals=0,
        ),
    )(place, *held, *pieces)
    weight_grad, blocks = lax.optimization_barrier((weight_grad, blocks))
    weight_grad = weight_grad.transpose(1, 0, 2)

    channels = residues.shape[0]
    by_pole = jax.ShapeDtypeStruct((order, channels), F32)
    residue_grad, rate_grad, skip_grad = call(
        functools.partial(assemble_kernel, rows=rows, order=order),
        [by_pole, by_pole, jax.ShapeDtypeStruct((1, channels), F32)], 0, 0, place, *blocks,
        scratch=[pltpu.VMEM((round_up(channels, 128), 128), F32)], indexed=True,
    )
    return (weight_grad, residue_grad.T, rate_grad.T, skip_grad.reshape(channels))


def solution(mesh):
    placed = (
        P("seq", "ch"),
        P("seq", None, "ch"),
        P("ch", "seq"),
        P("ch", None),
        P("ch", None),
        P("ch"),
    )
    return jax.shard_map(
        local,
        mesh=mesh,
        in_specs=placed,
        out_specs=(P("seq", None, "ch"), P("ch", None), P("ch", None), P("ch")),
        check_vma=False,
    )
```

```python
import functools
import math

import jax
import jax.numpy as jnp
import ml_dtypes
import numpy as np
from jax import lax
from jax.experimental import pallas as pl
from jax.experimental.pallas import tpu as pltpu
from jax.sharding import PartitionSpec as P

F32 = jnp.float32
BF16 = jnp.bfloat16
MIB = 1024 * 1024


def round_up(value, multiple):
    return -(-value // multiple) * multiple


def wave_tables(tokens):
    odd = 2 * np.arange(tokens, dtype=np.int64) + 1
    angles = (odd[:, None] * odd[None, :] % (8 * tokens)) * (math.pi / (4 * tokens))
    twist = odd * (math.pi / (4 * tokens))
    return (
        np.cos(angles).astype(ml_dtypes.bfloat16),
        np.sin(angles).astype(ml_dtypes.bfloat16),
        np.stack([np.cos(twist), np.sin(twist)]).astype(np.float32),
    )


def dot(left, right):
    return jnp.dot(left, right, preferred_element_type=F32)


def two_parts(value):
    high = value.astype(BF16)
    low = (value - high.astype(F32)).astype(BF16)
    return jnp.concatenate([high, low], 0)


def wide_dot(value, table):
    rows = value.shape[0]
    both = dot(two_parts(value), table)
    return both[:rows] + both[rows:]


def taps_kernel(poles_ref, cos_ref, sin_ref, twist_ref, hc_ref, hs_ref, *, order):
    rows, tokens = hc_ref.shape
    steps = lax.broadcasted_iota(jnp.int32, (rows, tokens), 1).astype(F32)
    taps = jnp.zeros((rows, tokens), F32)
    for pole in range(order):
        residue = poles_ref[:, pole : pole + 1]
        rate = jnp.exp(poles_ref[:, order + pole : order + pole + 1])
        taps = taps + residue * jnp.exp(-rate * steps)
    even = wide_dot(taps, cos_ref[...])
    uneven = wide_dot(taps, sin_ref[...])
    cos_half = twist_ref[0:1, :]
    sin_half = twist_ref[1:2, :]
    hc_ref[...] = cos_half * even + sin_half * uneven
    hs_ref[...] = cos_half * uneven - sin_half * even


def part_start(index, part, rows):
    return pl.multiple_of(jnp.minimum(index * part, rows - part), 8)


def pieces_kernel(grad_ref, pieces_ref, *, rows):
    n_ch, blocks, part, _ = pieces_ref.shape
    grad = grad_ref[...].astype(F32)
    for owner in range(n_ch):
        for block in range(blocks):
            start = block * rows + min(owner * part, rows - part)
            pieces_ref[owner, block] = grad[start : start + part].astype(BF16)


def poles_kernel(place_ref, packed_ref, poles_ref, *, rows, n_ch):
    part = poles_ref.shape[0]
    own = place_ref[0]
    start = own // n_ch * rows + part_start(own % n_ch, part, rows)
    poles_ref[...] = packed_ref[pl.ds(pl.multiple_of(start, 8), part), :]


def fetch(sources, targets, semaphores):
    copies = [
        pltpu.make_async_copy(source, target, semaphores.at[i])
        for i, (source, target) in enumerate(zip(sources, targets))
    ]
    for copy in copies:
        copy.start()
    return copies


def finish(copies):
    for copy in copies:
        copy.wait()


def project_kernel(place_ref, weight_ref, *refs, pieces):
    feature_refs = refs[:pieces]
    out_refs = refs[pieces:-3]
    features_ref, sums_ref, semaphores = refs[-3:]
    gates, _, _ = weight_ref.shape
    part = out_refs[0].shape[-2]
    targets, row = [], 0
    for feature_ref in feature_refs:
        targets.append(features_ref.at[pl.ds(row, feature_ref.shape[0]), :])
        row += feature_ref.shape[0]
    finish(fetch(feature_refs, targets, semaphores))
    for gate in range(gates):
        sums_ref[gate] = lax.dot_general(
            weight_ref[gate], features_ref[...], (((1,), (1,)), ((), ())),
            preferred_element_type=F32,
        )
    rows = weight_ref.shape[1]
    for step, out_ref in enumerate(out_refs):
        start = part_start(place_ref[1] ^ step, part, rows)
        out_ref[...] = sums_ref[:, pl.ds(start, part), :].astype(out_ref.dtype)


def ring_place(index, count):
    return jnp.where(index % 2 == 0, index // 2, count - (index + 1) // 2)


def ring_slot(index, place, count):
    ahead = (ring_place(index, count) - place + count) % count
    near = jnp.where(ahead * 2 < count, 2 * ahead, 2 * (count - ahead) - 1)
    return jnp.where(ahead * 2 == count, count - 1, near)


def conv_kernel(place_ref, *refs, order, group_slots, shares):
    count = len(group_slots) * shares
    partial_refs = refs[:count]
    (
        gout_ref, poles_ref, hc_ref, hs_ref, cos_ref, sin_ref, twist_ref, grad_ref,
        tgc_ref, tgs_ref, skip_ref, proj_ref, *scratch_refs,
    ) = refs[count:]
    *held_refs, semaphores = scratch_refs
    finish(fetch(partial_refs, held_refs, semaphores))
    rows, tokens = hc_ref.shape
    blocks, _, _, block_len = proj_ref.shape
    slot = 0
    for group, span in enumerate(group_slots):
        own_ref, *other_refs = held_refs[group * shares : (group + 1) * shares]
        total = own_ref[...]
        for other_ref in other_refs:
            total = total + other_ref[...].astype(F32)
        total = total.astype(BF16).astype(F32)
        for place in range(span):
            proj_ref[slot] = total[:, :, place * block_len : (place + 1) * block_len]
            slot += 1

    place = ring_place(place_ref[0], blocks)
    slots = [ring_slot(jnp.int32(b), place, blocks) for b in range(blocks)]

    def in_order(gate):
        return jnp.concatenate([proj_ref[slots[b], gate] for b in range(blocks)], 1)

    queries = in_order(0)
    keys = in_order(1)
    values = in_order(2)
    upper = jnp.concatenate([gout_ref[b].astype(F32) for b in range(blocks)], 1)
    product = keys * values
    middle = upper * queries
    signals = jnp.concatenate([product, middle], 0)
    parts = two_parts(signals)
    even = dot(parts, cos_ref[...])
    uneven = dot(parts, sin_ref[...])
    even = even[: 2 * rows] + even[2 * rows :]
    uneven = uneven[: 2 * rows] + uneven[2 * rows :]
    ac, mc = even[:rows], even[rows:]
    as_, ms = uneven[:rows], uneven[rows:]
    hc = hc_ref[...]
    hs = hs_ref[...]
    scale = 1.0 / tokens
    cos_sums = jnp.concatenate([hc * ac - hs * as_, hc * mc + hs * ms], 0) * scale
    sin_sums = jnp.concatenate([hc * as_ + hs * ac, hc * ms - hs * mc], 0) * scale
    tc = (ac * mc + as_ * ms) * scale
    ts = (ac * ms - as_ * mc) * scale
    cos_half = twist_ref[0:1, :]
    sin_half = twist_ref[1:2, :]
    tgc_ref[...] = tc * cos_half - ts * sin_half
    tgs_ref[...] = ts * cos_half + tc * sin_half
    restored = wide_dot(cos_sums, cos_ref[...]) + wide_dot(sin_sums, sin_ref[...])
    skip = poles_ref[:, 2 * order : 2 * order + 1]
    mix = restored[rows:] + skip * middle
    grads = (upper * (restored[:rows] + skip * product), mix * values, mix * keys)
    for gate, grad in enumerate(grads):
        for b in range(blocks):
            column = pl.multiple_of(slots[b] * block_len, block_len)
            grad_ref[gate, :, pl.ds(column, block_len)] = grad[
                :, b * block_len : (b + 1) * block_len
            ].astype(BF16)
    skip_ref[...] = jnp.sum(product * middle, axis=1, keepdims=True)


def pole_kernel(poles_ref, tgc_ref, tgs_ref, cos_ref, sin_ref, skip_ref, out_ref, *, order):
    rows, tokens = tgc_ref.shape
    taps_grad = wide_dot(tgc_ref[...], cos_ref[...]) + wide_dot(tgs_ref[...], sin_ref[...])
    steps = lax.broadcasted_iota(jnp.int32, (rows, tokens), 1).astype(F32)
    for pole in range(order):
        residue = poles_ref[:, pole : pole + 1]
        rate = jnp.exp(poles_ref[:, order + pole : order + pole + 1])
        decayed = taps_grad * jnp.exp(-rate * steps)
        out_ref[:, pole : pole + 1] = jnp.sum(decayed, axis=1, keepdims=True)
        moment = jnp.sum(decayed * steps, axis=1, keepdims=True)
        out_ref[:, order + pole : order + pole + 1] = -residue * rate * moment
    out_ref[:, 2 * order : 2 * order + 1] = skip_ref[...]


def share_start(own, share, shares, part, rows):
    core, step = share // (shares // 2), 2 * (share % (shares // 2))
    return part_start(own ^ core ^ step, part, rows)


def weight_kernel(place_ref, *refs, shares):
    grad_refs = refs[:shares]
    *feature_refs, out_ref, wide_ref, rows_ref, features_ref = refs[shares:]
    gates = out_ref.shape[0]
    part = grad_refs[0].shape[1]

    @pl.when(pl.program_id(0) == 0)
    def _():
        for share, grad_ref in enumerate(grad_refs):
            start = share_start(place_ref[1], share, shares, part, out_ref.shape[1])
            wide_ref[:, pl.ds(start, part), :] = grad_ref[...].astype(F32)
        rows_ref[...] = wide_ref[...].astype(BF16)

    row = 0
    for feature_ref in feature_refs:
        features_ref[row : row + feature_ref.shape[0], :] = feature_ref[...]
        row += feature_ref.shape[0]
    rows = out_ref.shape[1]
    if rows % 16 == 0:
        every = dot(rows_ref[...].reshape(gates * rows, -1), features_ref[...])
        out_ref[...] = every.reshape(out_ref.shape)
    else:
        for gate in range(gates):
            out_ref[gate] = dot(rows_ref[gate], features_ref[...])


def assemble_kernel(place_ref, *refs, rows, order):
    *block_refs, residue_ref, rate_ref, skip_ref, sums_ref = refs
    count = len(block_refs)
    sums_ref[...] = jnp.zeros_like(sums_ref)
    width = block_refs[0].shape[1]
    for turn, block_ref in enumerate(block_refs):
        block = (place_ref[0] + turn) % count
        sums_ref[pl.ds(pl.multiple_of(block * rows, 8), rows), :width] = block_ref[...]
    turned = sums_ref[...].T
    channels = residue_ref.shape[1]
    residue_ref[...] = turned[:order, :channels]
    rate_ref[...] = turned[order : 2 * order, :channels]
    skip_ref[...] = turned[2 * order : 2 * order + 1, :channels]


def gather_kernel(place_ref, *refs):
    *held_refs, out_ref = refs
    for share, held_ref in enumerate(held_refs):
        start = share_start(place_ref[1], share, len(held_refs), held_ref.shape[0], out_ref.shape[0])
        out_ref[pl.ds(start, held_ref.shape[0]), :] = held_ref[...]


def call(kernel, outs, flops, transcendentals, *operands, scratch=(), indexed=False, late=()):
    size = sum(a.size * a.dtype.itemsize for a in operands) + sum(
        o.size * o.dtype.itemsize for o in outs
    )
    scratch_size = sum(math.prod(a.shape) * a.dtype.itemsize for a in scratch)
    if late:
        scratch = [*scratch, pltpu.SemaphoreType.DMA((len(late),))]
    limit = min(56 * MIB, 2 * (size + scratch_size) + 8 * MIB)
    whole = pl.BlockSpec(memory_space=pltpu.VMEM)
    specs = [whole] * len(operands)
    if indexed:
        specs[0] = pl.BlockSpec(memory_space=pltpu.SMEM)
    for operand in late:
        specs[operand] = pl.BlockSpec(memory_space=pltpu.HBM)
    return pl.pallas_call(
        kernel,
        out_shape=outs,
        in_specs=specs,
        out_specs=[whole] * len(outs),
        scratch_shapes=scratch,
        compiler_params=pltpu.CompilerParams(vmem_limit_bytes=limit),
        cost_estimate=pl.CostEstimate(
            flops=flops, bytes_accessed=size, transcendentals=transcendentals
        ),
    )(*operands)


def ring_routes(ring):
    ahead = [(a, ring[(i + 1) % len(ring)]) for i, a in enumerate(ring)]
    return ahead, [(b, a) for a, b in ahead]


def local(features, qkv_weight, grad_out, residues, log_rates, skip_gain):
    n_seq = lax.axis_size("seq")
    n_ch = lax.axis_size("ch")
    seq_index = lax.axis_index("seq")
    ch_index = lax.axis_index("ch")
    rows, gates, width = qkv_weight.shape
    block_len = features.shape[0]
    tokens = n_seq * block_len
    order = residues.shape[1]
    part = round_up(-(-rows // n_ch), 8)
    cos_table, sin_table, twist = (jnp.asarray(a) for a in wave_tables(tokens))

    place = jnp.stack([seq_index, ch_index]).astype(jnp.int32)

    ring = list(range(0, n_seq, 2)) + list(range(n_seq - 1, 0, -2))
    ahead, behind = ring_routes(ring)

    def send_on(pair):
        return lax.ppermute(pair[0], "seq", ahead), lax.ppermute(pair[1], "seq", behind)

    square = part * tokens * tokens
    spectrum = jax.ShapeDtypeStruct((part, tokens), F32)
    weight = qkv_weight.transpose(1, 0, 2)

    def project(pieces):
        span = sum(piece.shape[0] for piece in pieces)
        sums = call(
            functools.partial(project_kernel, pieces=len(pieces)),
            [
                jax.ShapeDtypeStruct((gates, part, span), F32 if d == 0 else BF16)
                for d in range(n_ch)
            ],
            2 * gates * rows * width * span, 0, place, weight, *pieces,
            scratch=[pltpu.VMEM((span, width), BF16), pltpu.VMEM((gates, rows, span), F32)],
            indexed=True, late=range(2, 2 + len(pieces)),
        )
        return list(sums)

    def to_owners(sums):
        return [sums[0]] + [
            lax.ppermute(sums[d], "ch", [(h, h ^ d) for h in range(n_ch)])
            for d in range(1, n_ch)
        ]

    pair = send_on((features, features))

    spread = [((q % n_seq) * n_ch + q // n_seq, q) for q in range(n_seq * n_ch)]
    packed = jnp.concatenate([residues, log_rates, skip_gain[:, None]], 1)
    (poles,) = call(
        functools.partial(poles_kernel, rows=rows, n_ch=n_ch),
        (jax.ShapeDtypeStruct((part, packed.shape[1]), F32),), 0, 0, place, packed, indexed=True,
    )
    grad_out, poles = lax.optimization_barrier((grad_out, poles))
    poles = lax.ppermute(poles, ("seq", "ch"), spread)
    (upper,) = call(
        functools.partial(pieces_kernel, rows=rows),
        (jax.ShapeDtypeStruct((n_ch, n_seq // n_ch, part, block_len), BF16),), 0, 0, grad_out,
    )
    upper = lax.all_to_all(upper, "ch", split_axis=0, concat_axis=0, tiled=True)
    pair, upper, poles = lax.optimization_barrier((pair, upper, poles))
    upper = upper.reshape(n_seq, part, block_len)
    upper = lax.all_to_all(upper, "seq", split_axis=0, concat_axis=0, tiled=True)

    pieces, group_slots, partials = [features, *pair], [], []
    waiting = list(pieces)
    next_pair = send_on(pair)
    for step in range(2, n_seq // 2):
        pair = next_pair
        if step == 2:
            pair, upper = lax.optimization_barrier((pair, upper))
        else:
            pair, near = lax.optimization_barrier((pair, partials[1 - n_ch]))
            partials[1 - n_ch] = near
        pieces += pair
        waiting += pair
        if step < n_seq // 2 - 1:
            next_pair = send_on(pair)
        else:
            half = block_len // 2
            halves, waiting = lax.optimization_barrier(((pair[0][:half], pair[1][half:]), waiting))
            next_pair = send_on(halves)
        sums = project(waiting)
        partials += to_owners(sums)
        group_slots.append(len(waiting))
        waiting = []
    pair = next_pair
    pieces += pair
    partials += to_owners(project(list(pair)))
    group_slots.append(1)
    hc, hs = call(
        functools.partial(taps_kernel, order=order), (spectrum, spectrum),
        8 * square, part * tokens * order, poles, cos_table, sin_table, twist,
    )

    grads, tgc, tgs, skip_sum = call(
        functools.partial(conv_kernel, order=order, group_slots=group_slots, shares=n_ch),
        (
            jax.ShapeDtypeStruct((gates, part, tokens), BF16),
            spectrum,
            spectrum,
            jax.ShapeDtypeStruct((part, 1), F32),
        ),
        32 * square, 0, place, *partials, upper, poles, hc, hs, cos_table, sin_table, twist,
        scratch=[pltpu.VMEM((n_seq, gates, part, block_len), F32)]
        + [pltpu.VMEM(a.shape, a.dtype) for a in partials],
        indexed=True, late=range(1, 1 + len(partials)),
    )

    swap = [(h, h ^ 1) for h in range(n_ch)]

    def chips(array):
        return [
            lax.ppermute(array, "ch", [(h, h ^ d) for h in range(n_ch)])
            for d in range(2, n_ch, 2)
        ]

    across = chips(grads)
    swapped = lax.ppermute(grads, "ch", swap)
    (pole_sums,) = call(
        functools.partial(pole_kernel, order=order),
        (jax.ShapeDtypeStruct((part, 2 * order + 1), F32),),
        8 * square, part * tokens * order, poles, tgc, tgs, cos_table, sin_table, skip_sum,
    )

    sums = [pole_sums] + chips(pole_sums)
    across, sums = lax.optimization_barrier((across, sums))
    held = [grads] + across + [swapped] + [lax.ppermute(a, "ch", swap) for a in across]
    sums += [lax.ppermute(a, "ch", swap) for a in sums]
    (block_sums,) = call(
        gather_kernel, [jax.ShapeDtypeStruct((rows, 2 * order + 1), F32)], 0, 0, place, *sums,
        indexed=True,
    )
    tile = min(512, width)
    weight_grad = pl.pallas_call(
        functools.partial(weight_kernel, shares=n_ch),
        out_shape=jax.ShapeDtypeStruct((gates, rows, width), F32),
        grid=(width // tile,),
        in_specs=[pl.BlockSpec(memory_space=pltpu.SMEM)]
        + [pl.BlockSpec((gates, part, tokens), lambda i: (0, 0, 0))] * n_ch
        + [pl.BlockSpec((piece.shape[0], tile), lambda i: (0, i)) for piece in pieces],
        out_specs=pl.BlockSpec((gates, rows, tile), lambda i: (0, 0, i)),
        scratch_shapes=[
            pltpu.VMEM((gates, rows, tokens), F32),
            pltpu.VMEM((gates, rows, tokens), BF16),
            pltpu.VMEM((tokens, tile), BF16),
        ],
        compiler_params=pltpu.CompilerParams(
            vmem_limit_bytes=min(56 * MIB, 16 * MIB + 12 * gates * rows * tokens + 4 * tokens * tile)
        ),
        cost_estimate=pl.CostEstimate(
            flops=2 * gates * rows * width * tokens,
            bytes_accessed=4 * gates * rows * width + 2 * tokens * (width + gates * rows),
            transcendentals=0,
        ),
    )(place, *held, *pieces)
    weight_grad, block_sums = lax.optimization_barrier((weight_grad, block_sums))
    turns = n_seq // n_ch
    blocks = []
    for turn in range(turns):
        route = [
            ((h * turns + (s + turn) % turns) * n_ch + s // turns, s * n_ch + h)
            for s in range(n_seq)
            for h in range(n_ch)
        ]
        blocks.append(lax.ppermute(block_sums, ("seq", "ch"), route))
    weight_grad = weight_grad.transpose(1, 0, 2)

    channels = residues.shape[0]
    by_pole = jax.ShapeDtypeStruct((order, channels), F32)
    residue_grad, rate_grad, skip_grad = call(
        functools.partial(assemble_kernel, rows=rows, order=order),
        [by_pole, by_pole, jax.ShapeDtypeStruct((1, channels), F32)], 0, 0, place, *blocks,
        scratch=[pltpu.VMEM((round_up(channels, 128), 128), F32)], indexed=True,
    )
    return (weight_grad, residue_grad.T, rate_grad.T, skip_grad.reshape(channels))


def solution(mesh):
    placed = (
        P("seq", "ch"),
        P("seq", None, "ch"),
        P("ch", "seq"),
        P("ch", None),
        P("ch", None),
        P("ch"),
    )
    return jax.shard_map(
        local,
        mesh=mesh,
        in_specs=placed,
        out_specs=(P("seq", None, "ch"), P("ch", None), P("ch", None), P("ch")),
        check_vma=False,
    )
```

```python
import functools
import math

import jax
import jax.numpy as jnp
import ml_dtypes
import numpy as np
from jax import lax
from jax.experimental import pallas as pl
from jax.experimental.pallas import tpu as pltpu
from jax.sharding import PartitionSpec as P

F32 = jnp.float32
BF16 = jnp.bfloat16
MIB = 1024 * 1024


def round_up(value, multiple):
    return -(-value // multiple) * multiple


def wave_tables(tokens):
    odd = 2 * np.arange(tokens, dtype=np.int64) + 1
    angles = (odd[:, None] * odd[None, :] % (8 * tokens)) * (math.pi / (4 * tokens))
    twist = odd * (math.pi / (4 * tokens))
    return (
        np.cos(angles).astype(ml_dtypes.bfloat16),
        np.sin(angles).astype(ml_dtypes.bfloat16),
        np.stack([np.cos(twist), np.sin(twist)]).astype(np.float32),
    )


def dot(left, right):
    return jnp.dot(left, right, preferred_element_type=F32)


def two_parts(value):
    high = value.astype(BF16)
    low = (value - high.astype(F32)).astype(BF16)
    return jnp.concatenate([high, low], 0)


def wide_dot(value, table):
    rows = value.shape[0]
    both = dot(two_parts(value), table)
    return both[:rows] + both[rows:]


def taps_kernel(poles_ref, cos_ref, sin_ref, twist_ref, hc_ref, hs_ref, *, order):
    rows, tokens = hc_ref.shape
    steps = lax.broadcasted_iota(jnp.int32, (rows, tokens), 1).astype(F32)
    taps = jnp.zeros((rows, tokens), F32)
    for pole in range(order):
        residue = poles_ref[:, pole : pole + 1]
        rate = jnp.exp(poles_ref[:, order + pole : order + pole + 1])
        taps = taps + residue * jnp.exp(-rate * steps)
    even = wide_dot(taps, cos_ref[...])
    uneven = wide_dot(taps, sin_ref[...])
    cos_half = twist_ref[0:1, :]
    sin_half = twist_ref[1:2, :]
    hc_ref[...] = cos_half * even + sin_half * uneven
    hs_ref[...] = cos_half * uneven - sin_half * even


def part_start(index, part, rows):
    return pl.multiple_of(jnp.minimum(index * part, rows - part), 8)


def pieces_kernel(grad_ref, pieces_ref, *, rows):
    n_ch, blocks, part, _ = pieces_ref.shape
    grad = grad_ref[...].astype(F32)
    for owner in range(n_ch):
        for block in range(blocks):
            start = block * rows + min(owner * part, rows - part)
            pieces_ref[owner, block] = grad[start : start + part].astype(BF16)


def poles_kernel(place_ref, packed_ref, poles_ref, *, rows, n_ch):
    part = poles_ref.shape[0]
    own = place_ref[0]
    start = own // n_ch * rows + part_start(own % n_ch, part, rows)
    poles_ref[...] = packed_ref[pl.ds(pl.multiple_of(start, 8), part), :]


def fetch(sources, targets, semaphores):
    copies = [
        pltpu.make_async_copy(source, target, semaphores.at[i])
        for i, (source, target) in enumerate(zip(sources, targets))
    ]
    for copy in copies:
        copy.start()
    return copies


def finish(copies):
    for copy in copies:
        copy.wait()


def project_kernel(place_ref, weight_ref, *refs, pieces):
    feature_refs = refs[:pieces]
    out_refs = refs[pieces:-3]
    features_ref, sums_ref, semaphores = refs[-3:]
    gates, _, _ = weight_ref.shape
    part = out_refs[0].shape[-2]
    targets, row = [], 0
    for feature_ref in feature_refs:
        targets.append(features_ref.at[pl.ds(row, feature_ref.shape[0]), :])
        row += feature_ref.shape[0]
    finish(fetch(feature_refs, targets, semaphores))
    for gate in range(gates):
        sums_ref[gate] = lax.dot_general(
            weight_ref[gate], features_ref[...], (((1,), (1,)), ((), ())),
            preferred_element_type=F32,
        )
    rows = weight_ref.shape[1]
    for step, out_ref in enumerate(out_refs):
        start = part_start(place_ref[1] ^ step, part, rows)
        out_ref[...] = sums_ref[:, pl.ds(start, part), :].astype(out_ref.dtype)


def ring_place(index, count):
    return jnp.where(index % 2 == 0, index // 2, count - (index + 1) // 2)


def ring_slot(index, place, count):
    ahead = (ring_place(index, count) - place + count) % count
    near = jnp.where(ahead * 2 < count, 2 * ahead, 2 * (count - ahead) - 1)
    return jnp.where(ahead * 2 == count, count - 1, near)


def conv_kernel(place_ref, *refs, order, group_slots, shares):
    count = len(group_slots) * shares
    partial_refs = refs[:count]
    (
        gout_ref, poles_ref, hc_ref, hs_ref, cos_ref, sin_ref, twist_ref, grad_ref,
        tgc_ref, tgs_ref, skip_ref, proj_ref, *scratch_refs,
    ) = refs[count:]
    *held_refs, semaphores = scratch_refs
    finish(fetch(partial_refs, held_refs, semaphores))
    rows, tokens = hc_ref.shape
    blocks, _, _, block_len = proj_ref.shape
    slot = 0
    for group, span in enumerate(group_slots):
        own_ref, *other_refs = held_refs[group * shares : (group + 1) * shares]
        total = own_ref[...]
        for other_ref in other_refs:
            total = total + other_ref[...].astype(F32)
        total = total.astype(BF16).astype(F32)
        for place in range(span):
            proj_ref[slot] = total[:, :, place * block_len : (place + 1) * block_len]
            slot += 1

    place = ring_place(place_ref[0], blocks)
    slots = [ring_slot(jnp.int32(b), place, blocks) for b in range(blocks)]

    def in_order(gate):
        return jnp.concatenate([proj_ref[slots[b], gate] for b in range(blocks)], 1)

    queries = in_order(0)
    keys = in_order(1)
    values = in_order(2)
    upper = jnp.concatenate([gout_ref[b].astype(F32) for b in range(blocks)], 1)
    product = keys * values
    middle = upper * queries
    signals = jnp.concatenate([product, middle], 0)
    parts = two_parts(signals)
    even = dot(parts, cos_ref[...])
    uneven = dot(parts, sin_ref[...])
    even = even[: 2 * rows] + even[2 * rows :]
    uneven = uneven[: 2 * rows] + uneven[2 * rows :]
    ac, mc = even[:rows], even[rows:]
    as_, ms = uneven[:rows], uneven[rows:]
    hc = hc_ref[...]
    hs = hs_ref[...]
    scale = 1.0 / tokens
    cos_sums = jnp.concatenate([hc * ac - hs * as_, hc * mc + hs * ms], 0) * scale
    sin_sums = jnp.concatenate([hc * as_ + hs * ac, hc * ms - hs * mc], 0) * scale
    tc = (ac * mc + as_ * ms) * scale
    ts = (ac * ms - as_ * mc) * scale
    cos_half = twist_ref[0:1, :]
    sin_half = twist_ref[1:2, :]
    tgc_ref[...] = tc * cos_half - ts * sin_half
    tgs_ref[...] = ts * cos_half + tc * sin_half
    restored = wide_dot(cos_sums, cos_ref[...]) + wide_dot(sin_sums, sin_ref[...])
    skip = poles_ref[:, 2 * order : 2 * order + 1]
    mix = restored[rows:] + skip * middle
    grads = (upper * (restored[:rows] + skip * product), mix * values, mix * keys)
    for gate, grad in enumerate(grads):
        for b in range(blocks):
            column = pl.multiple_of(slots[b] * block_len, block_len)
            grad_ref[gate, :, pl.ds(column, block_len)] = grad[
                :, b * block_len : (b + 1) * block_len
            ].astype(BF16)
    skip_ref[...] = jnp.sum(product * middle, axis=1, keepdims=True)


def pole_kernel(poles_ref, tgc_ref, tgs_ref, cos_ref, sin_ref, skip_ref, out_ref, *, order):
    rows, tokens = tgc_ref.shape
    taps_grad = wide_dot(tgc_ref[...], cos_ref[...]) + wide_dot(tgs_ref[...], sin_ref[...])
    steps = lax.broadcasted_iota(jnp.int32, (rows, tokens), 1).astype(F32)
    for pole in range(order):
        residue = poles_ref[:, pole : pole + 1]
        rate = jnp.exp(poles_ref[:, order + pole : order + pole + 1])
        decayed = taps_grad * jnp.exp(-rate * steps)
        out_ref[:, pole : pole + 1] = jnp.sum(decayed, axis=1, keepdims=True)
        moment = jnp.sum(decayed * steps, axis=1, keepdims=True)
        out_ref[:, order + pole : order + pole + 1] = -residue * rate * moment
    out_ref[:, 2 * order : 2 * order + 1] = skip_ref[...]


def share_start(own, share, shares, part, rows):
    core, step = share // (shares // 2), 2 * (share % (shares // 2))
    return part_start(own ^ core ^ step, part, rows)


def weight_kernel(place_ref, *refs, shares):
    grad_refs = refs[:shares]
    *feature_refs, out_ref, wide_ref, rows_ref, features_ref = refs[shares:]
    gates = out_ref.shape[0]
    part = grad_refs[0].shape[1]

    @pl.when(pl.program_id(0) == 0)
    def _():
        for share, grad_ref in enumerate(grad_refs):
            start = share_start(place_ref[1], share, shares, part, out_ref.shape[1])
            wide_ref[:, pl.ds(start, part), :] = grad_ref[...].astype(F32)
        rows_ref[...] = wide_ref[...].astype(BF16)

    row = 0
    for feature_ref in feature_refs:
        features_ref[row : row + feature_ref.shape[0], :] = feature_ref[...]
        row += feature_ref.shape[0]
    rows = out_ref.shape[1]
    if rows % 16 == 0:
        every = dot(rows_ref[...].reshape(gates * rows, -1), features_ref[...])
        out_ref[...] = every.reshape(out_ref.shape)
    else:
        for gate in range(gates):
            out_ref[gate] = dot(rows_ref[gate], features_ref[...])


def assemble_kernel(place_ref, *refs, rows, order):
    *block_refs, residue_ref, rate_ref, skip_ref, sums_ref = refs
    count = len(block_refs)
    sums_ref[...] = jnp.zeros_like(sums_ref)
    width = block_refs[0].shape[1]
    for turn, block_ref in enumerate(block_refs):
        block = (place_ref[0] + turn) % count
        sums_ref[pl.ds(pl.multiple_of(block * rows, 8), rows), :width] = block_ref[...]
    turned = sums_ref[...].T
    channels = residue_ref.shape[1]
    residue_ref[...] = turned[:order, :channels]
    rate_ref[...] = turned[order : 2 * order, :channels]
    skip_ref[...] = turned[2 * order : 2 * order + 1, :channels]


def gather_kernel(place_ref, *refs):
    *held_refs, out_ref = refs
    for share, held_ref in enumerate(held_refs):
        start = share_start(place_ref[1], share, len(held_refs), held_ref.shape[0], out_ref.shape[0])
        out_ref[pl.ds(start, held_ref.shape[0]), :] = held_ref[...]


def call(kernel, outs, flops, transcendentals, *operands, scratch=(), indexed=False, late=()):
    size = sum(a.size * a.dtype.itemsize for a in operands) + sum(
        o.size * o.dtype.itemsize for o in outs
    )
    scratch_size = sum(math.prod(a.shape) * a.dtype.itemsize for a in scratch)
    if late:
        scratch = [*scratch, pltpu.SemaphoreType.DMA((len(late),))]
    limit = min(56 * MIB, 2 * (size + scratch_size) + 8 * MIB)
    whole = pl.BlockSpec(memory_space=pltpu.VMEM)
    specs = [whole] * len(operands)
    if indexed:
        specs[0] = pl.BlockSpec(memory_space=pltpu.SMEM)
    for operand in late:
        specs[operand] = pl.BlockSpec(memory_space=pltpu.HBM)
    return pl.pallas_call(
        kernel,
        out_shape=outs,
        in_specs=specs,
        out_specs=[whole] * len(outs),
        scratch_shapes=scratch,
        compiler_params=pltpu.CompilerParams(vmem_limit_bytes=limit),
        cost_estimate=pl.CostEstimate(
            flops=flops, bytes_accessed=size, transcendentals=transcendentals
        ),
    )(*operands)


def ring_routes(ring):
    ahead = [(a, ring[(i + 1) % len(ring)]) for i, a in enumerate(ring)]
    return ahead, [(b, a) for a, b in ahead]


def local(features, qkv_weight, grad_out, residues, log_rates, skip_gain):
    n_seq = lax.axis_size("seq")
    n_ch = lax.axis_size("ch")
    seq_index = lax.axis_index("seq")
    ch_index = lax.axis_index("ch")
    rows, gates, width = qkv_weight.shape
    block_len = features.shape[0]
    tokens = n_seq * block_len
    order = residues.shape[1]
    part = round_up(-(-rows // n_ch), 8)
    cos_table, sin_table, twist = (jnp.asarray(a) for a in wave_tables(tokens))

    place = jnp.stack([seq_index, ch_index]).astype(jnp.int32)

    ring = list(range(0, n_seq, 2)) + list(range(n_seq - 1, 0, -2))
    ahead, behind = ring_routes(ring)

    def send_on(pair):
        return lax.ppermute(pair[0], "seq", ahead), lax.ppermute(pair[1], "seq", behind)

    square = part * tokens * tokens
    spectrum = jax.ShapeDtypeStruct((part, tokens), F32)
    weight = qkv_weight.transpose(1, 0, 2)

    def project(pieces):
        span = sum(piece.shape[0] for piece in pieces)
        sums = call(
            functools.partial(project_kernel, pieces=len(pieces)),
            [
                jax.ShapeDtypeStruct((gates, part, span), F32 if d == 0 else BF16)
                for d in range(n_ch)
            ],
            2 * gates * rows * width * span, 0, place, weight, *pieces,
            scratch=[pltpu.VMEM((span, width), BF16), pltpu.VMEM((gates, rows, span), F32)],
            indexed=True, late=range(2, 2 + len(pieces)),
        )
        return list(sums)

    def to_owners(sums):
        return [sums[0]] + [
            lax.ppermute(sums[d], "ch", [(h, h ^ d) for h in range(n_ch)])
            for d in range(1, n_ch)
        ]

    pair = send_on((features, features))

    spread = [((q % n_seq) * n_ch + q // n_seq, q) for q in range(n_seq * n_ch)]
    packed = jnp.concatenate([residues, log_rates, skip_gain[:, None]], 1)
    (poles,) = call(
        functools.partial(poles_kernel, rows=rows, n_ch=n_ch),
        (jax.ShapeDtypeStruct((part, packed.shape[1]), F32),), 0, 0, place, packed, indexed=True,
    )
    grad_out, poles = lax.optimization_barrier((grad_out, poles))
    poles = lax.ppermute(poles, ("seq", "ch"), spread)
    (upper,) = call(
        functools.partial(pieces_kernel, rows=rows),
        (jax.ShapeDtypeStruct((n_ch, n_seq // n_ch, part, block_len), BF16),), 0, 0, grad_out,
    )
    upper = lax.all_to_all(upper, "ch", split_axis=0, concat_axis=0, tiled=True)
    pair, poles = lax.optimization_barrier((pair, poles))
    upper = upper.reshape(n_seq, part, block_len)
    upper = lax.all_to_all(upper, "seq", split_axis=0, concat_axis=0, tiled=True)

    pieces, group_slots, partials = [features, *pair], [], []
    waiting = list(pieces)
    next_pair = send_on(pair)
    for step in range(2, n_seq // 2):
        pair = next_pair
        if step == 2:
            pair, upper = lax.optimization_barrier((pair, upper))
        else:
            pair, near = lax.optimization_barrier((pair, partials[1 - n_ch]))
            partials[1 - n_ch] = near
        pieces += pair
        waiting += pair
        if step < n_seq // 2 - 1:
            next_pair = send_on(pair)
        else:
            half = block_len // 2
            halves, waiting = lax.optimization_barrier(((pair[0][:half], pair[1][half:]), waiting))
            next_pair = send_on(halves)
        sums = project(waiting)
        partials += to_owners(sums)
        group_slots.append(len(waiting))
        waiting = []
    pair = next_pair
    pieces += pair
    partials += to_owners(project(list(pair)))
    group_slots.append(1)
    hc, hs = call(
        functools.partial(taps_kernel, order=order), (spectrum, spectrum),
        8 * square, part * tokens * order, poles, cos_table, sin_table, twist,
    )

    grads, tgc, tgs, skip_sum = call(
        functools.partial(conv_kernel, order=order, group_slots=group_slots, shares=n_ch),
        (
            jax.ShapeDtypeStruct((gates, part, tokens), BF16),
            spectrum,
            spectrum,
            jax.ShapeDtypeStruct((part, 1), F32),
        ),
        32 * square, 0, place, *partials, upper, poles, hc, hs, cos_table, sin_table, twist,
        scratch=[pltpu.VMEM((n_seq, gates, part, block_len), F32)]
        + [pltpu.VMEM(a.shape, a.dtype) for a in partials],
        indexed=True, late=range(1, 1 + len(partials)),
    )

    swap = [(h, h ^ 1) for h in range(n_ch)]

    def chips(array):
        return [
            lax.ppermute(array, "ch", [(h, h ^ d) for h in range(n_ch)])
            for d in range(2, n_ch, 2)
        ]

    across = chips(grads)
    swapped = lax.ppermute(grads, "ch", swap)
    (pole_sums,) = call(
        functools.partial(pole_kernel, order=order),
        (jax.ShapeDtypeStruct((part, 2 * order + 1), F32),),
        8 * square, part * tokens * order, poles, tgc, tgs, cos_table, sin_table, skip_sum,
    )

    sums = [pole_sums] + chips(pole_sums)
    across, sums = lax.optimization_barrier((across, sums))
    held = [grads] + across + [swapped] + [lax.ppermute(a, "ch", swap) for a in across]
    sums += [lax.ppermute(a, "ch", swap) for a in sums]
    (block_sums,) = call(
        gather_kernel, [jax.ShapeDtypeStruct((rows, 2 * order + 1), F32)], 0, 0, place, *sums,
        indexed=True,
    )
    turns = n_seq // n_ch
    blocks = []
    for turn in range(turns):
        route = [
            ((h * turns + (s + turn) % turns) * n_ch + s // turns, s * n_ch + h)
            for s in range(n_seq)
            for h in range(n_ch)
        ]
        blocks.append(lax.ppermute(block_sums, ("seq", "ch"), route))

    tile = min(512, width)
    weight_grad = pl.pallas_call(
        functools.partial(weight_kernel, shares=n_ch),
        out_shape=jax.ShapeDtypeStruct((gates, rows, width), F32),
        grid=(width // tile,),
        in_specs=[pl.BlockSpec(memory_space=pltpu.SMEM)]
        + [pl.BlockSpec((gates, part, tokens), lambda i: (0, 0, 0))] * n_ch
        + [pl.BlockSpec((piece.shape[0], tile), lambda i: (0, i)) for piece in pieces],
        out_specs=pl.BlockSpec((gates, rows, tile), lambda i: (0, 0, i)),
        scratch_shapes=[
            pltpu.VMEM((gates, rows, tokens), F32),
            pltpu.VMEM((gates, rows, tokens), BF16),
            pltpu.VMEM((tokens, tile), BF16),
        ],
        compiler_params=pltpu.CompilerParams(
            vmem_limit_bytes=min(56 * MIB, 16 * MIB + 12 * gates * rows * tokens + 4 * tokens * tile)
        ),
        cost_estimate=pl.CostEstimate(
            flops=2 * gates * rows * width * tokens,
            bytes_accessed=4 * gates * rows * width + 2 * tokens * (width + gates * rows),
            transcendentals=0,
        ),
    )(place, *held, *pieces)
    weight_grad, blocks = lax.optimization_barrier((weight_grad, blocks))
    weight_grad = weight_grad.transpose(1, 0, 2)

    channels = residues.shape[0]
    by_pole = jax.ShapeDtypeStruct((order, channels), F32)
    residue_grad, rate_grad, skip_grad = call(
        functools.partial(assemble_kernel, rows=rows, order=order),
        [by_pole, by_pole, jax.ShapeDtypeStruct((1, channels), F32)], 0, 0, place, *blocks,
        scratch=[pltpu.VMEM((round_up(channels, 128), 128), F32)], indexed=True,
    )
    return (weight_grad, residue_grad.T, rate_grad.T, skip_grad.reshape(channels))


def solution(mesh):
    placed = (
        P("seq", "ch"),
        P("seq", None, "ch"),
        P("ch", "seq"),
        P("ch", None),
        P("ch", None),
        P("ch"),
    )
    return jax.shard_map(
        local,
        mesh=mesh,
        in_specs=placed,
        out_specs=(P("seq", None, "ch"), P("ch", None), P("ch", None), P("ch")),
        check_vma=False,
    )
```

```python
import functools
import math

import jax
import jax.numpy as jnp
import ml_dtypes
import numpy as np
from jax import lax
from jax.experimental import pallas as pl
from jax.experimental.pallas import tpu as pltpu
from jax.sharding import PartitionSpec as P

F32 = jnp.float32
BF16 = jnp.bfloat16
MIB = 1024 * 1024


def round_up(value, multiple):
    return -(-value // multiple) * multiple


def wave_tables(tokens):
    odd = 2 * np.arange(tokens, dtype=np.int64) + 1
    angles = (odd[:, None] * odd[None, :] % (8 * tokens)) * (math.pi / (4 * tokens))
    twist = odd * (math.pi / (4 * tokens))
    return (
        np.cos(angles).astype(ml_dtypes.bfloat16),
        np.sin(angles).astype(ml_dtypes.bfloat16),
        np.stack([np.cos(twist), np.sin(twist)]).astype(np.float32),
    )


def dot(left, right):
    return jnp.dot(left, right, preferred_element_type=F32)


def two_parts(value):
    high = value.astype(BF16)
    low = (value - high.astype(F32)).astype(BF16)
    return jnp.concatenate([high, low], 0)


def wide_dot(value, table):
    rows = value.shape[0]
    both = dot(two_parts(value), table)
    return both[:rows] + both[rows:]


def taps_kernel(poles_ref, cos_ref, sin_ref, twist_ref, hc_ref, hs_ref, *, order):
    rows, tokens = hc_ref.shape
    steps = lax.broadcasted_iota(jnp.int32, (rows, tokens), 1).astype(F32)
    taps = jnp.zeros((rows, tokens), F32)
    for pole in range(order):
        residue = poles_ref[:, pole : pole + 1]
        rate = jnp.exp(poles_ref[:, order + pole : order + pole + 1])
        taps = taps + residue * jnp.exp(-rate * steps)
    even = wide_dot(taps, cos_ref[...])
    uneven = wide_dot(taps, sin_ref[...])
    cos_half = twist_ref[0:1, :]
    sin_half = twist_ref[1:2, :]
    hc_ref[...] = cos_half * even + sin_half * uneven
    hs_ref[...] = cos_half * uneven - sin_half * even


def part_start(index, part, rows):
    return pl.multiple_of(jnp.minimum(index * part, rows - part), 8)


def pieces_kernel(grad_ref, pieces_ref, *, rows):
    n_ch, blocks, part, _ = pieces_ref.shape
    grad = grad_ref[...].astype(F32)
    for owner in range(n_ch):
        for block in range(blocks):
            start = block * rows + min(owner * part, rows - part)
            pieces_ref[owner, block] = grad[start : start + part].astype(BF16)


def poles_kernel(place_ref, packed_ref, poles_ref, *, rows, n_ch):
    part = poles_ref.shape[0]
    own = place_ref[0]
    start = own // n_ch * rows + part_start(own % n_ch, part, rows)
    poles_ref[...] = packed_ref[pl.ds(pl.multiple_of(start, 8), part), :]


def fetch(sources, targets, semaphores):
    copies = [
        pltpu.make_async_copy(source, target, semaphores.at[i])
        for i, (source, target) in enumerate(zip(sources, targets))
    ]
    for copy in copies:
        copy.start()
    return copies


def finish(copies):
    for copy in copies:
        copy.wait()


def project_kernel(place_ref, weight_ref, *refs, pieces):
    feature_refs = refs[:pieces]
    out_refs = refs[pieces:-3]
    features_ref, sums_ref, semaphores = refs[-3:]
    gates, _, _ = weight_ref.shape
    part = out_refs[0].shape[-2]
    targets, row = [], 0
    for feature_ref in feature_refs:
        targets.append(features_ref.at[pl.ds(row, feature_ref.shape[0]), :])
        row += feature_ref.shape[0]
    finish(fetch(feature_refs, targets, semaphores))
    for gate in range(gates):
        sums_ref[gate] = lax.dot_general(
            weight_ref[gate], features_ref[...], (((1,), (1,)), ((), ())),
            preferred_element_type=F32,
        )
    rows = weight_ref.shape[1]
    for step, out_ref in enumerate(out_refs):
        start = part_start(place_ref[1] ^ step, part, rows)
        out_ref[...] = sums_ref[:, pl.ds(start, part), :].astype(out_ref.dtype)


def ring_place(index, count):
    return jnp.where(index % 2 == 0, index // 2, count - (index + 1) // 2)


def ring_slot(index, place, count):
    ahead = (ring_place(index, count) - place + count) % count
    near = jnp.where(ahead * 2 < count, 2 * ahead, 2 * (count - ahead) - 1)
    return jnp.where(ahead * 2 == count, count - 1, near)


def conv_kernel(place_ref, *refs, order, group_slots, shares):
    count = len(group_slots) * shares
    partial_refs = refs[:count]
    (
        gout_ref, poles_ref, hc_ref, hs_ref, cos_ref, sin_ref, twist_ref, grad_ref,
        tgc_ref, tgs_ref, skip_ref, proj_ref, *scratch_refs,
    ) = refs[count:]
    *held_refs, semaphores = scratch_refs
    finish(fetch(partial_refs, held_refs, semaphores))
    rows, tokens = hc_ref.shape
    blocks, _, _, block_len = proj_ref.shape
    slot = 0
    for group, span in enumerate(group_slots):
        own_ref, *other_refs = held_refs[group * shares : (group + 1) * shares]
        total = own_ref[...]
        for other_ref in other_refs:
            total = total + other_ref[...].astype(F32)
        total = total.astype(BF16).astype(F32)
        for place in range(span):
            proj_ref[slot] = total[:, :, place * block_len : (place + 1) * block_len]
            slot += 1

    place = ring_place(place_ref[0], blocks)
    slots = [ring_slot(jnp.int32(b), place, blocks) for b in range(blocks)]

    def in_order(gate):
        return jnp.concatenate([proj_ref[slots[b], gate] for b in range(blocks)], 1)

    queries = in_order(0)
    keys = in_order(1)
    values = in_order(2)
    upper = jnp.concatenate([gout_ref[b].astype(F32) for b in range(blocks)], 1)
    product = keys * values
    middle = upper * queries
    signals = jnp.concatenate([product, middle], 0)
    parts = two_parts(signals)
    even = dot(parts, cos_ref[...])
    uneven = dot(parts, sin_ref[...])
    even = even[: 2 * rows] + even[2 * rows :]
    uneven = uneven[: 2 * rows] + uneven[2 * rows :]
    ac, mc = even[:rows], even[rows:]
    as_, ms = uneven[:rows], uneven[rows:]
    hc = hc_ref[...]
    hs = hs_ref[...]
    scale = 1.0 / tokens
    cos_sums = jnp.concatenate([hc * ac - hs * as_, hc * mc + hs * ms], 0) * scale
    sin_sums = jnp.concatenate([hc * as_ + hs * ac, hc * ms - hs * mc], 0) * scale
    tc = (ac * mc + as_ * ms) * scale
    ts = (ac * ms - as_ * mc) * scale
    cos_half = twist_ref[0:1, :]
    sin_half = twist_ref[1:2, :]
    tgc_ref[...] = tc * cos_half - ts * sin_half
    tgs_ref[...] = ts * cos_half + tc * sin_half
    restored = wide_dot(cos_sums, cos_ref[...]) + wide_dot(sin_sums, sin_ref[...])
    skip = poles_ref[:, 2 * order : 2 * order + 1]
    mix = restored[rows:] + skip * middle
    grads = (upper * (restored[:rows] + skip * product), mix * values, mix * keys)
    for gate, grad in enumerate(grads):
        for b in range(blocks):
            column = pl.multiple_of(slots[b] * block_len, block_len)
            grad_ref[gate, :, pl.ds(column, block_len)] = grad[
                :, b * block_len : (b + 1) * block_len
            ].astype(BF16)
    skip_ref[...] = jnp.sum(product * middle, axis=1, keepdims=True)


def pole_kernel(poles_ref, tgc_ref, tgs_ref, cos_ref, sin_ref, skip_ref, out_ref, *, order):
    rows, tokens = tgc_ref.shape
    taps_grad = wide_dot(tgc_ref[...], cos_ref[...]) + wide_dot(tgs_ref[...], sin_ref[...])
    steps = lax.broadcasted_iota(jnp.int32, (rows, tokens), 1).astype(F32)
    for pole in range(order):
        residue = poles_ref[:, pole : pole + 1]
        rate = jnp.exp(poles_ref[:, order + pole : order + pole + 1])
        decayed = taps_grad * jnp.exp(-rate * steps)
        out_ref[:, pole : pole + 1] = jnp.sum(decayed, axis=1, keepdims=True)
        moment = jnp.sum(decayed * steps, axis=1, keepdims=True)
        out_ref[:, order + pole : order + pole + 1] = -residue * rate * moment
    out_ref[:, 2 * order : 2 * order + 1] = skip_ref[...]


def share_start(own, share, shares, part, rows):
    core, step = share // (shares // 2), 2 * (share % (shares // 2))
    return part_start(own ^ core ^ step, part, rows)


def weight_kernel(place_ref, *refs, shares):
    grad_refs = refs[:shares]
    *feature_refs, out_ref, wide_ref, rows_ref, features_ref = refs[shares:]
    gates = out_ref.shape[0]
    part = grad_refs[0].shape[1]

    @pl.when(pl.program_id(0) == 0)
    def _():
        for share, grad_ref in enumerate(grad_refs):
            start = share_start(place_ref[1], share, shares, part, out_ref.shape[1])
            wide_ref[:, pl.ds(start, part), :] = grad_ref[...].astype(F32)
        rows_ref[...] = wide_ref[...].astype(BF16)

    row = 0
    for feature_ref in feature_refs:
        features_ref[row : row + feature_ref.shape[0], :] = feature_ref[...]
        row += feature_ref.shape[0]
    rows = out_ref.shape[1]
    if rows % 16 == 0:
        every = dot(rows_ref[...].reshape(gates * rows, -1), features_ref[...])
        out_ref[...] = every.reshape(out_ref.shape)
    else:
        for gate in range(gates):
            out_ref[gate] = dot(rows_ref[gate], features_ref[...])


def assemble_kernel(place_ref, *refs, rows, order):
    *block_refs, residue_ref, rate_ref, skip_ref, sums_ref = refs
    count = len(block_refs)
    sums_ref[...] = jnp.zeros_like(sums_ref)
    width = block_refs[0].shape[1]
    for turn, block_ref in enumerate(block_refs):
        block = (place_ref[0] + turn) % count
        sums_ref[pl.ds(pl.multiple_of(block * rows, 8), rows), :width] = block_ref[...]
    turned = sums_ref[...].T
    channels = residue_ref.shape[1]
    residue_ref[...] = turned[:order, :channels]
    rate_ref[...] = turned[order : 2 * order, :channels]
    skip_ref[...] = turned[2 * order : 2 * order + 1, :channels]


def gather_kernel(place_ref, *refs):
    *held_refs, out_ref = refs
    for share, held_ref in enumerate(held_refs):
        start = share_start(place_ref[1], share, len(held_refs), held_ref.shape[0], out_ref.shape[0])
        out_ref[pl.ds(start, held_ref.shape[0]), :] = held_ref[...]


def call(kernel, outs, flops, transcendentals, *operands, scratch=(), indexed=False, late=()):
    size = sum(a.size * a.dtype.itemsize for a in operands) + sum(
        o.size * o.dtype.itemsize for o in outs
    )
    scratch_size = sum(math.prod(a.shape) * a.dtype.itemsize for a in scratch)
    if late:
        scratch = [*scratch, pltpu.SemaphoreType.DMA((len(late),))]
    limit = min(56 * MIB, 2 * (size + scratch_size) + 8 * MIB)
    whole = pl.BlockSpec(memory_space=pltpu.VMEM)
    specs = [whole] * len(operands)
    if indexed:
        specs[0] = pl.BlockSpec(memory_space=pltpu.SMEM)
    for operand in late:
        specs[operand] = pl.BlockSpec(memory_space=pltpu.HBM)
    return pl.pallas_call(
        kernel,
        out_shape=outs,
        in_specs=specs,
        out_specs=[whole] * len(outs),
        scratch_shapes=scratch,
        compiler_params=pltpu.CompilerParams(vmem_limit_bytes=limit),
        cost_estimate=pl.CostEstimate(
            flops=flops, bytes_accessed=size, transcendentals=transcendentals
        ),
    )(*operands)


def ring_routes(ring):
    ahead = [(a, ring[(i + 1) % len(ring)]) for i, a in enumerate(ring)]
    return ahead, [(b, a) for a, b in ahead]


def local(features, qkv_weight, grad_out, residues, log_rates, skip_gain):
    n_seq = lax.axis_size("seq")
    n_ch = lax.axis_size("ch")
    seq_index = lax.axis_index("seq")
    ch_index = lax.axis_index("ch")
    rows, gates, width = qkv_weight.shape
    block_len = features.shape[0]
    tokens = n_seq * block_len
    order = residues.shape[1]
    part = round_up(-(-rows // n_ch), 8)
    cos_table, sin_table, twist = (jnp.asarray(a) for a in wave_tables(tokens))

    place = jnp.stack([seq_index, ch_index]).astype(jnp.int32)

    ring = list(range(0, n_seq, 2)) + list(range(n_seq - 1, 0, -2))
    ahead, behind = ring_routes(ring)

    def send_on(pair):
        return lax.ppermute(pair[0], "seq", ahead), lax.ppermute(pair[1], "seq", behind)

    square = part * tokens * tokens
    spectrum = jax.ShapeDtypeStruct((part, tokens), F32)
    weight = qkv_weight.transpose(1, 0, 2)

    def project(pieces):
        span = sum(piece.shape[0] for piece in pieces)
        sums = call(
            functools.partial(project_kernel, pieces=len(pieces)),
            [
                jax.ShapeDtypeStruct((gates, part, span), F32 if d == 0 else BF16)
                for d in range(n_ch)
            ],
            2 * gates * rows * width * span, 0, place, weight, *pieces,
            scratch=[pltpu.VMEM((span, width), BF16), pltpu.VMEM((gates, rows, span), F32)],
            indexed=True, late=range(2, 2 + len(pieces)),
        )
        return list(sums)

    def to_owners(sums):
        return [sums[0]] + [
            lax.ppermute(sums[d], "ch", [(h, h ^ d) for h in range(n_ch)])
            for d in range(1, n_ch)
        ]

    pair = send_on((features, features))

    spread = [((q % n_seq) * n_ch + q // n_seq, q) for q in range(n_seq * n_ch)]
    packed = jnp.concatenate([residues, log_rates, skip_gain[:, None]], 1)
    (poles,) = call(
        functools.partial(poles_kernel, rows=rows, n_ch=n_ch),
        (jax.ShapeDtypeStruct((part, packed.shape[1]), F32),), 0, 0, place, packed, indexed=True,
    )
    grad_out, poles = lax.optimization_barrier((grad_out, poles))
    poles = lax.ppermute(poles, ("seq", "ch"), spread)
    (upper,) = call(
        functools.partial(pieces_kernel, rows=rows),
        (jax.ShapeDtypeStruct((n_ch, n_seq // n_ch, part, block_len), BF16),), 0, 0, grad_out,
    )
    upper = lax.all_to_all(upper, "ch", split_axis=0, concat_axis=0, tiled=True)
    pair, upper, poles = lax.optimization_barrier((pair, upper, poles))
    upper = upper.reshape(n_seq, part, block_len)
    upper = lax.all_to_all(upper, "seq", split_axis=0, concat_axis=0, tiled=True)

    pieces, group_slots, partials = [features, *pair], [], []
    waiting = list(pieces)
    next_pair = send_on(pair)
    for step in range(2, n_seq // 2):
        pair = next_pair
        if step == 2:
            pair, upper = lax.optimization_barrier((pair, upper))
        else:
            pair, near = lax.optimization_barrier((pair, partials[1 - n_ch]))
            partials[1 - n_ch] = near
        pieces += pair
        waiting += pair
        if step < n_seq // 2 - 1:
            next_pair = send_on(pair)
        else:
            half = block_len // 2
            halves, waiting = lax.optimization_barrier(((pair[0][:half], pair[1][half:]), waiting))
            next_pair = send_on(halves)
            break
        sums = project(waiting)
        partials += to_owners(sums)
        group_slots.append(len(waiting))
        waiting = []
    pair = next_pair
    pieces += pair
    partials += to_owners(project([*waiting, *pair]))
    group_slots.append(len(waiting) + 1)
    hc, hs = call(
        functools.partial(taps_kernel, order=order), (spectrum, spectrum),
        8 * square, part * tokens * order, poles, cos_table, sin_table, twist,
    )

    grads, tgc, tgs, skip_sum = call(
        functools.partial(conv_kernel, order=order, group_slots=group_slots, shares=n_ch),
        (
            jax.ShapeDtypeStruct((gates, part, tokens), BF16),
            spectrum,
            spectrum,
            jax.ShapeDtypeStruct((part, 1), F32),
        ),
        32 * square, 0, place, *partials, upper, poles, hc, hs, cos_table, sin_table, twist,
        scratch=[pltpu.VMEM((n_seq, gates, part, block_len), F32)]
        + [pltpu.VMEM(a.shape, a.dtype) for a in partials],
        indexed=True, late=range(1, 1 + len(partials)),
    )

    swap = [(h, h ^ 1) for h in range(n_ch)]

    def chips(array):
        return [
            lax.ppermute(array, "ch", [(h, h ^ d) for h in range(n_ch)])
            for d in range(2, n_ch, 2)
        ]

    across = chips(grads)
    swapped = lax.ppermute(grads, "ch", swap)
    (pole_sums,) = call(
        functools.partial(pole_kernel, order=order),
        (jax.ShapeDtypeStruct((part, 2 * order + 1), F32),),
        8 * square, part * tokens * order, poles, tgc, tgs, cos_table, sin_table, skip_sum,
    )

    sums = [pole_sums] + chips(pole_sums)
    across, sums = lax.optimization_barrier((across, sums))
    held = [grads] + across + [swapped] + [lax.ppermute(a, "ch", swap) for a in across]
    sums += [lax.ppermute(a, "ch", swap) for a in sums]
    (block_sums,) = call(
        gather_kernel, [jax.ShapeDtypeStruct((rows, 2 * order + 1), F32)], 0, 0, place, *sums,
        indexed=True,
    )
    turns = n_seq // n_ch
    blocks = []
    for turn in range(turns):
        route = [
            ((h * turns + (s + turn) % turns) * n_ch + s // turns, s * n_ch + h)
            for s in range(n_seq)
            for h in range(n_ch)
        ]
        blocks.append(lax.ppermute(block_sums, ("seq", "ch"), route))

    tile = min(512, width)
    weight_grad = pl.pallas_call(
        functools.partial(weight_kernel, shares=n_ch),
        out_shape=jax.ShapeDtypeStruct((gates, rows, width), F32),
        grid=(width // tile,),
        in_specs=[pl.BlockSpec(memory_space=pltpu.SMEM)]
        + [pl.BlockSpec((gates, part, tokens), lambda i: (0, 0, 0))] * n_ch
        + [pl.BlockSpec((piece.shape[0], tile), lambda i: (0, i)) for piece in pieces],
        out_specs=pl.BlockSpec((gates, rows, tile), lambda i: (0, 0, i)),
        scratch_shapes=[
            pltpu.VMEM((gates, rows, tokens), F32),
            pltpu.VMEM((gates, rows, tokens), BF16),
            pltpu.VMEM((tokens, tile), BF16),
        ],
        compiler_params=pltpu.CompilerParams(
            vmem_limit_bytes=min(56 * MIB, 16 * MIB + 12 * gates * rows * tokens + 4 * tokens * tile)
        ),
        cost_estimate=pl.CostEstimate(
            flops=2 * gates * rows * width * tokens,
            bytes_accessed=4 * gates * rows * width + 2 * tokens * (width + gates * rows),
            transcendentals=0,
        ),
    )(place, *held, *pieces)
    weight_grad, blocks = lax.optimization_barrier((weight_grad, blocks))
    weight_grad = weight_grad.transpose(1, 0, 2)

    channels = residues.shape[0]
    by_pole = jax.ShapeDtypeStruct((order, channels), F32)
    residue_grad, rate_grad, skip_grad = call(
        functools.partial(assemble_kernel, rows=rows, order=order),
        [by_pole, by_pole, jax.ShapeDtypeStruct((1, channels), F32)], 0, 0, place, *blocks,
        scratch=[pltpu.VMEM((round_up(channels, 128), 128), F32)], indexed=True,
    )
    return (weight_grad, residue_grad.T, rate_grad.T, skip_grad.reshape(channels))


def solution(mesh):
    placed = (
        P("seq", "ch"),
        P("seq", None, "ch"),
        P("ch", "seq"),
        P("ch", None),
        P("ch", None),
        P("ch"),
    )
    return jax.shard_map(
        local,
        mesh=mesh,
        in_specs=placed,
        out_specs=(P("seq", None, "ch"), P("ch", None), P("ch", None), P("ch")),
        check_vma=False,
    )
```

```python
import functools
import math

import jax
import jax.numpy as jnp
import ml_dtypes
import numpy as np
from jax import lax
from jax.experimental import pallas as pl
from jax.experimental.pallas import tpu as pltpu
from jax.sharding import PartitionSpec as P

F32 = jnp.float32
BF16 = jnp.bfloat16
MIB = 1024 * 1024


def round_up(value, multiple):
    return -(-value // multiple) * multiple


def wave_tables(tokens):
    odd = 2 * np.arange(tokens, dtype=np.int64) + 1
    angles = (odd[:, None] * odd[None, :] % (8 * tokens)) * (math.pi / (4 * tokens))
    twist = odd * (math.pi / (4 * tokens))
    return (
        np.cos(angles).astype(ml_dtypes.bfloat16),
        np.sin(angles).astype(ml_dtypes.bfloat16),
        np.stack([np.cos(twist), np.sin(twist)]).astype(np.float32),
    )


def dot(left, right):
    return jnp.dot(left, right, preferred_element_type=F32)


def two_parts(value):
    high = value.astype(BF16)
    low = (value - high.astype(F32)).astype(BF16)
    return jnp.concatenate([high, low], 0)


def wide_dot(value, table):
    rows = value.shape[0]
    both = dot(two_parts(value), table)
    return both[:rows] + both[rows:]


def taps_kernel(poles_ref, cos_ref, sin_ref, twist_ref, hc_ref, hs_ref, *, order):
    rows, tokens = hc_ref.shape
    steps = lax.broadcasted_iota(jnp.int32, (rows, tokens), 1).astype(F32)
    taps = jnp.zeros((rows, tokens), F32)
    for pole in range(order):
        residue = poles_ref[:, pole : pole + 1]
        rate = jnp.exp(poles_ref[:, order + pole : order + pole + 1])
        taps = taps + residue * jnp.exp(-rate * steps)
    even = wide_dot(taps, cos_ref[...])
    uneven = wide_dot(taps, sin_ref[...])
    cos_half = twist_ref[0:1, :]
    sin_half = twist_ref[1:2, :]
    hc_ref[...] = cos_half * even + sin_half * uneven
    hs_ref[...] = cos_half * uneven - sin_half * even


def part_start(index, part, rows):
    return pl.multiple_of(jnp.minimum(index * part, rows - part), 8)


def pieces_kernel(grad_ref, pieces_ref, *, rows):
    n_ch, blocks, part, _ = pieces_ref.shape
    grad = grad_ref[...].astype(F32)
    for owner in range(n_ch):
        for block in range(blocks):
            start = block * rows + min(owner * part, rows - part)
            pieces_ref[owner, block] = grad[start : start + part].astype(BF16)


def poles_kernel(place_ref, packed_ref, poles_ref, *, rows, n_ch):
    part = poles_ref.shape[0]
    own = place_ref[0]
    start = own // n_ch * rows + part_start(own % n_ch, part, rows)
    poles_ref[...] = packed_ref[pl.ds(pl.multiple_of(start, 8), part), :]


def fetch(sources, targets, semaphores):
    copies = [
        pltpu.make_async_copy(source, target, semaphores.at[i])
        for i, (source, target) in enumerate(zip(sources, targets))
    ]
    for copy in copies:
        copy.start()
    return copies


def finish(copies):
    for copy in copies:
        copy.wait()


def project_kernel(place_ref, weight_ref, *refs, pieces):
    feature_refs = refs[:pieces]
    out_refs = refs[pieces:-3]
    features_ref, sums_ref, semaphores = refs[-3:]
    gates, _, _ = weight_ref.shape
    part = out_refs[0].shape[-2]
    targets, row = [], 0
    for feature_ref in feature_refs:
        targets.append(features_ref.at[pl.ds(row, feature_ref.shape[0]), :])
        row += feature_ref.shape[0]
    finish(fetch(feature_refs, targets, semaphores))
    for gate in range(gates):
        sums_ref[gate] = lax.dot_general(
            weight_ref[gate], features_ref[...], (((1,), (1,)), ((), ())),
            preferred_element_type=F32,
        )
    rows = weight_ref.shape[1]
    for step, out_ref in enumerate(out_refs):
        start = part_start(place_ref[1] ^ step, part, rows)
        out_ref[...] = sums_ref[:, pl.ds(start, part), :].astype(out_ref.dtype)


def ring_place(index, count):
    return jnp.where(index % 2 == 0, index // 2, count - (index + 1) // 2)


def ring_slot(index, place, count):
    ahead = (ring_place(index, count) - place + count) % count
    near = jnp.where(ahead * 2 < count, 2 * ahead, 2 * (count - ahead) - 1)
    return jnp.where(ahead * 2 == count, count - 1, near)


def conv_kernel(place_ref, *refs, order, group_slots, shares):
    count = len(group_slots) * shares
    partial_refs = refs[:count]
    (
        gout_ref, poles_ref, hc_ref, hs_ref, cos_ref, sin_ref, twist_ref, grad_ref,
        tgc_ref, tgs_ref, skip_ref, proj_ref, *scratch_refs,
    ) = refs[count:]
    *held_refs, semaphores = scratch_refs
    finish(fetch(partial_refs, held_refs, semaphores))
    rows, tokens = hc_ref.shape
    blocks, _, _, block_len = proj_ref.shape
    slot = 0
    for group, span in enumerate(group_slots):
        own_ref, *other_refs = held_refs[group * shares : (group + 1) * shares]
        total = own_ref[...]
        for other_ref in other_refs:
            total = total + other_ref[...].astype(F32)
        total = total.astype(BF16).astype(F32)
        for place in range(span):
            proj_ref[slot] = total[:, :, place * block_len : (place + 1) * block_len]
            slot += 1

    place = ring_place(place_ref[0], blocks)
    slots = [ring_slot(jnp.int32(b), place, blocks) for b in range(blocks)]

    def in_order(gate):
        return jnp.concatenate([proj_ref[slots[b], gate] for b in range(blocks)], 1)

    queries = in_order(0)
    keys = in_order(1)
    values = in_order(2)
    upper = jnp.concatenate([gout_ref[b].astype(F32) for b in range(blocks)], 1)
    product = keys * values
    middle = upper * queries
    signals = jnp.concatenate([product, middle], 0)
    parts = two_parts(signals)
    even = dot(parts, cos_ref[...])
    uneven = dot(parts, sin_ref[...])
    even = even[: 2 * rows] + even[2 * rows :]
    uneven = uneven[: 2 * rows] + uneven[2 * rows :]
    ac, mc = even[:rows], even[rows:]
    as_, ms = uneven[:rows], uneven[rows:]
    hc = hc_ref[...]
    hs = hs_ref[...]
    scale = 1.0 / tokens
    cos_sums = jnp.concatenate([hc * ac - hs * as_, hc * mc + hs * ms], 0) * scale
    sin_sums = jnp.concatenate([hc * as_ + hs * ac, hc * ms - hs * mc], 0) * scale
    tc = (ac * mc + as_ * ms) * scale
    ts = (ac * ms - as_ * mc) * scale
    cos_half = twist_ref[0:1, :]
    sin_half = twist_ref[1:2, :]
    tgc_ref[...] = tc * cos_half - ts * sin_half
    tgs_ref[...] = ts * cos_half + tc * sin_half
    restored = wide_dot(cos_sums, cos_ref[...]) + wide_dot(sin_sums, sin_ref[...])
    skip = poles_ref[:, 2 * order : 2 * order + 1]
    mix = restored[rows:] + skip * middle
    grads = (upper * (restored[:rows] + skip * product), mix * values, mix * keys)
    for gate, grad in enumerate(grads):
        for b in range(blocks):
            column = pl.multiple_of(slots[b] * block_len, block_len)
            grad_ref[gate, :, pl.ds(column, block_len)] = grad[
                :, b * block_len : (b + 1) * block_len
            ].astype(BF16)
    skip_ref[...] = jnp.sum(product * middle, axis=1, keepdims=True)


def pole_kernel(poles_ref, tgc_ref, tgs_ref, cos_ref, sin_ref, skip_ref, out_ref, *, order):
    rows, tokens = tgc_ref.shape
    taps_grad = wide_dot(tgc_ref[...], cos_ref[...]) + wide_dot(tgs_ref[...], sin_ref[...])
    steps = lax.broadcasted_iota(jnp.int32, (rows, tokens), 1).astype(F32)
    for pole in range(order):
        residue = poles_ref[:, pole : pole + 1]
        rate = jnp.exp(poles_ref[:, order + pole : order + pole + 1])
        decayed = taps_grad * jnp.exp(-rate * steps)
        out_ref[:, pole : pole + 1] = jnp.sum(decayed, axis=1, keepdims=True)
        moment = jnp.sum(decayed * steps, axis=1, keepdims=True)
        out_ref[:, order + pole : order + pole + 1] = -residue * rate * moment
    out_ref[:, 2 * order : 2 * order + 1] = skip_ref[...]


def share_start(own, share, shares, part, rows):
    core, step = share // (shares // 2), 2 * (share % (shares // 2))
    return part_start(own ^ core ^ step, part, rows)


def weight_kernel(place_ref, *refs, shares):
    grad_refs = refs[:shares]
    *feature_refs, out_ref, wide_ref, rows_ref, features_ref = refs[shares:]
    gates = out_ref.shape[0]
    part = grad_refs[0].shape[1]

    @pl.when(pl.program_id(0) == 0)
    def _():
        for share, grad_ref in enumerate(grad_refs):
            start = share_start(place_ref[1], share, shares, part, out_ref.shape[1])
            wide_ref[:, pl.ds(start, part), :] = grad_ref[...].astype(F32)
        rows_ref[...] = wide_ref[...].astype(BF16)

    row = 0
    for feature_ref in feature_refs:
        features_ref[row : row + feature_ref.shape[0], :] = feature_ref[...]
        row += feature_ref.shape[0]
    rows = out_ref.shape[1]
    if rows % 16 == 0:
        every = dot(rows_ref[...].reshape(gates * rows, -1), features_ref[...])
        out_ref[...] = every.reshape(out_ref.shape)
    else:
        for gate in range(gates):
            out_ref[gate] = dot(rows_ref[gate], features_ref[...])


def assemble_kernel(place_ref, *refs, rows, order):
    *block_refs, residue_ref, rate_ref, skip_ref, sums_ref = refs
    count = len(block_refs)
    sums_ref[...] = jnp.zeros_like(sums_ref)
    width = block_refs[0].shape[1]
    for turn, block_ref in enumerate(block_refs):
        block = (place_ref[0] + turn) % count
        sums_ref[pl.ds(pl.multiple_of(block * rows, 8), rows), :width] = block_ref[...]
    turned = sums_ref[...].T
    channels = residue_ref.shape[1]
    residue_ref[...] = turned[:order, :channels]
    rate_ref[...] = turned[order : 2 * order, :channels]
    skip_ref[...] = turned[2 * order : 2 * order + 1, :channels]


def gather_kernel(place_ref, *refs):
    *held_refs, out_ref = refs
    for share, held_ref in enumerate(held_refs):
        start = share_start(place_ref[1], share, len(held_refs), held_ref.shape[0], out_ref.shape[0])
        out_ref[pl.ds(start, held_ref.shape[0]), :] = held_ref[...]


def call(kernel, outs, flops, transcendentals, *operands, scratch=(), indexed=False, late=()):
    size = sum(a.size * a.dtype.itemsize for a in operands) + sum(
        o.size * o.dtype.itemsize for o in outs
    )
    scratch_size = sum(math.prod(a.shape) * a.dtype.itemsize for a in scratch)
    if late:
        scratch = [*scratch, pltpu.SemaphoreType.DMA((len(late),))]
    limit = min(56 * MIB, 2 * (size + scratch_size) + 8 * MIB)
    whole = pl.BlockSpec(memory_space=pltpu.VMEM)
    specs = [whole] * len(operands)
    if indexed:
        specs[0] = pl.BlockSpec(memory_space=pltpu.SMEM)
    for operand in late:
        specs[operand] = pl.BlockSpec(memory_space=pltpu.HBM)
    return pl.pallas_call(
        kernel,
        out_shape=outs,
        in_specs=specs,
        out_specs=[whole] * len(outs),
        scratch_shapes=scratch,
        compiler_params=pltpu.CompilerParams(vmem_limit_bytes=limit),
        cost_estimate=pl.CostEstimate(
            flops=flops, bytes_accessed=size, transcendentals=transcendentals
        ),
    )(*operands)


def ring_routes(ring):
    ahead = [(a, ring[(i + 1) % len(ring)]) for i, a in enumerate(ring)]
    return ahead, [(b, a) for a, b in ahead]


def local(features, qkv_weight, grad_out, residues, log_rates, skip_gain):
    n_seq = lax.axis_size("seq")
    n_ch = lax.axis_size("ch")
    seq_index = lax.axis_index("seq")
    ch_index = lax.axis_index("ch")
    rows, gates, width = qkv_weight.shape
    block_len = features.shape[0]
    tokens = n_seq * block_len
    order = residues.shape[1]
    part = round_up(-(-rows // n_ch), 8)
    cos_table, sin_table, twist = (jnp.asarray(a) for a in wave_tables(tokens))

    place = jnp.stack([seq_index, ch_index]).astype(jnp.int32)

    ring = list(range(0, n_seq, 2)) + list(range(n_seq - 1, 0, -2))
    ahead, behind = ring_routes(ring)

    def send_on(pair):
        return lax.ppermute(pair[0], "seq", ahead), lax.ppermute(pair[1], "seq", behind)

    square = part * tokens * tokens
    spectrum = jax.ShapeDtypeStruct((part, tokens), F32)
    weight = qkv_weight.transpose(1, 0, 2)

    def project(pieces):
        span = sum(piece.shape[0] for piece in pieces)
        sums = call(
            functools.partial(project_kernel, pieces=len(pieces)),
            [
                jax.ShapeDtypeStruct((gates, part, span), F32 if d == 0 else BF16)
                for d in range(n_ch)
            ],
            2 * gates * rows * width * span, 0, place, weight, *pieces,
            scratch=[pltpu.VMEM((span, width), BF16), pltpu.VMEM((gates, rows, span), F32)],
            indexed=True, late=range(2, 2 + len(pieces)),
        )
        return list(sums)

    def to_owners(sums):
        return [sums[0]] + [
            lax.ppermute(sums[d], "ch", [(h, h ^ d) for h in range(n_ch)])
            for d in range(1, n_ch)
        ]

    pair = send_on((features, features))

    spread = [((q % n_seq) * n_ch + q // n_seq, q) for q in range(n_seq * n_ch)]
    packed = jnp.concatenate([residues, log_rates, skip_gain[:, None]], 1)
    (poles,) = call(
        functools.partial(poles_kernel, rows=rows, n_ch=n_ch),
        (jax.ShapeDtypeStruct((part, packed.shape[1]), F32),), 0, 0, place, packed, indexed=True,
    )
    grad_out, poles = lax.optimization_barrier((grad_out, poles))
    poles = lax.ppermute(poles, ("seq", "ch"), spread)
    (upper,) = call(
        functools.partial(pieces_kernel, rows=rows),
        (jax.ShapeDtypeStruct((n_ch, n_seq // n_ch, part, block_len), BF16),), 0, 0, grad_out,
    )
    upper = lax.all_to_all(upper, "ch", split_axis=0, concat_axis=0, tiled=True)
    pair, upper, poles = lax.optimization_barrier((pair, upper, poles))
    upper = upper.reshape(n_seq, part, block_len)
    upper = lax.all_to_all(upper, "seq", split_axis=0, concat_axis=0, tiled=True)

    pieces, group_slots, partials = [features, *pair], [], []
    waiting = list(pieces)
    next_pair = send_on(pair)
    for step in range(2, n_seq // 2):
        pair = next_pair
        if step == 2:
            pair, upper = lax.optimization_barrier((pair, upper))
        else:
            pair, near = lax.optimization_barrier((pair, partials[1 - n_ch]))
            partials[1 - n_ch] = near
        pieces += pair
        waiting += pair
        if step < n_seq // 2 - 1:
            next_pair = send_on(pair)
        else:
            half = block_len // 2
            halves, waiting = lax.optimization_barrier(((pair[0][:half], pair[1][half:]), waiting))
            next_pair = send_on(halves)
            break
        sums = project(waiting)
        partials += to_owners(sums)
        group_slots.append(len(waiting))
        waiting = []
    pair = next_pair
    pieces += pair
    partials += to_owners(project([*waiting, *pair]))
    group_slots.append(len(waiting) + 1)
    hc, hs = call(
        functools.partial(taps_kernel, order=order), (spectrum, spectrum),
        8 * square, part * tokens * order, poles, cos_table, sin_table, twist,
    )

    grads, tgc, tgs, skip_sum = call(
        functools.partial(conv_kernel, order=order, group_slots=group_slots, shares=n_ch),
        (
            jax.ShapeDtypeStruct((gates, part, tokens), BF16),
            spectrum,
            spectrum,
            jax.ShapeDtypeStruct((part, 1), F32),
        ),
        32 * square, 0, place, *partials, upper, poles, hc, hs, cos_table, sin_table, twist,
        scratch=[pltpu.VMEM((n_seq, gates, part, block_len), F32)]
        + [pltpu.VMEM(a.shape, a.dtype) for a in partials],
        indexed=True, late=range(1, 1 + len(partials)),
    )

    swap = [(h, h ^ 1) for h in range(n_ch)]

    def chips(array):
        return [
            lax.ppermute(array, "ch", [(h, h ^ d) for h in range(n_ch)])
            for d in range(2, n_ch, 2)
        ]

    across = chips(grads)
    swapped = lax.ppermute(grads, "ch", swap)
    (pole_sums,) = call(
        functools.partial(pole_kernel, order=order),
        (jax.ShapeDtypeStruct((part, 2 * order + 1), F32),),
        8 * square, part * tokens * order, poles, tgc, tgs, cos_table, sin_table, skip_sum,
    )

    sums = [pole_sums] + chips(pole_sums)
    across, sums = lax.optimization_barrier((across, sums))
    held = [grads] + across + [swapped] + [lax.ppermute(a, "ch", swap) for a in across]
    sums += [lax.ppermute(a, "ch", swap) for a in sums]
    (block_sums,) = call(
        gather_kernel, [jax.ShapeDtypeStruct((rows, 2 * order + 1), F32)], 0, 0, place, *sums,
        indexed=True,
    )
    turns = n_seq // n_ch
    blocks = []
    for turn in range(turns):
        route = [
            ((h * turns + (s + turn) % turns) * n_ch + s // turns, s * n_ch + h)
            for s in range(n_seq)
            for h in range(n_ch)
        ]
        blocks.append(lax.ppermute(block_sums, ("seq", "ch"), route))

    tile = min(256, width)
    weight_grad = pl.pallas_call(
        functools.partial(weight_kernel, shares=n_ch),
        out_shape=jax.ShapeDtypeStruct((gates, rows, width), F32),
        grid=(width // tile,),
        in_specs=[pl.BlockSpec(memory_space=pltpu.SMEM)]
        + [pl.BlockSpec((gates, part, tokens), lambda i: (0, 0, 0))] * n_ch
        + [pl.BlockSpec((piece.shape[0], tile), lambda i: (0, i)) for piece in pieces],
        out_specs=pl.BlockSpec((gates, rows, tile), lambda i: (0, 0, i)),
        scratch_shapes=[
            pltpu.VMEM((gates, rows, tokens), F32),
            pltpu.VMEM((gates, rows, tokens), BF16),
            pltpu.VMEM((tokens, tile), BF16),
        ],
        compiler_params=pltpu.CompilerParams(
            vmem_limit_bytes=min(56 * MIB, 16 * MIB + 12 * gates * rows * tokens + 4 * tokens * tile)
        ),
        cost_estimate=pl.CostEstimate(
            flops=2 * gates * rows * width * tokens,
            bytes_accessed=4 * gates * rows * width + 2 * tokens * (width + gates * rows),
            transcendentals=0,
        ),
    )(place, *held, *pieces)
    weight_grad, blocks = lax.optimization_barrier((weight_grad, blocks))
    weight_grad = weight_grad.transpose(1, 0, 2)

    channels = residues.shape[0]
    by_pole = jax.ShapeDtypeStruct((order, channels), F32)
    residue_grad, rate_grad, skip_grad = call(
        functools.partial(assemble_kernel, rows=rows, order=order),
        [by_pole, by_pole, jax.ShapeDtypeStruct((1, channels), F32)], 0, 0, place, *blocks,
        scratch=[pltpu.VMEM((round_up(channels, 128), 128), F32)], indexed=True,
    )
    return (weight_grad, residue_grad.T, rate_grad.T, skip_grad.reshape(channels))


def solution(mesh):
    placed = (
        P("seq", "ch"),
        P("seq", None, "ch"),
        P("ch", "seq"),
        P("ch", None),
        P("ch", None),
        P("ch"),
    )
    return jax.shard_map(
        local,
        mesh=mesh,
        in_specs=placed,
        out_specs=(P("seq", None, "ch"), P("ch", None), P("ch", None), P("ch")),
        check_vma=False,
    )
```
